512 devices in a mesh: sx: 8 (over y), sy: 4 (over z_hi), vel: 16 (over x, z_lo, core).
Axes of the slice: x: 4, y: 8, z: 8 (z_hi: 4, z_lo: 2; z = z_hi * 2 + z_lo), core: 2. Of those that a mesh axis runs over, the one named last changes fastest.
Arguments:
- distribution: float32 [128, 128, 13824], P('sx', 'sy', 'vel'), as said below
- cell_kind: int32 [128, 128], P('sx', 'sy'), may hold values from 0 to 2, as said below
- local_knudsen: float32 [128, 128], P('sx', 'sy'), may hold values from 0.3 to 30
Outputs:
- evolved: float32 [128, 128, 13824], P('sx', 'sy', 'vel')
The draws below stay inside these ranges and needn't reach their ends.
Inputs may be any that keep to these rules, and one draw needn't show every extreme that they name: `cell_kind`: 0 marks a gas cell, 1 a wall cell, 2 an inflow cell. `distribution`: every entry is positive.
All inputs are finite; a program needn't handle non-finite values.
Results may differ from the reference program's by a relative error of at most 0.0003.
Values sent between devices are 32-bit elements; how exact they have to be, the bound alone decides.
No kernel may reach another device: no remote copies, remote signals or barrier semaphores. Data moves between devices by JAX's collectives and lax.ppermute only.
A program may use at most 128 MiB of HBM per device.

```python
import math
import jax
import jax.numpy as jnp
from jax import lax

NVX = 24
STEPS = 2
NX = 128
NY = 128
N_VEL = 16


VEL_LIMIT = 4.8


def draw_distribution(key, part):
    key = jax.random.fold_in(key, 11)
    sampler_seeds = jax.random.split(key, 8)
    lattice_slice_xy = (NX, NY)
    molecule_crowding = jnp.exp(jax.random.uniform(sampler_seeds[0], lattice_slice_xy, jnp.float32, math.log(8.0), math.log(24.0)))
    noise = jax.random.uniform(sampler_seeds[6], (NX, NY, NVX ** 3), jnp.float32, -1.0, 1.0)
    mean_motion_x = jax.random.uniform(sampler_seeds[1], lattice_slice_xy, jnp.float32, -0.6, 0.6)[..., None]
    mean_motion_y = jax.random.uniform(sampler_seeds[2], lattice_slice_xy, jnp.float32, -0.4, 0.4)[..., None]
    mean_motion_z = jax.random.uniform(sampler_seeds[3], lattice_slice_xy, jnp.float32, -0.2, 0.2)[..., None]
    molecular_agitation = jax.random.uniform(sampler_seeds[4], lattice_slice_xy, jnp.float32, 0.7, 1.4)[..., None]
    ripple_magnitude = jax.random.uniform(sampler_seeds[5], lattice_slice_xy, jnp.float32, -1.0, 1.0)[..., None]
    spacing = 2.0 * VEL_LIMIT / NVX
    points = jnp.arange(NVX, dtype=jnp.int32)
    line = ((points // 2).astype(jnp.float32) + 0.5) * spacing * (2 * (points % 2) - 1).astype(jnp.float32)
    relative_motion_component = jnp.tile(line, NVX * NVX) - mean_motion_x
    drift_y = jnp.tile(jnp.repeat(line, NVX), NVX) - mean_motion_y
    drift_z = jnp.repeat(line, NVX * NVX) - mean_motion_z
    relative_motion_norm = relative_motion_component * relative_motion_component + drift_y * drift_y + drift_z * drift_z
    maxwell_profile = molecule_crowding[..., None] / (2.0 * math.pi * molecular_agitation) ** 1.5 * jnp.exp(-relative_motion_norm / (2.0 * molecular_agitation))
    extent_tuple = jnp.exp(0.3 * ripple_magnitude * jnp.tanh(relative_motion_component * (relative_motion_norm / molecular_agitation - 5.0) / 10.0))
    return maxwell_profile * extent_tuple * (1.0 + 0.4 * noise)


def draw_cell_kind(key, part):
    key = jax.random.fold_in(key, 23)
    sampler_seeds = jax.random.split(key, 5)
    number = 6
    centre_x = jax.random.randint(sampler_seeds[0], (number,), 0, NX)
    centre_y = jax.random.randint(sampler_seeds[1], (number,), 0, NY)
    half_x = jax.random.randint(sampler_seeds[2], (number,), 1, 2 + NX // 16)
    half_y = jax.random.randint(sampler_seeds[3], (number,), 1, 2 + NY // 16)
    rows = jnp.arange(NX, dtype=jnp.int32)[:, None, None]
    columns = jnp.arange(NY, dtype=jnp.int32)[None, :, None]
    apart_x = jnp.abs(rows - centre_x)
    apart_x = jnp.minimum(apart_x, NX - apart_x)
    apart_y = jnp.abs(columns - centre_y)
    apart_y = jnp.minimum(apart_y, NY - apart_y)
    wall = jnp.any((apart_x <= half_x) & (apart_y <= half_y), axis=-1)
    band = jax.random.randint(sampler_seeds[4], (), 0, NX)
    inflow = ((jnp.arange(NX, dtype=jnp.int32) - band) % NX < 2)[:, None]
    return jnp.where(inflow, 2, jnp.where(wall, 1, 0)).astype(jnp.int32)


def level_of(stream_key, shape, pieces, least, largest):
    factor_of = 1.0
    for dim, shards_of in pieces:
        draws = jax.random.uniform(jax.random.fold_in(jax.random.fold_in(stream_key, 6), dim), (shards_of,), jnp.float32, least / len(pieces), largest / len(pieces))
        factor_of = factor_of * jnp.repeat(jnp.exp(draws), shape[dim] // shards_of).reshape((-1,) + (1,) * (len(shape) - 1 - dim))
    return factor_of


def setup_inputs(seed: int = 0) -> dict:
    arg_keys = jax.random.split(jax.random.key(seed), 4)
    return {
        "distribution": draw_distribution(jax.random.fold_in(arg_keys[3], 71), 0),
        "cell_kind": draw_cell_kind(jax.random.fold_in(arg_keys[3], 71), 0),
        "local_knudsen": jnp.clip(jnp.exp(math.log(30.0) - 4.6051701 * jax.random.uniform(arg_keys[2], (NX, NY), jnp.float32) ** level_of(arg_keys[2], (NX, NY), ((0, 8), (1, 4)), -0.2, 0.2)), 0.3, 30.0),
    }


VEL_LIMIT = 4.8
CLOCK_ADVANCE = 0.09
VISCOUS_RATIO = 2.0 / 3.0
WALL_TEMP = 1.0
INFLOW_DENSITY = 12.0
INFLOW_SPEED = 0.5
INFLOW_TEMP = 1.0

def velocity_grid():
    spacing = 2.0 * VEL_LIMIT / NVX
    points = jnp.arange(NVX, dtype=jnp.int32)
    line = ((points // 2).astype(jnp.float32) + 0.5) * spacing * (2 * (points % 2) - 1).astype(jnp.float32)
    speed_x = jnp.tile(line, NVX * NVX)
    speed_y = jnp.tile(jnp.repeat(line, NVX), NVX)
    speed_z = jnp.repeat(line, NVX * NVX)
    return (speed_x, speed_y, speed_z, spacing ** 3)

def widen_last_index(value):
    return value[..., None]

def conserved_integrals(quadrature_totals):
    molecule_crowding = quadrature_totals[0]
    mean_motion_x = quadrature_totals[1] / molecule_crowding
    mean_motion_y = quadrature_totals[2] / molecule_crowding
    mean_motion_z = quadrature_totals[3] / molecule_crowding
    molecular_agitation = (quadrature_totals[4] / molecule_crowding - (mean_motion_x * mean_motion_x + mean_motion_y * mean_motion_y + mean_motion_z * mean_motion_z)) / 3.0
    return (molecule_crowding, mean_motion_x, mean_motion_y, mean_motion_z, molecular_agitation)

def relax(present_state, macro_integrals, local_knudsen, cell_kind, speed_x, speed_y, speed_z):
    molecule_crowding, mean_motion_x, mean_motion_y, mean_motion_z, molecular_agitation, conduction_x, conduction_y, conduction_z = macro_integrals
    relative_motion_component = speed_x - widen_last_index(mean_motion_x)
    drift_y = speed_y - widen_last_index(mean_motion_y)
    drift_z = speed_z - widen_last_index(mean_motion_z)
    relative_motion_norm = relative_motion_component * relative_motion_component + drift_y * drift_y + drift_z * drift_z
    maxwell_profile = widen_last_index(molecule_crowding / (2.0 * math.pi * molecular_agitation) ** 1.5) * jnp.exp(-relative_motion_norm / widen_last_index(2.0 * molecular_agitation))
    thermal_dot_offset = relative_motion_component * widen_last_index(conduction_x) + drift_y * widen_last_index(conduction_y) + drift_z * widen_last_index(conduction_z)
    leading_coefficient = (1.0 - VISCOUS_RATIO) * thermal_dot_offset / widen_last_index(5.0 * molecule_crowding * molecular_agitation * molecular_agitation) * (relative_motion_norm / widen_last_index(molecular_agitation) - 5.0)
    shakhov_closure_model = maxwell_profile * (1.0 + leading_coefficient)
    remaining_indicator = jnp.exp(-CLOCK_ADVANCE * molecule_crowding * jnp.sqrt(molecular_agitation) / local_knudsen)
    medium_cells = shakhov_closure_model + (present_state - shakhov_closure_model) * widen_last_index(remaining_indicator)
    speed_sq = speed_x * speed_x + speed_y * speed_y + speed_z * speed_z
    wall = widen_last_index(molecule_crowding / (2.0 * math.pi * WALL_TEMP) ** 1.5) * jnp.exp(-speed_sq / (2.0 * WALL_TEMP))
    shifted = speed_x - INFLOW_SPEED
    inflow = INFLOW_DENSITY / (2.0 * math.pi * INFLOW_TEMP) ** 1.5 * jnp.exp(-(shifted * shifted + speed_y * speed_y + speed_z * speed_z) / (2.0 * INFLOW_TEMP))
    return jnp.where(widen_last_index(cell_kind == 1), wall, jnp.where(widen_last_index(cell_kind == 2), inflow, medium_cells))

def minmod(left, right):
    return 0.5 * (jnp.sign(left) + jnp.sign(right)) * jnp.minimum(jnp.abs(left), jnp.abs(right))

def sweep_periodic(values, speed, axis):
    upper = jnp.roll(values, -1, axis)
    lower = jnp.roll(values, 1, axis)
    slope = minmod(values - lower, upper - values)
    forward = jnp.maximum(speed, 0.0)
    backward = jnp.minimum(speed, 0.0)
    right = forward * (values + 0.5 * slope) + backward * (upper - 0.5 * jnp.roll(slope, -1, axis))
    return right - jnp.roll(right, 1, axis)

def macroscopic(present_state, grid):
    speed_x, speed_y, speed_z, weight = grid
    basis = jnp.stack([jnp.ones_like(speed_x), speed_x, speed_y, speed_z, speed_x * speed_x + speed_y * speed_y + speed_z * speed_z]) * weight
    quadrature_totals = jnp.einsum('kv,xyv->kxy', basis, present_state, precision=lax.Precision.HIGHEST)
    molecule_crowding, mean_motion_x, mean_motion_y, mean_motion_z, molecular_agitation = conserved_integrals(quadrature_totals)
    width = NVX ** 3 // N_VEL

    def add_block(block_index, total):
        start = (block_index * width).astype(jnp.int32)
        piece = lax.dynamic_slice_in_dim(present_state, start, width, 2)
        relative_motion_component = lax.dynamic_slice_in_dim(speed_x, start, width, 0) - widen_last_index(mean_motion_x)
        drift_y = lax.dynamic_slice_in_dim(speed_y, start, width, 0) - widen_last_index(mean_motion_y)
        drift_z = lax.dynamic_slice_in_dim(speed_z, start, width, 0) - widen_last_index(mean_motion_z)
        relative_motion_norm = relative_motion_component * relative_motion_component + drift_y * drift_y + drift_z * drift_z
        return total + jnp.stack([lax.optimization_barrier(jnp.sum(relative_motion_component * relative_motion_norm * piece, axis=-1)), lax.optimization_barrier(jnp.sum(drift_y * relative_motion_norm * piece, axis=-1)), lax.optimization_barrier(jnp.sum(drift_z * relative_motion_norm * piece, axis=-1))])
    conduction_triple = lax.fori_loop(0, N_VEL, add_block, jnp.zeros((3, NX, NY), jnp.float32)) * (0.5 * weight)
    return (molecule_crowding, mean_motion_x, mean_motion_y, mean_motion_z, molecular_agitation, conduction_triple[0], conduction_triple[1], conduction_triple[2])

def advance(present_state, macro_integrals, local_knudsen, cell_kind, grid):
    speed_x, speed_y, speed_z, weight = grid
    width = NVX ** 3 // N_VEL

    def one_block(block_index, output):
        start = (block_index * width).astype(jnp.int32)
        piece = lax.dynamic_slice_in_dim(present_state, start, width, 2)
        part_x = lax.dynamic_slice_in_dim(speed_x, start, width, 0)
        part_y = lax.dynamic_slice_in_dim(speed_y, start, width, 0)
        part_z = lax.dynamic_slice_in_dim(speed_z, start, width, 0)
        relaxed = relax(piece, macro_integrals, local_knudsen, cell_kind, part_x, part_y, part_z)
        change = sweep_periodic(relaxed, part_x, 0) + sweep_periodic(relaxed, part_y, 1)
        return lax.dynamic_update_slice_in_dim(output, relaxed - CLOCK_ADVANCE * change, start, 2)
    return lax.fori_loop(0, N_VEL, one_block, jnp.zeros_like(present_state))

def reference(distribution, cell_kind, local_knudsen):
    grid = velocity_grid()
    present_state = distribution
    for section_index in range(STEPS):
        macro_integrals = macroscopic(present_state, grid)
        present_state = advance(present_state, macro_integrals, local_knudsen, cell_kind, grid)
    return present_state
```

```python
import functools
import math

import jax
import jax.numpy as jnp
from jax import lax
from jax.experimental import pallas as pl
from jax.experimental.pallas import tpu as pltpu
from jax.sharding import PartitionSpec as P

NVX = 24
STEPS = 2

VEL_LIMIT = 4.8
CLOCK_ADVANCE = 0.09
VISCOUS_RATIO = 2.0 / 3.0
WALL_TEMP = 1.0
INFLOW_DENSITY = 12.0
INFLOW_SPEED = 0.5
INFLOW_TEMP = 1.0

SPACING = 2.0 * VEL_LIMIT / NVX
WEIGHT = SPACING**3
LOG2E = 1.0 / math.log(2.0)

LANE = 128
REACH = 2 * STEPS
MOMENTS = 13
COEFFICIENTS = 32
CHUNKS = 8
F32 = jnp.float32
BF16 = jnp.bfloat16


def lattice(first, velocities, lanes):
    lane = lax.broadcasted_iota(jnp.int32, (1, lanes), 1)
    held = lane < velocities
    index = jnp.where(held, first + lane, 0).astype(F32)

    def split(value, by):
        over = jnp.floor((value + 0.5) * (1.0 / by))
        return over, value - by * over

    def line(points):
        half, odd = split(points, 2.0)
        return jnp.where(odd > 0.5, half, -half - 1.0)

    index, a = split(index, float(NVX))
    c, b = split(index, float(NVX))
    return line(a), line(b), line(c), held, lane


def tables_kernel(velocities, first_ref, moment_ref, relax_ref, courant_ref, turn_ref):
    lanes = courant_ref.shape[1]
    a, b, c, held, lane = lattice(first_ref[0], velocities, lanes)
    zero, one = jnp.zeros((1, lanes), F32), jnp.ones((1, lanes), F32)
    square = a * a + b * b + c * c
    cubic = [a * square, b * square, c * square]
    high = [v.astype(BF16).astype(F32) for v in cubic]
    low = [v - h for v, h in zip(cubic, high)]
    rows = [one, a, b, c, a * a, b * b, c * c, a * b, a * c, b * c, *high, *low]
    rows = [jnp.where(held, v, 0.0) for v in rows]
    rows += [jnp.where(lane == velocities + i, 1.0, 0.0) for i in range(2)]
    turn_ref[...] = jnp.zeros_like(turn_ref)
    for i, value in enumerate(rows):
        turn_ref[i : i + 1, :] = value
    for start in range(0, lanes, LANE):
        turned = turn_ref[:, start : start + LANE].T
        moment_ref[start : start + LANE, :] = turned.astype(BF16)

    half = 0.5 * (square + a + b + c)
    turn_ref[...] = jnp.zeros_like(turn_ref)
    for i, value in enumerate((one, a, b, c, half)):
        for j in range(3):
            turn_ref[3 * i + j : 3 * i + j + 1, :] = jnp.where(held, value, 0.0)
    for i, value in enumerate((one, a, b, c)):
        for j in range(2):
            at = COEFFICIENTS + 15 + 2 * i + j
            turn_ref[at : at + 1, :] = jnp.where(held, value, 0.0)
    for start in range(0, lanes, LANE):
        for i in range(2):
            part = turn_ref[i * COEFFICIENTS : (i + 1) * COEFFICIENTS, start : start + LANE]
            at = 2 * start + i * LANE
            relax_ref[:, at : at + LANE] = part.astype(BF16)
    row = lax.broadcasted_iota(jnp.int32, (COEFFICIENTS, LANE), 0)
    for i in range(2):
        at = 2 * lanes + i * LANE
        picked = jnp.where((row >= 23 + 3 * i) & (row < 26 + 3 * i), 1.0, 0.0)
        relax_ref[:, at : at + LANE] = picked.astype(BF16)

    speeds = [jnp.where(held, CLOCK_ADVANCE * SPACING * (v + 0.5), 0.0) for v in (a, b)]
    signs = [jnp.where(v >= 0.0, 0.5, -0.5) for v in (a, b)]
    for i, value in enumerate([*speeds, *signs, zero, zero, zero, zero]):
        courant_ref[i : i + 1, :] = value


def cell_columns(kind_ref, knudsen_ref):
    nx, ny = kind_ref.shape
    both = jnp.concatenate([knudsen_ref[...], kind_ref[...].astype(F32)], axis=0)
    return jnp.concatenate([both, jnp.zeros((2 * nx, LANE - ny), F32)], axis=1).T


def widen(state, columns, x, nx, velocities, out_ref, at):
    ny, lanes = state.shape[0], out_ref.shape[1]
    full = velocities // LANE * LANE
    out_ref[at : at + ny, :full] = state[:, :full]
    last = jnp.concatenate(
        [state[:, full:], jnp.zeros((ny, lanes - velocities), F32)], axis=1
    )
    lane = lax.broadcasted_iota(jnp.int32, (ny, LANE), 1) + full
    last = jnp.where(lane == velocities, columns[:ny, x : x + 1], last)
    last = jnp.where(lane == velocities + 1, columns[:ny, nx + x : nx + x + 1], last)
    out_ref[at : at + ny, full:] = last


def sides_kernel(velocities, kind_ref, knudsen_ref, first_ref, last_ref, low_ref, high_ref):
    nx, ny = kind_ref.shape
    columns = cell_columns(kind_ref, knudsen_ref)
    for i in range(REACH):
        widen(last_ref[i], columns, nx - REACH + i, nx, velocities, low_ref, i * ny)
        widen(first_ref[i], columns, i, nx, velocities, high_ref, i * ny)


def own_kernel(velocities, kind_ref, knudsen_ref, state_ref, own_ref):
    nx, ny = kind_ref.shape
    columns = cell_columns(kind_ref, knudsen_ref)
    for x in range(nx):
        widen(state_ref[x], columns, x, nx, velocities, own_ref, x * ny)


def edges_kernel(own_ref, low_x_ref, high_x_ref, low_ref, high_ref):
    ny = low_x_ref.shape[0] // REACH
    at = 0
    for source in (low_x_ref, own_ref, high_x_ref):
        for start in range(0, source.shape[0], ny):
            low_ref[at : at + REACH, :] = source[start + ny - REACH : start + ny, :]
            high_ref[at : at + REACH, :] = source[start : start + REACH, :]
            at += REACH


def pieces(value, count):
    out = []
    for _ in range(count - 1):
        high = value.astype(BF16).astype(F32)
        out.append(high)
        value = value - high
    return out + [value]


def moment_rows(rows_ref, cells, basis_ref, sums_ref, block_ref, totals_ref, aux_ref):
    step = 160
    for start in range(0, cells, step):
        rows = rows_ref[start : start + step, :]
        high = rows.astype(BF16)
        low = (rows - high.astype(F32)).astype(BF16)
        basis = basis_ref[...]
        sums_ref[start : start + step, :] = jnp.dot(
            high, basis, preferred_element_type=F32
        ) + jnp.dot(low, basis, preferred_element_type=F32)
    sums_ref[cells:, :] = jnp.zeros((CHUNKS * LANE - cells, LANE), F32)
    for chunk in range(CHUNKS):
        turned = sums_ref[chunk * LANE : (chunk + 1) * LANE, :].T
        block_ref[pl.ds(chunk, 24, stride=CHUNKS), :] = turned[:24, :]
    totals_ref[: 10 * CHUNKS, :] = block_ref[: 10 * CHUNKS, :]
    totals_ref[10 * CHUNKS :, :] = (
        block_ref[10 * CHUNKS : 13 * CHUNKS, :] + block_ref[13 * CHUNKS : 16 * CHUNKS, :]
    )
    aux_ref[...] = block_ref[16 * CHUNKS : 18 * CHUNKS, :]


def coefficients(gathered_ref, aux_ref, block_ref):
    total = gathered_ref[0]
    for device in range(1, gathered_ref.shape[0]):
        total = total + gathered_ref[device]
    n, nx, ny, nz, xx, yy, zz, xy, xz, yz, cx, cy, cz = (
        total[i * CHUNKS : (i + 1) * CHUNKS, :] for i in range(MOMENTS)
    )
    knudsen = aux_ref[:CHUNKS, :]
    kind = aux_ref[CHUNKS:, :]
    inverse = 1.0 / n
    ux, uy, uz = nx * inverse, ny * inverse, nz * inverse
    uu = ux * ux + uy * uy + uz * uz
    trace = xx + yy + zz
    spread = (trace * inverse - uu) / 3.0
    temperature = SPACING * SPACING * spread
    density = WEIGHT * n
    qx = cx - ux * trace - 2.0 * (ux * xx + uy * xy + uz * xz) + 2.0 * ux * uu * n
    qy = cy - uy * trace - 2.0 * (ux * xy + uy * yy + uz * yz) + 2.0 * uy * uu * n
    qz = cz - uz * trace - 2.0 * (ux * xz + uy * yz + uz * zz) + 2.0 * uz * uu * n
    root = jnp.sqrt(temperature)
    keep = jnp.exp(-CLOCK_ADVANCE * density * root / knudsen)
    scale = (1.0 - keep) * density / ((2.0 * math.pi) ** 1.5 * temperature * root)
    heat = (
        scale
        * ((1.0 - VISCOUS_RATIO) * -2.0 * math.log(2.0) / 10.0)
        / (n * spread * spread)
    )

    wall, inflow = kind == 1.0, kind == 2.0
    solid = wall | inflow
    ux = jnp.where(inflow, INFLOW_SPEED / SPACING - 0.5, jnp.where(wall, -0.5, ux))
    uy = jnp.where(solid, -0.5, uy)
    uz = jnp.where(solid, -0.5, uz)
    spread = jnp.where(
        inflow,
        INFLOW_TEMP / SPACING**2,
        jnp.where(wall, WALL_TEMP / SPACING**2, spread),
    )
    scale = jnp.where(
        inflow,
        INFLOW_DENSITY / (2.0 * math.pi * INFLOW_TEMP) ** 1.5,
        jnp.where(wall, density / (2.0 * math.pi * WALL_TEMP) ** 1.5, scale),
    )
    keep = jnp.where(solid, 0.0, keep)
    qx = jnp.where(solid, 0.0, heat * qx)
    qy = jnp.where(solid, 0.0, heat * qy)
    qz = jnp.where(solid, 0.0, heat * qz)
    rate = (0.5 * LOG2E) / spread

    rows = []
    rows += pieces(-rate * (ux * ux + uy * uy + uz * uz), 3)
    for u in (ux, uy, uz):
        rows += pieces(rate * (2.0 * u + 1.0), 3)
    rows += pieces(-2.0 * rate, 3)
    for q in (-(qx * ux + qy * uy + qz * uz), qx, qy, qz):
        rows += pieces(q, 2)
    rows += pieces(keep, 3)
    rows += pieces(scale, 3)
    rows += [jnp.zeros_like(n)] * (COEFFICIENTS - len(rows))
    for i, value in enumerate(rows):
        block_ref[i * CHUNKS : (i + 1) * CHUNKS, :] = value


def relaxed_rows(rows_ref, cells, lanes, velocities, basis_ref, block_ref, out_ref):
    tail = 2 * lanes
    for chunk in range(-(-cells // LANE)):
        start, size = chunk * LANE, min(LANE, cells - chunk * LANE)
        here = slice(start, start + size)
        left = block_ref[pl.ds(chunk, COEFFICIENTS, stride=CHUNKS), :].T
        left = left[:size, :].astype(BF16)
        pair = jnp.dot(left, basis_ref[:, tail : tail + 2 * LANE], preferred_element_type=F32)
        keep, scale = pair[:, :LANE], pair[:, LANE:]
        for lane in range(0, lanes, LANE):
            pair = jnp.dot(
                left, basis_ref[:, 2 * lane : 2 * lane + 2 * LANE], preferred_element_type=F32
            )
            power, linear = pair[:, :LANE], pair[:, LANE:]
            state = rows_ref[here, lane : lane + LANE]
            value = state * keep + jnp.exp2(power) * (
                scale + linear * (power + 2.5 * LOG2E)
            )
            if lane + LANE > velocities:
                held = lax.broadcasted_iota(jnp.int32, value.shape, 1) < velocities - lane
                value = jnp.where(held, value, state)
            out_ref[here, lane : lane + LANE] = value


def limited(left, right):
    least, most = jnp.minimum(left, right), jnp.maximum(left, right)
    return jnp.maximum(least, 0.0) + jnp.minimum(most, 0.0)


def transported_rows(rows_ref, count, row, lanes, courant_ref, write):
    for lane in range(0, lanes, LANE):
        along = slice(lane, lane + LANE)
        speed_x, speed_y = courant_ref[0:1, along], courant_ref[1:2, along]
        half_x, half_y = courant_ref[2:3, along], courant_ref[3:4, along]
        positive_x = jnp.broadcast_to(half_x, (row, LANE)) > 0.0
        positive_y = jnp.broadcast_to(half_y, (row, LANE)) > 0.0

        def load(x):
            return rows_ref[x * row : (x + 1) * row, along]

        before, centre = load(0), load(1)
        slope_before = centre - before
        edge_before = face_before = centre_before = None
        for x in range(1, count - 1):
            after = load(x + 1)
            slope_after = after - centre
            edge = centre + half_x * limited(slope_before, slope_after)
            face = None if edge_before is None else edge - edge_before
            if face_before is not None:
                middle = centre_before
                rise = pltpu.roll(middle, row - 1, 0) - middle
                edge_y = middle + half_y * limited(pltpu.roll(rise, 1, 0), rise)
                face_y = pltpu.roll(edge_y, row - 1, 0) - edge_y
                change_x = jnp.where(positive_x, face_before, face)
                change_y = jnp.where(positive_y, pltpu.roll(face_y, 1, 0), face_y)
                write(x - 3, lane, middle - speed_x * change_x - speed_y * change_y)
            centre_before, centre = centre, after
            slope_before = slope_after
            edge_before, face_before = edge, face


def first_kernel(
    own_ref, low_x_ref, high_x_ref, low_y_ref, high_y_ref, basis_ref,
    rows_ref, totals_ref, aux_ref, sums_ref, block_ref,
):
    ny = low_x_ref.shape[0] // REACH
    nx = own_ref.shape[0] // ny
    row = ny + 2 * REACH
    for x in range(nx + 2 * REACH):
        if x < REACH:
            source, at = low_x_ref, x
        elif x < nx + REACH:
            source, at = own_ref, x - REACH
        else:
            source, at = high_x_ref, x - nx - REACH
        rows_ref[x * row : x * row + ny, :] = source[at * ny : (at + 1) * ny, :]
        rows_ref[x * row + ny : x * row + ny + REACH, :] = high_y_ref[x * REACH : (x + 1) * REACH, :]
        rows_ref[x * row + ny + REACH : (x + 1) * row, :] = low_y_ref[x * REACH : (x + 1) * REACH, :]
    cells = (nx + 2 * REACH) * row
    moment_rows(rows_ref, cells, basis_ref, sums_ref, block_ref, totals_ref, aux_ref)


def middle_kernel(
    velocities, row, gathered_ref, aux_in_ref, rows_in_ref, relax_ref, courant_ref, basis_ref,
    rows_ref, totals_ref, aux_ref, relaxed_ref, sums_ref, block_ref,
):
    cells, lanes = rows_in_ref.shape
    coefficients(gathered_ref, aux_in_ref, block_ref)
    relaxed_rows(rows_in_ref, cells, lanes, velocities, relax_ref, block_ref, relaxed_ref)

    def write(x, lane, value):
        rows_ref[x * row : (x + 1) * row, lane : lane + LANE] = value

    transported_rows(relaxed_ref, cells // row, row, lanes, courant_ref, write)
    moment_rows(rows_ref, cells - 4 * row, basis_ref, sums_ref, block_ref, totals_ref, aux_ref)


def last_kernel(
    velocities, row, gathered_ref, aux_in_ref, rows_in_ref, relax_ref, courant_ref,
    out_ref, relaxed_ref, block_ref,
):
    cells, lanes = rows_in_ref.shape
    ny = out_ref.shape[1]
    coefficients(gathered_ref, aux_in_ref, block_ref)
    relaxed_rows(rows_in_ref, cells, lanes, velocities, relax_ref, block_ref, relaxed_ref)

    def write(x, lane, value):
        width = min(LANE, velocities - lane)
        out_ref[x, :, lane : lane + width] = value[:ny, :width]

    transported_rows(relaxed_ref, cells // row, row, lanes, courant_ref, write)


BLOCK = pltpu.VMEM((COEFFICIENTS * CHUNKS, LANE), F32)
SUMS = pltpu.VMEM((CHUNKS * LANE, LANE), F32)
TOTALS = jax.ShapeDtypeStruct((MOMENTS * CHUNKS, LANE), F32)
AUX = jax.ShapeDtypeStruct((2 * CHUNKS, LANE), F32)


def rows_of(*shape):
    return jax.ShapeDtypeStruct(shape, F32)


def call(kernel, name, out_shape, scratch=(), **options):
    return pl.pallas_call(
        kernel,
        out_shape=out_shape,
        scratch_shapes=scratch,
        compiler_params=pltpu.CompilerParams(vmem_limit_bytes=40 * 1024 * 1024),
        name=name,
        **options,
    )


def gather(totals):
    devices = lax.axis_size("vel")
    copies = jnp.broadcast_to(totals[None], (devices, *totals.shape))
    return lax.all_to_all(copies, "vel", 0, 0)


def ring(axis):
    devices = lax.axis_size(axis)
    up = [(i, (i + 1) % devices) for i in range(devices)]
    return up, [(j, i) for i, j in up]


def body(distribution, cell_kind, local_knudsen):
    nx, ny, velocities = distribution.shape
    lanes = -(-(velocities + 2) // LANE) * LANE
    row = ny + 2 * REACH
    side = rows_of(REACH * ny, lanes)
    whole = pl.BlockSpec((nx, ny), lambda i: (0, 0))
    to_upper, to_lower = call(
        functools.partial(sides_kernel, velocities),
        "x_sides",
        (side, side),
        grid=(1,),
        in_specs=[
            whole,
            whole,
            pl.BlockSpec((REACH, ny, velocities), lambda i: (0, 0, 0)),
            pl.BlockSpec((REACH, ny, velocities), lambda i: (nx // REACH - 1, 0, 0)),
        ],
    )(cell_kind, local_knudsen, distribution, distribution)
    up, down = ring("sx")
    low_x = lax.ppermute(to_upper, "sx", up)
    high_x = lax.ppermute(to_lower, "sx", down)

    own = call(
        functools.partial(own_kernel, velocities), "own_rows", rows_of(nx * ny, lanes)
    )(cell_kind, local_knudsen, distribution)
    first = jnp.full((1,), lax.axis_index("vel") * velocities, jnp.int32)
    moment_basis, relax_basis, courant = call(
        functools.partial(tables_kernel, velocities),
        "tables",
        (
            jax.ShapeDtypeStruct((lanes, LANE), BF16),
            jax.ShapeDtypeStruct((COEFFICIENTS, 2 * lanes + 2 * LANE), BF16),
            rows_of(8, lanes),
        ),
        [pltpu.VMEM((LANE, lanes), F32)],
        in_specs=[pl.BlockSpec(memory_space=pltpu.SMEM)],
    )(first)

    edge = rows_of((nx + 2 * REACH) * REACH, lanes)
    to_upper, to_lower = call(edges_kernel, "y_sides", (edge, edge))(own, low_x, high_x)
    up, down = ring("sy")
    low_y = lax.ppermute(to_upper, "sy", up)
    high_y = lax.ppermute(to_lower, "sy", down)

    cells = (nx + 2 * REACH) * row
    rows, totals, aux = call(
        first_kernel,
        "first_moments",
        (rows_of(cells, lanes), TOTALS, AUX),
        [SUMS, BLOCK],
    )(own, low_x, high_x, low_y, high_y, moment_basis)
    for _ in range(STEPS - 1):
        cells -= 4 * row
        rows, totals, aux = call(
            functools.partial(middle_kernel, velocities, row),
            "step_and_moments",
            (rows_of(cells, lanes), TOTALS, AUX),
            [pltpu.VMEM((cells + 4 * row, lanes), F32), SUMS, BLOCK],
        )(gather(totals), aux, rows, relax_basis, courant, moment_basis)
    return call(
        functools.partial(last_kernel, velocities, row),
        "last_step",
        rows_of(nx, ny, velocities),
        [pltpu.VMEM((cells, lanes), F32), BLOCK],
    )(gather(totals), aux, rows, relax_basis, courant)


def solution(mesh):
    return jax.shard_map(
        body,
        mesh=mesh,
        in_specs=(P("sx", "sy", "vel"), P("sx", "sy"), P("sx", "sy")),
        out_specs=P("sx", "sy", "vel"),
        check_vma=False,
    )
```

```python
import functools
import math

import jax
import jax.numpy as jnp
from jax import lax
from jax.experimental import pallas as pl
from jax.experimental.pallas import tpu as pltpu
from jax.sharding import PartitionSpec as P

NVX = 24
STEPS = 2

VEL_LIMIT = 4.8
CLOCK_ADVANCE = 0.09
VISCOUS_RATIO = 2.0 / 3.0
WALL_TEMP = 1.0
INFLOW_DENSITY = 12.0
INFLOW_SPEED = 0.5
INFLOW_TEMP = 1.0

SPACING = 2.0 * VEL_LIMIT / NVX
WEIGHT = SPACING**3
LOG2E = 1.0 / math.log(2.0)

LANE = 128
SUBLANE = 8
REACH = 2
MOMENTS = 13
COEFFICIENTS = 32
F32 = jnp.float32
BF16 = jnp.bfloat16


def lattice(first, velocities, lanes):
    lane = lax.broadcasted_iota(jnp.int32, (1, lanes), 1)
    held = lane < velocities
    index = jnp.where(held, first + lane, 0).astype(F32)

    def split(value, by):
        over = jnp.floor((value + 0.5) * (1.0 / by))
        return over, value - by * over

    def line(points):
        half, odd = split(points, 2.0)
        return jnp.where(odd > 0.5, half, -half - 1.0)

    index, a = split(index, float(NVX))
    c, b = split(index, float(NVX))
    return line(a), line(b), line(c), held


def tables_kernel(velocities, first_ref, moment_ref, relax_ref, courant_ref, turn_ref):
    lanes = courant_ref.shape[1]
    a, b, c, held = lattice(first_ref[0], velocities, lanes)
    zero, one = jnp.zeros((1, lanes), F32), jnp.ones((1, lanes), F32)
    square = a * a + b * b + c * c
    cubic = [a * square, b * square, c * square]
    high = [v.astype(BF16).astype(F32) for v in cubic]
    low = [v - h for v, h in zip(cubic, high)]
    rows = [one, a, b, c, a * a, b * b, c * c, a * b, a * c, b * c, *high, *low]
    rows = [jnp.where(held, v, 0.0) for v in rows]
    turn_ref[...] = jnp.zeros_like(turn_ref)
    for i, value in enumerate(rows):
        turn_ref[i : i + 1, :] = value
    for start in range(0, lanes, LANE):
        turned = turn_ref[:, start : start + LANE].T
        moment_ref[start : start + LANE, :] = turned.astype(BF16)

    half = 0.5 * (square + a + b + c)
    turn_ref[...] = jnp.zeros_like(turn_ref)
    for i, value in enumerate((one, a, b, c, half)):
        for j in range(3):
            turn_ref[3 * i + j : 3 * i + j + 1, :] = jnp.where(held, value, 0.0)
    for i, value in enumerate((one, a, b, c)):
        for j in range(2):
            at = COEFFICIENTS + 15 + 2 * i + j
            turn_ref[at : at + 1, :] = jnp.where(held, value, 0.0)
    for start in range(0, lanes, LANE):
        for i in range(2):
            part = turn_ref[i * COEFFICIENTS : (i + 1) * COEFFICIENTS, start : start + LANE]
            at = 2 * start + i * LANE
            relax_ref[:, at : at + LANE] = part.astype(BF16)
    row = lax.broadcasted_iota(jnp.int32, (COEFFICIENTS, LANE), 0)
    for i in range(2):
        at = 2 * lanes + i * LANE
        picked = jnp.where((row >= 23 + 3 * i) & (row < 26 + 3 * i), 1.0, 0.0)
        relax_ref[:, at : at + LANE] = picked.astype(BF16)

    speeds = [jnp.where(held, CLOCK_ADVANCE * SPACING * (v + 0.5), 0.0) for v in (a, b)]
    signs = [jnp.where(v >= 0.0, 0.5, -0.5) for v in (a, b)]
    for i, value in enumerate([*speeds, *signs, zero, zero, zero, zero]):
        courant_ref[i : i + 1, :] = value


def pieces(value, count):
    out = []
    for _ in range(count - 1):
        high = value.astype(BF16).astype(F32)
        out.append(high)
        value = value - high
    return out + [value]


def add_moments(rows, basis, sums_ref, at):
    high = rows.astype(BF16)
    low = (rows - high.astype(F32)).astype(BF16)
    sums_ref[at : at + rows.shape[0], :] = jnp.dot(
        high, basis, preferred_element_type=F32
    ) + jnp.dot(low, basis, preferred_element_type=F32)


def blocks_of(sums_ref, block_ref, totals_ref):
    chunks = sums_ref.shape[0] // LANE
    for chunk in range(chunks):
        turned = sums_ref[chunk * LANE : (chunk + 1) * LANE, :].T
        block_ref[pl.ds(chunk, 16, stride=chunks), :] = turned[:16, :]
    totals_ref[: 10 * chunks, :] = block_ref[: 10 * chunks, :]
    totals_ref[10 * chunks :, :] = (
        block_ref[10 * chunks : 13 * chunks, :] + block_ref[13 * chunks : 16 * chunks, :]
    )


def coefficients(gathered_ref, aux_ref, block_ref):
    chunks = aux_ref.shape[0] // 2
    total = gathered_ref[0]
    for device in range(1, gathered_ref.shape[0]):
        total = total + gathered_ref[device]
    block_ref[: MOMENTS * chunks, :] = total
    n, nx, ny, nz, xx, yy, zz, xy, xz, yz, cx, cy, cz = (
        block_ref[i * chunks : (i + 1) * chunks, :] for i in range(MOMENTS)
    )
    knudsen = aux_ref[:chunks, :]
    kind = aux_ref[chunks:, :]
    inverse = 1.0 / n
    ux, uy, uz = nx * inverse, ny * inverse, nz * inverse
    uu = ux * ux + uy * uy + uz * uz
    trace = xx + yy + zz
    spread = (trace * inverse - uu) / 3.0
    temperature = SPACING * SPACING * spread
    density = WEIGHT * n
    qx = cx - ux * trace - 2.0 * (ux * xx + uy * xy + uz * xz) + 2.0 * ux * uu * n
    qy = cy - uy * trace - 2.0 * (ux * xy + uy * yy + uz * yz) + 2.0 * uy * uu * n
    qz = cz - uz * trace - 2.0 * (ux * xz + uy * yz + uz * zz) + 2.0 * uz * uu * n
    root = jnp.sqrt(temperature)
    keep = jnp.exp(-CLOCK_ADVANCE * density * root / knudsen)
    scale = (1.0 - keep) * density / ((2.0 * math.pi) ** 1.5 * temperature * root)
    heat = (
        scale
        * ((1.0 - VISCOUS_RATIO) * -2.0 * math.log(2.0) / 10.0)
        / (n * spread * spread)
    )

    wall, inflow = kind == 1.0, kind == 2.0
    solid = wall | inflow
    ux = jnp.where(inflow, INFLOW_SPEED / SPACING - 0.5, jnp.where(wall, -0.5, ux))
    uy = jnp.where(solid, -0.5, uy)
    uz = jnp.where(solid, -0.5, uz)
    spread = jnp.where(
        inflow,
        INFLOW_TEMP / SPACING**2,
        jnp.where(wall, WALL_TEMP / SPACING**2, spread),
    )
    scale = jnp.where(
        inflow,
        INFLOW_DENSITY / (2.0 * math.pi * INFLOW_TEMP) ** 1.5,
        jnp.where(wall, density / (2.0 * math.pi * WALL_TEMP) ** 1.5, scale),
    )
    keep = jnp.where(solid, 0.0, keep)
    qx = jnp.where(solid, 0.0, heat * qx)
    qy = jnp.where(solid, 0.0, heat * qy)
    qz = jnp.where(solid, 0.0, heat * qz)
    rate = (0.5 * LOG2E) / spread

    rows = []
    rows += pieces(-rate * (ux * ux + uy * uy + uz * uz), 3)
    for u in (ux, uy, uz):
        rows += pieces(rate * (2.0 * u + 1.0), 3)
    rows += pieces(-2.0 * rate, 3)
    for q in (-(qx * ux + qy * uy + qz * uz), qx, qy, qz):
        rows += pieces(q, 2)
    rows += pieces(keep, 3)
    rows += pieces(scale, 3)
    rows += [jnp.zeros_like(n)] * (COEFFICIENTS - len(rows))
    for i, value in enumerate(rows):
        block_ref[i * chunks : (i + 1) * chunks, :] = value


def relaxed_rows(load, chunks, lanes, basis_ref, block_ref, out_ref):
    tail = 2 * lanes
    for chunk in range(chunks):
        start = chunk * LANE
        left = block_ref[pl.ds(chunk, COEFFICIENTS, stride=chunks), :].T.astype(BF16)
        pair = jnp.dot(left, basis_ref[:, tail : tail + 2 * LANE], preferred_element_type=F32)
        keep, scale = pair[:, :LANE], pair[:, LANE:]
        for lane in range(0, lanes, LANE):
            pair = jnp.dot(
                left, basis_ref[:, 2 * lane : 2 * lane + 2 * LANE], preferred_element_type=F32
            )
            power, linear = pair[:, :LANE], pair[:, LANE:]
            out_ref[start : start + LANE, lane : lane + LANE] = load(start, lane) * keep + (
                jnp.exp2(power) * (scale + linear * (power + 2.5 * LOG2E))
            )


def limited(left, right):
    least, most = jnp.minimum(left, right), jnp.maximum(left, right)
    return jnp.maximum(least, 0.0) + jnp.minimum(most, 0.0)


def transported_rows(load, side, xs, ny, lanes, courant_ref, write):
    row = ny + SUBLANE
    for lane in range(0, lanes, LANE):
        along = slice(lane, lane + LANE)
        speed_x, speed_y = courant_ref[0:1, along], courant_ref[1:2, along]
        half_x, half_y = courant_ref[2:3, along], courant_ref[3:4, along]
        positive_x = jnp.broadcast_to(half_x, (ny, LANE)) > 0.0
        positive_y = jnp.broadcast_to(half_y, (ny, LANE)) > 0.0

        before, centre = load(xs[0] - 2, lane), load(xs[0] - 1, lane)
        slope_before = centre - before
        edge_before = face_before = centre_before = None
        for x in range(xs[0] - 1, xs[-1] + 2):
            after = load(x + 1, lane)
            slope_after = after - centre
            edge = centre + half_x * limited(slope_before, slope_after)
            face = None if edge_before is None else edge - edge_before
            if face_before is not None:
                middle = jnp.concatenate([centre_before, side(x - 1, lane)], axis=0)
                rise = pltpu.roll(middle, row - 1, 0) - middle
                edge_y = middle + half_y * limited(pltpu.roll(rise, 1, 0), rise)
                face_y = pltpu.roll(edge_y, row - 1, 0) - edge_y
                change_x = jnp.where(positive_x, face_before, face)
                change_y = jnp.where(positive_y, pltpu.roll(face_y, 1, 0)[:ny], face_y[:ny])
                write(x - 1, lane, centre_before - speed_x * change_x - speed_y * change_y)
            centre_before, centre = centre, after
            slope_before = slope_after
            edge_before, face_before = edge, face


def side_rows(low_ref, high_ref):
    def side(x, lane):
        at, along = slice(x * REACH, (x + 1) * REACH), slice(lane, lane + LANE)
        gap = jnp.zeros((SUBLANE - 2 * REACH, LANE), F32)
        return jnp.concatenate([high_ref[at, along], gap, low_ref[at, along]], axis=0)

    return side


def first_kernel(state_ref, knudsen_ref, kind_ref, basis_ref, totals_ref, aux_ref, sums_ref, block_ref):
    nx, ny, velocities = state_ref.shape
    step = LANE // ny
    for i, value in enumerate((knudsen_ref[...], kind_ref[...].astype(F32))):
        for x in range(0, nx, step):
            row = [value[x + j : x + j + 1, :] for j in range(step)]
            at = (i * nx + x) // step
            aux_ref[at : at + 1, :] = jnp.concatenate(row, axis=1)
    basis = basis_ref[:velocities, :]
    for x in range(0, nx, step):
        rows = state_ref[x : x + step].reshape(step * ny, velocities)
        add_moments(rows, basis, sums_ref, x * ny)
    blocks_of(sums_ref, block_ref, totals_ref)


def relax_kernel(ny, gathered_ref, aux_ref, *refs):
    *state_refs, basis_ref, out_ref, low_x_ref, high_x_ref, low_y_ref, high_y_ref, block_ref = refs
    cells, lanes = out_ref.shape
    nx = cells // ny
    coefficients(gathered_ref, aux_ref, block_ref)

    def load(start, lane):
        if len(state_refs) == 1:
            (state_ref,) = state_refs
            velocities = state_ref.shape[2]
            width = min(LANE, velocities - lane)
            rows = state_ref[start // ny : (start + LANE) // ny, :, lane : lane + width]
            rows = rows.reshape(LANE, width)
            if width == LANE:
                return rows
            return jnp.concatenate([rows, jnp.zeros((LANE, LANE - width), F32)], axis=1)
        inner_ref, outer_ref = state_refs
        along, edge = slice(lane, lane + LANE), REACH * ny
        if start == 0:
            parts = [outer_ref[:edge, along], inner_ref[: LANE - edge, along]]
        elif start + LANE == cells:
            parts = [inner_ref[start - edge :, along], outer_ref[edge:, along]]
        else:
            return inner_ref[start - edge : start - edge + LANE, along]
        return jnp.concatenate(parts, axis=0)

    relaxed_rows(load, cells // LANE, lanes, basis_ref, block_ref, out_ref)
    low_x_ref[...] = out_ref[: REACH * ny, :]
    high_x_ref[...] = out_ref[cells - REACH * ny :, :]
    for x in range(nx):
        at = slice(x * REACH, (x + 1) * REACH)
        low_y_ref[at, :] = out_ref[x * ny : x * ny + REACH, :]
        high_y_ref[at, :] = out_ref[(x + 1) * ny - REACH : (x + 1) * ny, :]


def inner_kernel(ny, velocities, state_ref, low_y_ref, high_y_ref, courant_ref, *refs):
    cells, lanes = state_ref.shape
    nx = cells // ny

    def load(x, lane):
        return state_ref[x * ny : (x + 1) * ny, lane : lane + LANE]

    if velocities is None:
        basis_ref, out_ref, sums_ref = refs

        def write(x, lane, value):
            at = (x - REACH) * ny
            out_ref[at : at + ny, lane : lane + LANE] = value

    else:
        (out_ref,) = refs

        def write(x, lane, value):
            width = min(LANE, velocities - lane)
            out_ref[x - REACH, :, lane : lane + width] = value[:, :width]

    side = side_rows(low_y_ref, high_y_ref)
    transported_rows(load, side, range(REACH, nx - REACH), ny, lanes, courant_ref, write)
    if velocities is None:
        for at in range(0, out_ref.shape[0], LANE):
            add_moments(out_ref[at : at + LANE, :], basis_ref[...], sums_ref, at)


def outer_kernel(ny, final, state_ref, low_x_ref, high_x_ref, low_y_ref, high_y_ref, courant_ref, *refs):
    cells, lanes = state_ref.shape
    nx = cells // ny

    def load(x, lane):
        if x < 0:
            ref, x = low_x_ref, x + REACH
        elif x >= nx:
            ref, x = high_x_ref, x - nx
        else:
            ref = state_ref
        return ref[x * ny : (x + 1) * ny, lane : lane + LANE]

    if final:
        inner_ref, out_ref = refs
        out_ref[REACH : nx - REACH] = inner_ref[...]

        def write(x, lane, value):
            width = min(LANE, out_ref.shape[2] - lane)
            out_ref[x, :, lane : lane + width] = value[:, :width]

    else:
        basis_ref, inner_sums_ref, out_ref, totals_ref, sums_ref, block_ref = refs

        def write(x, lane, value):
            at = (x if x < REACH else x - nx + 2 * REACH) * ny
            out_ref[at : at + ny, lane : lane + LANE] = value

    side = side_rows(low_y_ref, high_y_ref)
    for xs in (range(REACH), range(nx - REACH, nx)):
        transported_rows(load, side, xs, ny, lanes, courant_ref, write)
    if not final:
        edge = REACH * ny
        sums_ref[edge : cells - edge, :] = inner_sums_ref[...]
        for at, to in ((0, 0), (edge, cells - edge)):
            add_moments(out_ref[at : at + edge, :], basis_ref[...], sums_ref, to)
        blocks_of(sums_ref, block_ref, totals_ref)


def rows_of(*shape):
    return jax.ShapeDtypeStruct(shape, F32)


def call(kernel, name, out_shape, scratch=(), **options):
    return pl.pallas_call(
        kernel,
        out_shape=out_shape,
        scratch_shapes=scratch,
        compiler_params=pltpu.CompilerParams(vmem_limit_bytes=40 * 1024 * 1024),
        name=name,
        **options,
    )


def gather(totals):
    devices = lax.axis_size("vel")
    copies = jnp.broadcast_to(totals[None], (devices, *totals.shape))
    return lax.all_to_all(copies, "vel", 0, 0)


def ring(axis):
    devices = lax.axis_size(axis)
    up = [(i, (i + 1) % devices) for i in range(devices)]
    return up, [(j, i) for i, j in up]


def body(distribution, cell_kind, local_knudsen):
    nx, ny, velocities = distribution.shape
    lanes = -(-velocities // LANE) * LANE
    cells = nx * ny
    chunks = cells // LANE
    first = jnp.full((1,), lax.axis_index("vel") * velocities, jnp.int32)
    moment_basis, relax_basis, courant = call(
        functools.partial(tables_kernel, velocities),
        "tables",
        (
            jax.ShapeDtypeStruct((lanes, LANE), BF16),
            jax.ShapeDtypeStruct((COEFFICIENTS, 2 * lanes + 2 * LANE), BF16),
            rows_of(SUBLANE, lanes),
        ),
        [pltpu.VMEM((LANE, lanes), F32)],
        in_specs=[pl.BlockSpec(memory_space=pltpu.SMEM)],
    )(first)
    sums = pltpu.VMEM((cells, LANE), F32)
    block = pltpu.VMEM((COEFFICIENTS * chunks, LANE), F32)
    totals_shape = rows_of(MOMENTS * chunks, LANE)
    side_x, side_y = rows_of(REACH * ny, lanes), rows_of(REACH * nx, lanes)

    totals, aux = call(
        first_kernel, "first_moments", (totals_shape, rows_of(2 * chunks, LANE)), [sums, block]
    )(distribution, local_knudsen, cell_kind, moment_basis)
    state = (distribution,)
    for step in range(STEPS):
        final = step == STEPS - 1
        relaxed, low_x, high_x, low_y, high_y = call(
            functools.partial(relax_kernel, ny),
            "relax",
            (rows_of(cells, lanes), side_x, side_x, side_y, side_y),
            [block],
        )(gather(totals), aux, *state, relax_basis)
        up, down = ring("sy")
        from_low_y = lax.ppermute(high_y, "sy", up)
        from_high_y = lax.ppermute(low_y, "sy", down)
        up, down = ring("sx")
        from_low_x = lax.ppermute(high_x, "sx", up)
        from_high_x = lax.ppermute(low_x, "sx", down)
        sides_y = (from_low_y, from_high_y, courant)
        sides = (relaxed, from_low_x, from_high_x, *sides_y)
        inner_cells = cells - 2 * REACH * ny
        if final:
            inner = call(
                functools.partial(inner_kernel, ny, velocities),
                "last_inner",
                rows_of(nx - 2 * REACH, ny, velocities),
            )(relaxed, *sides_y)
            return call(
                functools.partial(outer_kernel, ny, True),
                "last_outer",
                rows_of(nx, ny, velocities),
            )(*sides, inner)
        inner, inner_sums = call(
            functools.partial(inner_kernel, ny, None),
            "inner",
            (rows_of(inner_cells, lanes), rows_of(inner_cells, LANE)),
        )(relaxed, *sides_y, moment_basis)
        outer, totals = call(
            functools.partial(outer_kernel, ny, False),
            "outer",
            (rows_of(2 * REACH * ny, lanes), totals_shape),
            [sums, block],
        )(*sides, moment_basis, inner_sums)
        state = (inner, outer)


def solution(mesh):
    return jax.shard_map(
        body,
        mesh=mesh,
        in_specs=(P("sx", "sy", "vel"), P("sx", "sy"), P("sx", "sy")),
        out_specs=P("sx", "sy", "vel"),
        check_vma=False,
    )
```

```python
import functools
import math

import jax
import jax.numpy as jnp
from jax import lax
from jax.experimental import pallas as pl
from jax.experimental.pallas import tpu as pltpu
from jax.sharding import PartitionSpec as P

NVX = 24
STEPS = 2

VEL_LIMIT = 4.8
CLOCK_ADVANCE = 0.09
VISCOUS_RATIO = 2.0 / 3.0
WALL_TEMP = 1.0
INFLOW_DENSITY = 12.0
INFLOW_SPEED = 0.5
INFLOW_TEMP = 1.0

SPACING = 2.0 * VEL_LIMIT / NVX
WEIGHT = SPACING**3
LOG2E = 1.0 / math.log(2.0)

LANE = 128
SUBLANE = 8
REACH = 2
MOMENTS = 13
COEFFICIENTS = 32
F32 = jnp.float32
BF16 = jnp.bfloat16


def lattice(first, velocities, lanes):
    lane = lax.broadcasted_iota(jnp.int32, (1, lanes), 1)
    held = lane < velocities
    index = jnp.where(held, first + lane, 0).astype(F32)

    def split(value, by):
        over = jnp.floor((value + 0.5) * (1.0 / by))
        return over, value - by * over

    def line(points):
        half, odd = split(points, 2.0)
        return jnp.where(odd > 0.5, half, -half - 1.0)

    index, a = split(index, float(NVX))
    c, b = split(index, float(NVX))
    return line(a), line(b), line(c), held


def tables_kernel(velocities, first_ref, moment_ref, relax_ref, courant_ref, turn_ref):
    lanes = courant_ref.shape[1]
    a, b, c, held = lattice(first_ref[0], velocities, lanes)
    zero, one = jnp.zeros((1, lanes), F32), jnp.ones((1, lanes), F32)
    square = a * a + b * b + c * c
    cubic = [a * square, b * square, c * square]
    high = [v.astype(BF16).astype(F32) for v in cubic]
    low = [v - h for v, h in zip(cubic, high)]
    rows = [one, a, b, c, a * a, b * b, c * c, a * b, a * c, b * c, *high, *low]
    rows = [jnp.where(held, v, 0.0) for v in rows]
    turn_ref[...] = jnp.zeros_like(turn_ref)
    for i, value in enumerate(rows):
        turn_ref[i : i + 1, :] = value
    for start in range(0, lanes, LANE):
        turned = turn_ref[:, start : start + LANE].T
        moment_ref[start : start + LANE, :] = turned.astype(BF16)

    half = 0.5 * (square + a + b + c)
    turn_ref[...] = jnp.zeros_like(turn_ref)
    for i, value in enumerate((one, a, b, c, half)):
        for j in range(3):
            turn_ref[3 * i + j : 3 * i + j + 1, :] = jnp.where(held, value, 0.0)
    for i, value in enumerate((one, a, b, c)):
        for j in range(2):
            at = COEFFICIENTS + 15 + 2 * i + j
            turn_ref[at : at + 1, :] = jnp.where(held, value, 0.0)
    for start in range(0, lanes, LANE):
        for i in range(2):
            part = turn_ref[i * COEFFICIENTS : (i + 1) * COEFFICIENTS, start : start + LANE]
            at = 2 * start + i * LANE
            relax_ref[:, at : at + LANE] = part.astype(BF16)
    row = lax.broadcasted_iota(jnp.int32, (COEFFICIENTS, LANE), 0)
    for i in range(2):
        at = 2 * lanes + i * LANE
        picked = jnp.where((row >= 23 + 3 * i) & (row < 26 + 3 * i), 1.0, 0.0)
        relax_ref[:, at : at + LANE] = picked.astype(BF16)

    speeds = [jnp.where(held, CLOCK_ADVANCE * SPACING * (v + 0.5), 0.0) for v in (a, b)]
    signs = [jnp.where(v >= 0.0, 0.5, -0.5) for v in (a, b)]
    for i, value in enumerate([*speeds, *signs, zero, zero, zero, zero]):
        courant_ref[i : i + 1, :] = value


def pieces(value, count):
    out = []
    for _ in range(count - 1):
        high = value.astype(BF16).astype(F32)
        out.append(high)
        value = value - high
    return out + [value]


def add_moments(rows, basis, sums_ref, at):
    high = rows.astype(BF16)
    low = (rows - high.astype(F32)).astype(BF16)
    sums_ref[at : at + rows.shape[0], :] = jnp.dot(
        high, basis, preferred_element_type=F32
    ) + jnp.dot(low, basis, preferred_element_type=F32)


def blocks_of(sums_ref, block_ref, totals_ref):
    chunks = sums_ref.shape[0] // LANE
    for chunk in range(chunks):
        turned = sums_ref[chunk * LANE : (chunk + 1) * LANE, :].T
        block_ref[pl.ds(chunk, 16, stride=chunks), :] = turned[:16, :]
    totals_ref[: 10 * chunks, :] = block_ref[: 10 * chunks, :]
    totals_ref[10 * chunks :, :] = (
        block_ref[10 * chunks : 13 * chunks, :] + block_ref[13 * chunks : 16 * chunks, :]
    )


def coefficients(gathered_ref, knudsen_ref, kind_ref, block_ref):
    nx, ny = kind_ref.shape
    step = LANE // ny
    chunks = nx // step
    for i, value in enumerate((knudsen_ref[...], kind_ref[...].astype(F32))):
        for x in range(0, nx, step):
            row = [value[x + j : x + j + 1, :] for j in range(step)]
            at = (MOMENTS + i) * chunks + x // step
            block_ref[at : at + 1, :] = jnp.concatenate(row, axis=1)
    total = gathered_ref[0]
    for device in range(1, gathered_ref.shape[0]):
        total = total + gathered_ref[device]
    block_ref[: MOMENTS * chunks, :] = total
    n, nx, ny, nz, xx, yy, zz, xy, xz, yz, cx, cy, cz, knudsen, kind = (
        block_ref[i * chunks : (i + 1) * chunks, :] for i in range(MOMENTS + 2)
    )
    inverse = 1.0 / n
    ux, uy, uz = nx * inverse, ny * inverse, nz * inverse
    uu = ux * ux + uy * uy + uz * uz
    trace = xx + yy + zz
    spread = (trace * inverse - uu) / 3.0
    temperature = SPACING * SPACING * spread
    density = WEIGHT * n
    qx = cx - ux * trace - 2.0 * (ux * xx + uy * xy + uz * xz) + 2.0 * ux * uu * n
    qy = cy - uy * trace - 2.0 * (ux * xy + uy * yy + uz * yz) + 2.0 * uy * uu * n
    qz = cz - uz * trace - 2.0 * (ux * xz + uy * yz + uz * zz) + 2.0 * uz * uu * n
    root = jnp.sqrt(temperature)
    keep = jnp.exp(-CLOCK_ADVANCE * density * root / knudsen)
    scale = (1.0 - keep) * density / ((2.0 * math.pi) ** 1.5 * temperature * root)
    heat = (
        scale
        * ((1.0 - VISCOUS_RATIO) * -2.0 * math.log(2.0) / 10.0)
        / (n * spread * spread)
    )

    wall, inflow = kind == 1.0, kind == 2.0
    solid = wall | inflow
    ux = jnp.where(inflow, INFLOW_SPEED / SPACING - 0.5, jnp.where(wall, -0.5, ux))
    uy = jnp.where(solid, -0.5, uy)
    uz = jnp.where(solid, -0.5, uz)
    spread = jnp.where(
        inflow,
        INFLOW_TEMP / SPACING**2,
        jnp.where(wall, WALL_TEMP / SPACING**2, spread),
    )
    scale = jnp.where(
        inflow,
        INFLOW_DENSITY / (2.0 * math.pi * INFLOW_TEMP) ** 1.5,
        jnp.where(wall, density / (2.0 * math.pi * WALL_TEMP) ** 1.5, scale),
    )
    keep = jnp.where(solid, 0.0, keep)
    qx = jnp.where(solid, 0.0, heat * qx)
    qy = jnp.where(solid, 0.0, heat * qy)
    qz = jnp.where(solid, 0.0, heat * qz)
    rate = (0.5 * LOG2E) / spread

    rows = []
    rows += pieces(-rate * (ux * ux + uy * uy + uz * uz), 3)
    for u in (ux, uy, uz):
        rows += pieces(rate * (2.0 * u + 1.0), 3)
    rows += pieces(-2.0 * rate, 3)
    for q in (-(qx * ux + qy * uy + qz * uz), qx, qy, qz):
        rows += pieces(q, 2)
    rows += pieces(keep, 3)
    rows += pieces(scale, 3)
    rows += [jnp.zeros_like(n)] * (COEFFICIENTS - len(rows))
    for i, value in enumerate(rows):
        block_ref[i * chunks : (i + 1) * chunks, :] = value


def relaxed_rows(load, chunks, lanes, basis_ref, block_ref, out_ref):
    tail = 2 * lanes
    for chunk in range(chunks):
        start = chunk * LANE
        left = block_ref[pl.ds(chunk, COEFFICIENTS, stride=chunks), :].T.astype(BF16)
        pair = jnp.dot(left, basis_ref[:, tail : tail + 2 * LANE], preferred_element_type=F32)
        keep, scale = pair[:, :LANE], pair[:, LANE:]
        for lane in range(0, lanes, LANE):
            pair = jnp.dot(
                left, basis_ref[:, 2 * lane : 2 * lane + 2 * LANE], preferred_element_type=F32
            )
            power, linear = pair[:, :LANE], pair[:, LANE:]
            out_ref[start : start + LANE, lane : lane + LANE] = load(start, lane) * keep + (
                jnp.exp2(power) * (scale + linear * (power + 2.5 * LOG2E))
            )


def limited(left, right):
    least, most = jnp.minimum(left, right), jnp.maximum(left, right)
    return jnp.maximum(least, 0.0) + jnp.minimum(most, 0.0)


def transported_rows(load, side, xs, ny, lanes, courant_ref, write):
    row = ny + SUBLANE
    for lane in range(0, lanes, LANE):
        along = slice(lane, lane + LANE)
        speed_x, speed_y = courant_ref[0:1, along], courant_ref[1:2, along]
        half_x, half_y = courant_ref[2:3, along], courant_ref[3:4, along]
        positive_x = jnp.broadcast_to(half_x, (ny, LANE)) > 0.0
        positive_y = jnp.broadcast_to(half_y, (ny, LANE)) > 0.0

        before, centre = load(xs[0] - 2, lane), load(xs[0] - 1, lane)
        slope_before = centre - before
        edge_before = face_before = centre_before = None
        for x in range(xs[0] - 1, xs[-1] + 2):
            after = load(x + 1, lane)
            slope_after = after - centre
            edge = centre + half_x * limited(slope_before, slope_after)
            face = None if edge_before is None else edge - edge_before
            if face_before is not None:
                middle = jnp.concatenate([centre_before, side(x - 1, lane)], axis=0)
                rise = pltpu.roll(middle, row - 1, 0) - middle
                edge_y = middle + half_y * limited(pltpu.roll(rise, 1, 0), rise)
                face_y = pltpu.roll(edge_y, row - 1, 0) - edge_y
                change_x = jnp.where(positive_x, face_before, face)
                change_y = jnp.where(positive_y, pltpu.roll(face_y, 1, 0)[:ny], face_y[:ny])
                write(x - 1, lane, centre_before - speed_x * change_x - speed_y * change_y)
            centre_before, centre = centre, after
            slope_before = slope_after
            edge_before, face_before = edge, face


def side_rows(low_ref, high_ref):
    def side(x, lane):
        at, along = slice(x * REACH, (x + 1) * REACH), slice(lane, lane + LANE)
        gap = jnp.zeros((SUBLANE - 2 * REACH, LANE), F32)
        return jnp.concatenate([high_ref[at, along], gap, low_ref[at, along]], axis=0)

    return side


def first_kernel(state_ref, basis_ref, totals_ref, sums_ref, block_ref):
    nx, ny, velocities = state_ref.shape
    step = LANE // ny
    basis = basis_ref[:velocities, :]
    for x in range(0, nx, step):
        rows = state_ref[x : x + step].reshape(step * ny, velocities)
        add_moments(rows, basis, sums_ref, x * ny)
    blocks_of(sums_ref, block_ref, totals_ref)


def relax_kernel(ny, gathered_ref, knudsen_ref, kind_ref, *refs):
    *state_refs, basis_ref, out_ref, low_x_ref, high_x_ref, low_y_ref, high_y_ref, block_ref = refs
    cells, lanes = out_ref.shape
    nx = cells // ny
    coefficients(gathered_ref, knudsen_ref, kind_ref, block_ref)

    def load(start, lane):
        if len(state_refs) == 1:
            (state_ref,) = state_refs
            velocities = state_ref.shape[2]
            width = min(LANE, velocities - lane)
            rows = state_ref[start // ny : (start + LANE) // ny, :, lane : lane + width]
            rows = rows.reshape(LANE, width)
            if width == LANE:
                return rows
            return jnp.concatenate([rows, jnp.zeros((LANE, LANE - width), F32)], axis=1)
        inner_ref, outer_ref = state_refs
        along, edge = slice(lane, lane + LANE), REACH * ny
        if start == 0:
            parts = [outer_ref[:edge, along], inner_ref[: LANE - edge, along]]
        elif start + LANE == cells:
            parts = [inner_ref[start - edge :, along], outer_ref[edge:, along]]
        else:
            return inner_ref[start - edge : start - edge + LANE, along]
        return jnp.concatenate(parts, axis=0)

    relaxed_rows(load, cells // LANE, lanes, basis_ref, block_ref, out_ref)
    low_x_ref[...] = out_ref[: REACH * ny, :]
    high_x_ref[...] = out_ref[cells - REACH * ny :, :]
    for x in range(nx):
        at = slice(x * REACH, (x + 1) * REACH)
        low_y_ref[at, :] = out_ref[x * ny : x * ny + REACH, :]
        high_y_ref[at, :] = out_ref[(x + 1) * ny - REACH : (x + 1) * ny, :]


def inner_kernel(ny, velocities, state_ref, low_y_ref, high_y_ref, courant_ref, *refs):
    cells, lanes = state_ref.shape
    nx = cells // ny

    def load(x, lane):
        return state_ref[x * ny : (x + 1) * ny, lane : lane + LANE]

    if velocities is None:
        basis_ref, out_ref, sums_ref = refs

        def write(x, lane, value):
            at = (x - REACH) * ny
            out_ref[at : at + ny, lane : lane + LANE] = value

    else:
        (out_ref,) = refs

        def write(x, lane, value):
            width = min(LANE, velocities - lane)
            out_ref[x, :, lane : lane + width] = value[:, :width]

    side = side_rows(low_y_ref, high_y_ref)
    transported_rows(load, side, range(REACH, nx - REACH), ny, lanes, courant_ref, write)
    if velocities is None:
        for at in range(0, out_ref.shape[0], LANE):
            add_moments(out_ref[at : at + LANE, :], basis_ref[...], sums_ref, at)


def outer_kernel(ny, final, state_ref, low_x_ref, high_x_ref, low_y_ref, high_y_ref, courant_ref, *refs):
    cells, lanes = state_ref.shape
    nx = cells // ny

    def load(x, lane):
        if x < 0:
            ref, x = low_x_ref, x + REACH
        elif x >= nx:
            ref, x = high_x_ref, x - nx
        else:
            ref = state_ref
        return ref[x * ny : (x + 1) * ny, lane : lane + LANE]

    if final:
        _, out_ref, edge_ref, sent = refs

        def write(x, lane, value):
            width = min(LANE, out_ref.shape[2] - lane)
            at = x if x < REACH else x - nx + 2 * REACH
            edge_ref[at, :, lane : lane + width] = value[:, :width]

    else:
        basis_ref, inner_sums_ref, out_ref, totals_ref, sums_ref, block_ref = refs

        def write(x, lane, value):
            at = (x if x < REACH else x - nx + 2 * REACH) * ny
            out_ref[at : at + ny, lane : lane + LANE] = value

    side = side_rows(low_y_ref, high_y_ref)
    copies = []
    for i, xs in enumerate((range(REACH), range(nx - REACH, nx))):
        transported_rows(load, side, xs, ny, lanes, courant_ref, write)
        if final:
            part = edge_ref.at[i * REACH : (i + 1) * REACH]
            copies.append(
                pltpu.make_async_copy(part, out_ref.at[xs[0] : xs[0] + REACH], sent.at[i])
            )
            copies[-1].start()
    for copy in copies:
        copy.wait()
    if not final:
        edge = REACH * ny
        sums_ref[edge : cells - edge, :] = inner_sums_ref[...]
        for at, to in ((0, 0), (edge, cells - edge)):
            add_moments(out_ref[at : at + edge, :], basis_ref[...], sums_ref, to)
        blocks_of(sums_ref, block_ref, totals_ref)


INNER_COST = pl.CostEstimate(flops=30_000_000_000, bytes_accessed=4_000_000, transcendentals=0)


def rows_of(*shape):
    return jax.ShapeDtypeStruct(shape, F32)


def call(kernel, name, out_shape, scratch=(), **options):
    return pl.pallas_call(
        kernel,
        out_shape=out_shape,
        scratch_shapes=scratch,
        compiler_params=pltpu.CompilerParams(vmem_limit_bytes=40 * 1024 * 1024),
        name=name,
        **options,
    )


def gather(totals):
    devices = lax.axis_size("vel")
    copies = jnp.broadcast_to(totals[None], (devices, *totals.shape))
    return lax.all_to_all(copies, "vel", 0, 0)


def ring(axis):
    devices = lax.axis_size(axis)
    up = [(i, (i + 1) % devices) for i in range(devices)]
    return up, [(j, i) for i, j in up]


def body(distribution, cell_kind, local_knudsen):
    nx, ny, velocities = distribution.shape
    lanes = -(-velocities // LANE) * LANE
    cells = nx * ny
    chunks = cells // LANE
    sums = pltpu.VMEM((cells, LANE), F32)
    block = pltpu.VMEM((COEFFICIENTS * chunks, LANE), F32)
    totals_shape = rows_of(MOMENTS * chunks, LANE)
    side_x, side_y = rows_of(REACH * ny, lanes), rows_of(REACH * nx, lanes)

    moment_basis, relax_basis, courant = call(
        functools.partial(tables_kernel, velocities),
        "tables",
        (
            jax.ShapeDtypeStruct((lanes, LANE), BF16),
            jax.ShapeDtypeStruct((COEFFICIENTS, 2 * lanes + 2 * LANE), BF16),
            rows_of(SUBLANE, lanes),
        ),
        [pltpu.VMEM((LANE, lanes), F32)],
        in_specs=[pl.BlockSpec(memory_space=pltpu.SMEM)],
    )(jnp.full((1,), lax.axis_index("vel") * velocities, jnp.int32))
    totals = call(first_kernel, "first_moments", totals_shape, [sums, block])(
        distribution, moment_basis
    )
    state = (distribution,)
    for step in range(STEPS):
        final = step == STEPS - 1
        relaxed, low_x, high_x, low_y, high_y = call(
            functools.partial(relax_kernel, ny),
            "relax",
            (rows_of(cells, lanes), side_x, side_x, side_y, side_y),
            [block],
        )(gather(totals), local_knudsen, cell_kind, *state, relax_basis)
        up, down = ring("sy")
        from_low_y = lax.ppermute(high_y, "sy", up)
        from_high_y = lax.ppermute(low_y, "sy", down)
        up, down = ring("sx")
        from_low_x = lax.ppermute(high_x, "sx", up)
        from_high_x = lax.ppermute(low_x, "sx", down)
        sides_y = (from_low_y, from_high_y, courant)
        sides = (relaxed, from_low_x, from_high_x, *sides_y)
        inner_cells = cells - 2 * REACH * ny
        if final:
            inner = call(
                functools.partial(inner_kernel, ny, velocities),
                "last_inner",
                rows_of(nx, ny, velocities),
                cost_estimate=INNER_COST,
            )(relaxed, *sides_y)
            return call(
                functools.partial(outer_kernel, ny, True),
                "last_outer",
                rows_of(nx, ny, velocities),
                [pltpu.VMEM((2 * REACH, ny, velocities), F32), pltpu.SemaphoreType.DMA((2,))],
                in_specs=[pl.BlockSpec(memory_space=pltpu.VMEM)] * len(sides)
                + [pl.BlockSpec(memory_space=pltpu.HBM)],
                out_specs=pl.BlockSpec(memory_space=pltpu.HBM),
                input_output_aliases={len(sides): 0},
            )(*sides, inner)
        inner, inner_sums = call(
            functools.partial(inner_kernel, ny, None),
            "inner",
            (rows_of(inner_cells, lanes), rows_of(inner_cells, LANE)),
            cost_estimate=INNER_COST,
        )(relaxed, *sides_y, moment_basis)
        outer, totals = call(
            functools.partial(outer_kernel, ny, False),
            "outer",
            (rows_of(2 * REACH * ny, lanes), totals_shape),
            [sums, block],
        )(*sides, moment_basis, inner_sums)
        state = (inner, outer)


def solution(mesh):
    return jax.shard_map(
        body,
        mesh=mesh,
        in_specs=(P("sx", "sy", "vel"), P("sx", "sy"), P("sx", "sy")),
        out_specs=P("sx", "sy", "vel"),
        check_vma=False,
    )
```

```python
import functools
import math

import jax
import jax.numpy as jnp
from jax import lax
from jax.experimental import pallas as pl
from jax.experimental.pallas import tpu as pltpu
from jax.sharding import PartitionSpec as P

NVX = 24
STEPS = 2

VEL_LIMIT = 4.8
CLOCK_ADVANCE = 0.09
VISCOUS_RATIO = 2.0 / 3.0
WALL_TEMP = 1.0
INFLOW_DENSITY = 12.0
INFLOW_SPEED = 0.5
INFLOW_TEMP = 1.0

SPACING = 2.0 * VEL_LIMIT / NVX
WEIGHT = SPACING**3
LOG2E = 1.0 / math.log(2.0)

LANE = 128
SUBLANE = 8
REACH = 2
MOMENTS = 13
COEFFICIENTS = 32
F32 = jnp.float32
BF16 = jnp.bfloat16


def lattice(first, velocities, lanes):
    lane = lax.broadcasted_iota(jnp.int32, (1, lanes), 1)
    held = lane < velocities
    index = jnp.where(held, first + lane, 0).astype(F32)

    def split(value, by):
        over = jnp.floor((value + 0.5) * (1.0 / by))
        return over, value - by * over

    def line(points):
        half, odd = split(points, 2.0)
        return jnp.where(odd > 0.5, half, -half - 1.0)

    index, a = split(index, float(NVX))
    c, b = split(index, float(NVX))
    return line(a), line(b), line(c), held


def tables_kernel(velocities, first_ref, moment_ref, relax_ref, courant_ref, turn_ref):
    lanes = courant_ref.shape[1]
    a, b, c, held = lattice(first_ref[0], velocities, lanes)
    zero, one = jnp.zeros((1, lanes), F32), jnp.ones((1, lanes), F32)
    square = a * a + b * b + c * c
    cubic = [a * square, b * square, c * square]
    high = [v.astype(BF16).astype(F32) for v in cubic]
    low = [v - h for v, h in zip(cubic, high)]
    rows = [one, a, b, c, a * a, b * b, c * c, a * b, a * c, b * c, *high, *low]
    rows = [jnp.where(held, v, 0.0) for v in rows]
    turn_ref[...] = jnp.zeros_like(turn_ref)
    for i, value in enumerate(rows):
        turn_ref[i : i + 1, :] = value
    for start in range(0, lanes, LANE):
        turned = turn_ref[:, start : start + LANE].T
        moment_ref[start : start + LANE, :] = turned.astype(BF16)

    half = 0.5 * (square + a + b + c)
    turn_ref[...] = jnp.zeros_like(turn_ref)
    for i, value in enumerate((one, a, b, c, half)):
        for j in range(3):
            turn_ref[3 * i + j : 3 * i + j + 1, :] = jnp.where(held, value, 0.0)
    for i, value in enumerate((one, a, b, c)):
        for j in range(2):
            at = COEFFICIENTS + 15 + 2 * i + j
            turn_ref[at : at + 1, :] = jnp.where(held, value, 0.0)
    for start in range(0, lanes, LANE):
        for i in range(2):
            part = turn_ref[i * COEFFICIENTS : (i + 1) * COEFFICIENTS, start : start + LANE]
            at = 2 * start + i * LANE
            relax_ref[:, at : at + LANE] = part.astype(BF16)
    row = lax.broadcasted_iota(jnp.int32, (COEFFICIENTS, LANE), 0)
    for i in range(2):
        at = 2 * lanes + i * LANE
        picked = jnp.where((row >= 23 + 3 * i) & (row < 26 + 3 * i), 1.0, 0.0)
        relax_ref[:, at : at + LANE] = picked.astype(BF16)

    speeds = [jnp.where(held, CLOCK_ADVANCE * SPACING * (v + 0.5), 0.0) for v in (a, b)]
    signs = [jnp.where(v >= 0.0, 0.5, -0.5) for v in (a, b)]
    for i, value in enumerate([*speeds, *signs, zero, zero, zero, zero]):
        courant_ref[i : i + 1, :] = value


def pieces(value, count):
    out = []
    for _ in range(count - 1):
        high = value.astype(BF16).astype(F32)
        out.append(high)
        value = value - high
    return out + [value]


def moment_sums(rows, basis):
    high = rows.astype(BF16)
    low = (rows - high.astype(F32)).astype(BF16)
    return jnp.dot(high, basis, preferred_element_type=F32) + jnp.dot(
        low, basis, preferred_element_type=F32
    )


def blocks_of(sums, chunk, chunks, block_ref):
    block_ref[pl.ds(chunk, 16, stride=chunks), :] = sums.T[:16, :]


def write_totals(chunks, block_ref, totals_ref):
    totals_ref[: 10 * chunks, :] = block_ref[: 10 * chunks, :]
    totals_ref[10 * chunks :, :] = (
        block_ref[10 * chunks : 13 * chunks, :] + block_ref[13 * chunks : 16 * chunks, :]
    )


def rows_in_chunk(chunk, nx, step):
    if chunk == 0:
        return [*range(REACH), *range(nx - REACH, nx)]
    start = REACH + (chunk - 1) * step
    return list(range(start, start + step))


def coefficients(gathered_ref, knudsen_ref, kind_ref, block_ref):
    nx, ny = kind_ref.shape
    step = LANE // ny
    chunks = nx // step
    for i, value in enumerate((knudsen_ref[...], kind_ref[...].astype(F32))):
        for chunk in range(chunks):
            row = [value[x : x + 1, :] for x in rows_in_chunk(chunk, nx, step)]
            at = (MOMENTS + i) * chunks + chunk
            block_ref[at : at + 1, :] = jnp.concatenate(row, axis=1)
    total = gathered_ref[0]
    for device in range(1, gathered_ref.shape[0]):
        total = total + gathered_ref[device]
    block_ref[: MOMENTS * chunks, :] = total
    n, nx, ny, nz, xx, yy, zz, xy, xz, yz, cx, cy, cz, knudsen, kind = (
        block_ref[i * chunks : (i + 1) * chunks, :] for i in range(MOMENTS + 2)
    )
    inverse = 1.0 / n
    ux, uy, uz = nx * inverse, ny * inverse, nz * inverse
    uu = ux * ux + uy * uy + uz * uz
    trace = xx + yy + zz
    spread = (trace * inverse - uu) / 3.0
    temperature = SPACING * SPACING * spread
    density = WEIGHT * n
    qx = cx - ux * trace - 2.0 * (ux * xx + uy * xy + uz * xz) + 2.0 * ux * uu * n
    qy = cy - uy * trace - 2.0 * (ux * xy + uy * yy + uz * yz) + 2.0 * uy * uu * n
    qz = cz - uz * trace - 2.0 * (ux * xz + uy * yz + uz * zz) + 2.0 * uz * uu * n
    root = jnp.sqrt(temperature)
    keep = jnp.exp(-CLOCK_ADVANCE * density * root / knudsen)
    scale = (1.0 - keep) * density / ((2.0 * math.pi) ** 1.5 * temperature * root)
    heat = (
        scale
        * ((1.0 - VISCOUS_RATIO) * -2.0 * math.log(2.0) / 10.0)
        / (n * spread * spread)
    )

    wall, inflow = kind == 1.0, kind == 2.0
    solid = wall | inflow
    ux = jnp.where(inflow, INFLOW_SPEED / SPACING - 0.5, jnp.where(wall, -0.5, ux))
    uy = jnp.where(solid, -0.5, uy)
    uz = jnp.where(solid, -0.5, uz)
    spread = jnp.where(
        inflow,
        INFLOW_TEMP / SPACING**2,
        jnp.where(wall, WALL_TEMP / SPACING**2, spread),
    )
    scale = jnp.where(
        inflow,
        INFLOW_DENSITY / (2.0 * math.pi * INFLOW_TEMP) ** 1.5,
        jnp.where(wall, density / (2.0 * math.pi * WALL_TEMP) ** 1.5, scale),
    )
    keep = jnp.where(solid, 0.0, keep)
    qx = jnp.where(solid, 0.0, heat * qx)
    qy = jnp.where(solid, 0.0, heat * qy)
    qz = jnp.where(solid, 0.0, heat * qz)
    rate = (0.5 * LOG2E) / spread

    rows = []
    rows += pieces(-rate * (ux * ux + uy * uy + uz * uz), 3)
    for u in (ux, uy, uz):
        rows += pieces(rate * (2.0 * u + 1.0), 3)
    rows += pieces(-2.0 * rate, 3)
    for q in (-(qx * ux + qy * uy + qz * uz), qx, qy, qz):
        rows += pieces(q, 2)
    rows += pieces(keep, 3)
    rows += pieces(scale, 3)
    rows += [jnp.zeros_like(n)] * (COEFFICIENTS - len(rows))
    for i, value in enumerate(rows):
        block_ref[i * chunks : (i + 1) * chunks, :] = value


def relaxed_rows(load, nx, ny, lanes, basis_ref, block_ref, out_ref):
    step = LANE // ny
    chunks, tail = nx // step, 2 * lanes
    for chunk in range(chunks):
        xs = rows_in_chunk(chunk, nx, step)
        left = block_ref[pl.ds(chunk, COEFFICIENTS, stride=chunks), :].T.astype(BF16)
        pair = jnp.dot(left, basis_ref[:, tail : tail + 2 * LANE], preferred_element_type=F32)
        keep, scale = pair[:, :LANE], pair[:, LANE:]
        for lane in range(0, lanes, LANE):
            pair = jnp.dot(
                left, basis_ref[:, 2 * lane : 2 * lane + 2 * LANE], preferred_element_type=F32
            )
            power, linear = pair[:, :LANE], pair[:, LANE:]
            value = load(chunk, xs, lane) * keep + (
                jnp.exp2(power) * (scale + linear * (power + 2.5 * LOG2E))
            )
            for half in (0, step // 2):
                rows = value[half * ny : (half + step // 2) * ny, :]
                at = xs[half] * ny
                out_ref[at : at + rows.shape[0], lane : lane + LANE] = rows


def limited(left, right):
    least, most = jnp.minimum(left, right), jnp.maximum(left, right)
    return jnp.maximum(least, 0.0) + jnp.minimum(most, 0.0)


def transported_rows(load, side, xs, ny, lanes, courant_ref, write):
    row = ny + SUBLANE
    for lane in range(0, lanes, LANE):
        along = slice(lane, lane + LANE)
        speed_x, speed_y = courant_ref[0:1, along], courant_ref[1:2, along]
        half_x, half_y = courant_ref[2:3, along], courant_ref[3:4, along]
        positive_x = jnp.broadcast_to(half_x, (ny, LANE)) > 0.0
        positive_y = jnp.broadcast_to(half_y, (ny, LANE)) > 0.0

        before, centre = load(xs[0] - 2, lane), load(xs[0] - 1, lane)
        slope_before = centre - before
        edge_before = face_before = centre_before = None
        for x in range(xs[0] - 1, xs[-1] + 2):
            after = load(x + 1, lane)
            slope_after = after - centre
            edge = centre + half_x * limited(slope_before, slope_after)
            face = None if edge_before is None else edge - edge_before
            if face_before is not None:
                middle = jnp.concatenate([centre_before, side(x - 1, lane)], axis=0)
                rise = pltpu.roll(middle, row - 1, 0) - middle
                edge_y = middle + half_y * limited(pltpu.roll(rise, 1, 0), rise)
                face_y = pltpu.roll(edge_y, row - 1, 0) - edge_y
                change_x = jnp.where(positive_x, face_before, face)
                change_y = jnp.where(positive_y, pltpu.roll(face_y, 1, 0)[:ny], face_y[:ny])
                write(x - 1, lane, centre_before - speed_x * change_x - speed_y * change_y)
            centre_before, centre = centre, after
            slope_before = slope_after
            edge_before, face_before = edge, face


def side_rows(low_ref, high_ref):
    def side(x, lane):
        at, along = slice(x * REACH, (x + 1) * REACH), slice(lane, lane + LANE)
        gap = jnp.zeros((SUBLANE - 2 * REACH, LANE), F32)
        return jnp.concatenate([high_ref[at, along], gap, low_ref[at, along]], axis=0)

    return side


def first_kernel(state_ref, basis_ref, totals_ref, block_ref):
    nx, ny, velocities = state_ref.shape
    step = LANE // ny
    basis = basis_ref[:velocities, :]
    for chunk in range(nx // step):
        xs = rows_in_chunk(chunk, nx, step)
        halves = [state_ref[xs[i] : xs[i] + step // 2] for i in (0, step // 2)]
        rows = jnp.concatenate(halves, axis=0).reshape(LANE, velocities)
        blocks_of(moment_sums(rows, basis), chunk, nx // step, block_ref)
    write_totals(nx // step, block_ref, totals_ref)


def relax_kernel(ny, gathered_ref, knudsen_ref, kind_ref, *refs):
    *state_refs, basis_ref, out_ref, low_x_ref, high_x_ref, low_y_ref, high_y_ref, block_ref = refs
    cells, lanes = out_ref.shape
    nx = cells // ny
    coefficients(gathered_ref, knudsen_ref, kind_ref, block_ref)

    def load_given(chunk, xs, lane):
        (state_ref,) = state_refs
        velocities = state_ref.shape[2]
        width = min(LANE, velocities - lane)
        half = len(xs) // 2
        parts = [state_ref[xs[i] : xs[i] + half, :, lane : lane + width] for i in (0, half)]
        rows = jnp.concatenate(parts, axis=0).reshape(LANE, width)
        if width == LANE:
            return rows
        return jnp.concatenate([rows, jnp.zeros((LANE, LANE - width), F32)], axis=1)

    def load(chunk, xs, lane):
        inner_ref, low_ref, high_ref = state_refs
        along = slice(lane, lane + LANE)
        if chunk == 0:
            return jnp.concatenate([low_ref[:, along], high_ref[:, along]], axis=0)
        return inner_ref[(chunk - 1) * LANE : chunk * LANE, along]

    load = load_given if len(state_refs) == 1 else load
    relaxed_rows(load, nx, ny, lanes, basis_ref, block_ref, out_ref)
    low_x_ref[...] = out_ref[: REACH * ny, :]
    high_x_ref[...] = out_ref[cells - REACH * ny :, :]
    for x in range(nx):
        at = slice(x * REACH, (x + 1) * REACH)
        low_y_ref[at, :] = out_ref[x * ny : x * ny + REACH, :]
        high_y_ref[at, :] = out_ref[(x + 1) * ny - REACH : (x + 1) * ny, :]


def inner_kernel(ny, velocities, state_ref, low_y_ref, high_y_ref, courant_ref, *refs):
    cells, lanes = state_ref.shape
    nx = cells // ny

    def load(x, lane):
        return state_ref[x * ny : (x + 1) * ny, lane : lane + LANE]

    if velocities is None:
        basis_ref, out_ref, block_ref = refs

        def write(x, lane, value):
            at = (x - REACH) * ny
            out_ref[at : at + ny, lane : lane + LANE] = value

    else:
        (out_ref,) = refs

        def write(x, lane, value):
            width = min(LANE, velocities - lane)
            out_ref[x, :, lane : lane + width] = value[:, :width]

    side = side_rows(low_y_ref, high_y_ref)
    transported_rows(load, side, range(REACH, nx - REACH), ny, lanes, courant_ref, write)
    if velocities is None:
        chunks = cells // LANE
        for chunk in range(1, chunks):
            rows = out_ref[(chunk - 1) * LANE : chunk * LANE, :]
            blocks_of(moment_sums(rows, basis_ref[...]), chunk, chunks, block_ref)


def outer_kernel(ny, high, final, state_ref, side_x_ref, low_y_ref, high_y_ref, courant_ref, *refs):
    cells, lanes = state_ref.shape
    nx = cells // ny
    first = nx - REACH if high else 0

    def load(x, lane):
        if x < 0:
            ref, x = side_x_ref, x + REACH
        elif x >= nx:
            ref, x = side_x_ref, x - nx
        else:
            ref = state_ref
        return ref[x * ny : (x + 1) * ny, lane : lane + LANE]

    if final:
        _, out_ref, edge_ref, sent = refs

        def write(x, lane, value):
            width = min(LANE, out_ref.shape[2] - lane)
            edge_ref[x - first, :, lane : lane + width] = value[:, :width]

    else:
        basis_ref, *refs = refs
        if high:
            low_sums_ref, inner_block_ref, out_ref, totals_ref, block_ref = refs
        else:
            out_ref, sums_ref = refs

        def write(x, lane, value):
            at = (x - first) * ny
            out_ref[at : at + ny, lane : lane + LANE] = value

    side = side_rows(low_y_ref, high_y_ref)
    xs = range(first, first + REACH)
    transported_rows(load, side, xs, ny, lanes, courant_ref, write)
    if final:
        copy = pltpu.make_async_copy(edge_ref, out_ref.at[first : first + REACH], sent)
        copy.start()
        copy.wait()
        return
    sums = moment_sums(out_ref[...], basis_ref[...])
    if not high:
        sums_ref[...] = sums
        return
    chunks = cells // LANE
    block_ref[...] = inner_block_ref[...]
    sums = jnp.concatenate([low_sums_ref[...], sums], axis=0)
    blocks_of(sums, 0, chunks, block_ref)
    write_totals(chunks, block_ref, totals_ref)


INNER_COST = pl.CostEstimate(flops=30_000_000_000, bytes_accessed=4_000_000, transcendentals=0)


def rows_of(*shape):
    return jax.ShapeDtypeStruct(shape, F32)


def call(kernel, name, out_shape, scratch=(), **options):
    return pl.pallas_call(
        kernel,
        out_shape=out_shape,
        scratch_shapes=scratch,
        compiler_params=pltpu.CompilerParams(vmem_limit_bytes=40 * 1024 * 1024),
        name=name,
        **options,
    )


def gather(totals):
    devices = lax.axis_size("vel")
    copies = jnp.broadcast_to(totals[None], (devices, *totals.shape))
    return lax.all_to_all(copies, "vel", 0, 0)


def ring(axis):
    devices = lax.axis_size(axis)
    up = [(i, (i + 1) % devices) for i in range(devices)]
    return up, [(j, i) for i, j in up]


def body(distribution, cell_kind, local_knudsen):
    nx, ny, velocities = distribution.shape
    lanes = -(-velocities // LANE) * LANE
    cells = nx * ny
    chunks = cells // LANE
    block = pltpu.VMEM((COEFFICIENTS * chunks, LANE), F32)
    totals_shape = rows_of(MOMENTS * chunks, LANE)
    side_x, side_y = rows_of(REACH * ny, lanes), rows_of(REACH * nx, lanes)

    moment_basis, relax_basis, courant = call(
        functools.partial(tables_kernel, velocities),
        "tables",
        (
            jax.ShapeDtypeStruct((lanes, LANE), BF16),
            jax.ShapeDtypeStruct((COEFFICIENTS, 2 * lanes + 2 * LANE), BF16),
            rows_of(SUBLANE, lanes),
        ),
        [pltpu.VMEM((LANE, lanes), F32)],
        in_specs=[pl.BlockSpec(memory_space=pltpu.SMEM)],
    )(jnp.full((1,), lax.axis_index("vel") * velocities, jnp.int32))
    totals = call(first_kernel, "first_moments", totals_shape, [block])(
        distribution, moment_basis
    )
    state = (distribution,)
    for step in range(STEPS):
        final = step == STEPS - 1
        relaxed, low_x, high_x, low_y, high_y = call(
            functools.partial(relax_kernel, ny),
            "relax",
            (rows_of(cells, lanes), side_x, side_x, side_y, side_y),
            [block],
        )(gather(totals), local_knudsen, cell_kind, *state, relax_basis)
        up, down = ring("sy")
        from_low_y = lax.ppermute(high_y, "sy", up)
        from_high_y = lax.ppermute(low_y, "sy", down)
        up, down = ring("sx")
        from_low_x = lax.ppermute(high_x, "sx", up)
        from_high_x = lax.ppermute(low_x, "sx", down)
        sides_y = (from_low_y, from_high_y, courant)
        if final:
            out = call(
                functools.partial(inner_kernel, ny, velocities),
                "last_inner",
                rows_of(nx, ny, velocities),
                cost_estimate=INNER_COST,
            )(relaxed, *sides_y)
            for high, side in enumerate((from_low_x, from_high_x)):
                out = call(
                    functools.partial(outer_kernel, ny, high, True),
                    "last_high" if high else "last_low",
                    rows_of(nx, ny, velocities),
                    [pltpu.VMEM((REACH, ny, velocities), F32), pltpu.SemaphoreType.DMA],
                    in_specs=[pl.BlockSpec(memory_space=pltpu.VMEM)] * 5
                    + [pl.BlockSpec(memory_space=pltpu.HBM)],
                    out_specs=pl.BlockSpec(memory_space=pltpu.HBM),
                    input_output_aliases={5: 0},
                )(relaxed, side, *sides_y, out)
            return out
        inner, inner_block = call(
            functools.partial(inner_kernel, ny, None),
            "inner",
            (rows_of(cells - 2 * REACH * ny, lanes), rows_of(16 * chunks, LANE)),
            cost_estimate=INNER_COST,
        )(relaxed, *sides_y, moment_basis)
        low, low_sums = call(
            functools.partial(outer_kernel, ny, False, False),
            "outer_low",
            (side_x, rows_of(REACH * ny, LANE)),
        )(relaxed, from_low_x, *sides_y, moment_basis)
        high, totals = call(
            functools.partial(outer_kernel, ny, True, False),
            "outer_high",
            (side_x, totals_shape),
            [pltpu.VMEM((16 * chunks, LANE), F32)],
        )(relaxed, from_high_x, *sides_y, moment_basis, low_sums, inner_block)
        state = (inner, low, high)


def solution(mesh):
    return jax.shard_map(
        body,
        mesh=mesh,
        in_specs=(P("sx", "sy", "vel"), P("sx", "sy"), P("sx", "sy")),
        out_specs=P("sx", "sy", "vel"),
        check_vma=False,
    )
```

```python
import functools
import math

import jax
import jax.numpy as jnp
from jax import lax
from jax.experimental import pallas as pl
from jax.experimental.pallas import tpu as pltpu
from jax.sharding import PartitionSpec as P

NVX = 24
STEPS = 2

VEL_LIMIT = 4.8
CLOCK_ADVANCE = 0.09
VISCOUS_RATIO = 2.0 / 3.0
WALL_TEMP = 1.0
INFLOW_DENSITY = 12.0
INFLOW_SPEED = 0.5
INFLOW_TEMP = 1.0

SPACING = 2.0 * VEL_LIMIT / NVX
WEIGHT = SPACING**3
LOG2E = 1.0 / math.log(2.0)

LANE = 128
SUBLANE = 8
REACH = 2
MOMENTS = 13
COEFFICIENTS = 32
F32 = jnp.float32
BF16 = jnp.bfloat16


def lattice(first, velocities, lanes):
    lane = lax.broadcasted_iota(jnp.int32, (1, lanes), 1)
    held = lane < velocities
    index = jnp.where(held, first + lane, 0).astype(F32)

    def split(value, by):
        over = jnp.floor((value + 0.5) * (1.0 / by))
        return over, value - by * over

    def line(points):
        half, odd = split(points, 2.0)
        return jnp.where(odd > 0.5, half, -half - 1.0)

    index, a = split(index, float(NVX))
    c, b = split(index, float(NVX))
    return line(a), line(b), line(c), held


def tables_kernel(velocities, first_ref, moment_ref, relax_ref, courant_ref, turn_ref):
    lanes = courant_ref.shape[1]
    a, b, c, held = lattice(first_ref[0], velocities, lanes)
    zero, one = jnp.zeros((1, lanes), F32), jnp.ones((1, lanes), F32)
    square = a * a + b * b + c * c
    cubic = [a * square, b * square, c * square]
    high = [v.astype(BF16).astype(F32) for v in cubic]
    low = [v - h for v, h in zip(cubic, high)]
    rows = [one, a, b, c, a * a, b * b, c * c, a * b, a * c, b * c, *high, *low]
    rows = [jnp.where(held, v, 0.0) for v in rows]
    turn_ref[...] = jnp.zeros_like(turn_ref)
    for i, value in enumerate(rows):
        turn_ref[i : i + 1, :] = value
    for start in range(0, lanes, LANE):
        turned = turn_ref[:, start : start + LANE].T
        moment_ref[start : start + LANE, :] = turned.astype(BF16)

    half = 0.5 * (square + a + b + c)
    turn_ref[...] = jnp.zeros_like(turn_ref)
    for i, value in enumerate((one, a, b, c, half)):
        for j in range(3):
            turn_ref[3 * i + j : 3 * i + j + 1, :] = jnp.where(held, value, 0.0)
    for i, value in enumerate((one, a, b, c)):
        for j in range(2):
            at = COEFFICIENTS + 15 + 2 * i + j
            turn_ref[at : at + 1, :] = jnp.where(held, value, 0.0)
    for start in range(0, lanes, LANE):
        for i in range(2):
            part = turn_ref[i * COEFFICIENTS : (i + 1) * COEFFICIENTS, start : start + LANE]
            at = 2 * start + i * LANE
            relax_ref[:, at : at + LANE] = part.astype(BF16)
    row = lax.broadcasted_iota(jnp.int32, (COEFFICIENTS, LANE), 0)
    for i in range(2):
        at = 2 * lanes + i * LANE
        picked = jnp.where((row >= 23 + 3 * i) & (row < 26 + 3 * i), 1.0, 0.0)
        relax_ref[:, at : at + LANE] = picked.astype(BF16)

    speeds = [jnp.where(held, CLOCK_ADVANCE * SPACING * (v + 0.5), 0.0) for v in (a, b)]
    signs = [jnp.where(v >= 0.0, 0.5, -0.5) for v in (a, b)]
    for i, value in enumerate([*speeds, *signs, zero, zero, zero, zero]):
        courant_ref[i : i + 1, :] = value


def pieces(value, count):
    out = []
    for _ in range(count - 1):
        high = value.astype(BF16).astype(F32)
        out.append(high)
        value = value - high
    return out + [value]


def moment_sums(rows, basis):
    high = rows.astype(BF16)
    low = (rows - high.astype(F32)).astype(BF16)
    return jnp.dot(high, basis, preferred_element_type=F32) + jnp.dot(
        low, basis, preferred_element_type=F32
    )


def blocks_of(sums, chunk, chunks, block_ref):
    block_ref[pl.ds(chunk, 16, stride=chunks), :] = sums.T[:16, :]


def write_totals(chunks, block_ref, totals_ref):
    totals_ref[: 10 * chunks, :] = block_ref[: 10 * chunks, :]
    totals_ref[10 * chunks :, :] = (
        block_ref[10 * chunks : 13 * chunks, :] + block_ref[13 * chunks : 16 * chunks, :]
    )


def rows_in_chunk(chunk, nx, step):
    if chunk == 0:
        return [*range(REACH), *range(nx - REACH, nx)]
    start = REACH + (chunk - 1) * step
    return list(range(start, start + step))


def coefficients(gathered_ref, knudsen_ref, kind_ref, block_ref):
    nx, ny = kind_ref.shape
    step = LANE // ny
    chunks = nx // step
    for i, value in enumerate((knudsen_ref[...], kind_ref[...].astype(F32))):
        for chunk in range(chunks):
            row = [value[x : x + 1, :] for x in rows_in_chunk(chunk, nx, step)]
            at = (MOMENTS + i) * chunks + chunk
            block_ref[at : at + 1, :] = jnp.concatenate(row, axis=1)
    total = gathered_ref[0]
    for device in range(1, gathered_ref.shape[0]):
        total = total + gathered_ref[device]
    block_ref[: MOMENTS * chunks, :] = total
    n, nx, ny, nz, xx, yy, zz, xy, xz, yz, cx, cy, cz, knudsen, kind = (
        block_ref[i * chunks : (i + 1) * chunks, :] for i in range(MOMENTS + 2)
    )
    inverse = 1.0 / n
    ux, uy, uz = nx * inverse, ny * inverse, nz * inverse
    uu = ux * ux + uy * uy + uz * uz
    trace = xx + yy + zz
    spread = (trace * inverse - uu) / 3.0
    temperature = SPACING * SPACING * spread
    density = WEIGHT * n
    qx = cx - ux * trace - 2.0 * (ux * xx + uy * xy + uz * xz) + 2.0 * ux * uu * n
    qy = cy - uy * trace - 2.0 * (ux * xy + uy * yy + uz * yz) + 2.0 * uy * uu * n
    qz = cz - uz * trace - 2.0 * (ux * xz + uy * yz + uz * zz) + 2.0 * uz * uu * n
    root = jnp.sqrt(temperature)
    keep = jnp.exp(-CLOCK_ADVANCE * density * root / knudsen)
    scale = (1.0 - keep) * density / ((2.0 * math.pi) ** 1.5 * temperature * root)
    heat = (
        scale
        * ((1.0 - VISCOUS_RATIO) * -2.0 * math.log(2.0) / 10.0)
        / (n * spread * spread)
    )

    wall, inflow = kind == 1.0, kind == 2.0
    solid = wall | inflow
    ux = jnp.where(inflow, INFLOW_SPEED / SPACING - 0.5, jnp.where(wall, -0.5, ux))
    uy = jnp.where(solid, -0.5, uy)
    uz = jnp.where(solid, -0.5, uz)
    spread = jnp.where(
        inflow,
        INFLOW_TEMP / SPACING**2,
        jnp.where(wall, WALL_TEMP / SPACING**2, spread),
    )
    scale = jnp.where(
        inflow,
        INFLOW_DENSITY / (2.0 * math.pi * INFLOW_TEMP) ** 1.5,
        jnp.where(wall, density / (2.0 * math.pi * WALL_TEMP) ** 1.5, scale),
    )
    keep = jnp.where(solid, 0.0, keep)
    qx = jnp.where(solid, 0.0, heat * qx)
    qy = jnp.where(solid, 0.0, heat * qy)
    qz = jnp.where(solid, 0.0, heat * qz)
    rate = (0.5 * LOG2E) / spread

    rows = []
    rows += pieces(-rate * (ux * ux + uy * uy + uz * uz), 3)
    for u in (ux, uy, uz):
        rows += pieces(rate * (2.0 * u + 1.0), 3)
    rows += pieces(-2.0 * rate, 3)
    for q in (-(qx * ux + qy * uy + qz * uz), qx, qy, qz):
        rows += pieces(q, 2)
    rows += pieces(keep, 3)
    rows += pieces(scale, 3)
    rows += [jnp.zeros_like(n)] * (COEFFICIENTS - len(rows))
    for i, value in enumerate(rows):
        block_ref[i * chunks : (i + 1) * chunks, :] = value


def relaxed_rows(load, nx, ny, lanes, basis_ref, block_ref, out_ref):
    step = LANE // ny
    chunks, tail = nx // step, 2 * lanes
    for chunk in range(chunks):
        xs = rows_in_chunk(chunk, nx, step)
        left = block_ref[pl.ds(chunk, COEFFICIENTS, stride=chunks), :].T.astype(BF16)
        pair = jnp.dot(left, basis_ref[:, tail : tail + 2 * LANE], preferred_element_type=F32)
        keep, scale = pair[:, :LANE], pair[:, LANE:]
        for lane in range(0, lanes, LANE):
            pair = jnp.dot(
                left, basis_ref[:, 2 * lane : 2 * lane + 2 * LANE], preferred_element_type=F32
            )
            power, linear = pair[:, :LANE], pair[:, LANE:]
            value = load(chunk, xs, lane) * keep + (
                jnp.exp2(power) * (scale + linear * (power + 2.5 * LOG2E))
            )
            for half in (0, step // 2):
                rows = value[half * ny : (half + step // 2) * ny, :]
                at = xs[half] * ny
                out_ref[at : at + rows.shape[0], lane : lane + LANE] = rows


def limited(left, right):
    least, most = jnp.minimum(left, right), jnp.maximum(left, right)
    return jnp.maximum(least, 0.0) + jnp.minimum(most, 0.0)


def transported_rows(load, side, xs, ny, lanes, courant_ref, write):
    row = ny + SUBLANE
    for lane in range(0, lanes, LANE):
        along = slice(lane, lane + LANE)
        speed_x, speed_y = courant_ref[0:1, along], courant_ref[1:2, along]
        half_x, half_y = courant_ref[2:3, along], courant_ref[3:4, along]
        positive_x = jnp.broadcast_to(half_x, (ny, LANE)) > 0.0
        positive_y = jnp.broadcast_to(half_y, (ny, LANE)) > 0.0

        before, centre = load(xs[0] - 2, lane), load(xs[0] - 1, lane)
        slope_before = centre - before
        edge_before = face_before = centre_before = None
        for x in range(xs[0] - 1, xs[-1] + 2):
            after = load(x + 1, lane)
            slope_after = after - centre
            edge = centre + half_x * limited(slope_before, slope_after)
            face = None if edge_before is None else edge - edge_before
            if face_before is not None:
                middle = jnp.concatenate([centre_before, side(x - 1, lane)], axis=0)
                rise = pltpu.roll(middle, row - 1, 0) - middle
                edge_y = middle + half_y * limited(pltpu.roll(rise, 1, 0), rise)
                face_y = pltpu.roll(edge_y, row - 1, 0) - edge_y
                change_x = jnp.where(positive_x, face_before, face)
                change_y = jnp.where(positive_y, pltpu.roll(face_y, 1, 0)[:ny], face_y[:ny])
                write(x - 1, lane, centre_before - speed_x * change_x - speed_y * change_y)
            centre_before, centre = centre, after
            slope_before = slope_after
            edge_before, face_before = edge, face


def side_rows(low_ref, high_ref):
    def side(x, lane):
        at, along = slice(x * REACH, (x + 1) * REACH), slice(lane, lane + LANE)
        gap = jnp.zeros((SUBLANE - 2 * REACH, LANE), F32)
        return jnp.concatenate([high_ref[at, along], gap, low_ref[at, along]], axis=0)

    return side


def first_kernel(state_ref, basis_ref, totals_ref, block_ref):
    nx, ny, velocities = state_ref.shape
    step = LANE // ny
    basis = basis_ref[:velocities, :]
    for chunk in range(nx // step):
        xs = rows_in_chunk(chunk, nx, step)
        halves = [state_ref[xs[i] : xs[i] + step // 2] for i in (0, step // 2)]
        rows = jnp.concatenate(halves, axis=0).reshape(LANE, velocities)
        blocks_of(moment_sums(rows, basis), chunk, nx // step, block_ref)
    write_totals(nx // step, block_ref, totals_ref)


def relax_kernel(ny, gathered_ref, knudsen_ref, kind_ref, *refs):
    *state_refs, basis_ref, out_ref, low_x_ref, high_x_ref, low_y_ref, high_y_ref, block_ref = refs
    cells, lanes = out_ref.shape
    nx = cells // ny
    coefficients(gathered_ref, knudsen_ref, kind_ref, block_ref)

    def load_given(chunk, xs, lane):
        (state_ref,) = state_refs
        velocities = state_ref.shape[2]
        width = min(LANE, velocities - lane)
        half = len(xs) // 2
        parts = [state_ref[xs[i] : xs[i] + half, :, lane : lane + width] for i in (0, half)]
        rows = jnp.concatenate(parts, axis=0).reshape(LANE, width)
        if width == LANE:
            return rows
        return jnp.concatenate([rows, jnp.zeros((LANE, LANE - width), F32)], axis=1)

    def load(chunk, xs, lane):
        inner_ref, low_ref, high_ref = state_refs
        along = slice(lane, lane + LANE)
        if chunk == 0:
            return jnp.concatenate([low_ref[:, along], high_ref[:, along]], axis=0)
        return inner_ref[(chunk - 1) * LANE : chunk * LANE, along]

    load = load_given if len(state_refs) == 1 else load
    relaxed_rows(load, nx, ny, lanes, basis_ref, block_ref, out_ref)
    low_x_ref[...] = out_ref[: REACH * ny, :]
    high_x_ref[...] = out_ref[cells - REACH * ny :, :]
    for x in range(nx):
        at = slice(x * REACH, (x + 1) * REACH)
        low_y_ref[at, :] = out_ref[x * ny : x * ny + REACH, :]
        high_y_ref[at, :] = out_ref[(x + 1) * ny - REACH : (x + 1) * ny, :]


def inner_kernel(ny, velocities, state_ref, low_y_ref, high_y_ref, courant_ref, *refs):
    cells, lanes = state_ref.shape
    nx = cells // ny

    def load(x, lane):
        return state_ref[x * ny : (x + 1) * ny, lane : lane + LANE]

    if velocities is None:
        basis_ref, out_ref, block_ref = refs

        def write(x, lane, value):
            at = (x - REACH) * ny
            out_ref[at : at + ny, lane : lane + LANE] = value

    else:
        (out_ref,) = refs

        def write(x, lane, value):
            width = min(LANE, velocities - lane)
            out_ref[x, :, lane : lane + width] = value[:, :width]

    side = side_rows(low_y_ref, high_y_ref)
    transported_rows(load, side, range(REACH, nx - REACH), ny, lanes, courant_ref, write)
    if velocities is None:
        chunks = cells // LANE
        for chunk in range(1, chunks):
            rows = out_ref[(chunk - 1) * LANE : chunk * LANE, :]
            blocks_of(moment_sums(rows, basis_ref[...]), chunk, chunks, block_ref)


def outer_kernel(ny, high, final, state_ref, side_x_ref, low_y_ref, high_y_ref, courant_ref, *refs):
    cells, lanes = state_ref.shape
    nx = cells // ny
    first = nx - REACH if high else 0

    def load(x, lane):
        if x < 0:
            ref, x = side_x_ref, x + REACH
        elif x >= nx:
            ref, x = side_x_ref, x - nx
        else:
            ref = state_ref
        return ref[x * ny : (x + 1) * ny, lane : lane + LANE]

    if final:
        _, out_ref, edge_ref, sent = refs

        def write(x, lane, value):
            width = min(LANE, out_ref.shape[2] - lane)
            edge_ref[x - first, :, lane : lane + width] = value[:, :width]

    else:
        basis_ref, *refs = refs
        if high:
            low_sums_ref, inner_block_ref, out_ref, totals_ref, block_ref = refs
        else:
            out_ref, sums_ref = refs

        def write(x, lane, value):
            at = (x - first) * ny
            out_ref[at : at + ny, lane : lane + LANE] = value

    side = side_rows(low_y_ref, high_y_ref)
    xs = range(first, first + REACH)
    transported_rows(load, side, xs, ny, lanes, courant_ref, write)
    if final:
        copy = pltpu.make_async_copy(edge_ref, out_ref.at[first : first + REACH], sent)
        copy.start()
        copy.wait()
        return
    sums = moment_sums(out_ref[...], basis_ref[...])
    if not high:
        sums_ref[...] = sums
        return
    chunks = cells // LANE
    block_ref[...] = inner_block_ref[...]
    sums = jnp.concatenate([low_sums_ref[...], sums], axis=0)
    blocks_of(sums, 0, chunks, block_ref)
    write_totals(chunks, block_ref, totals_ref)


INNER_COST = pl.CostEstimate(flops=2_000_000_000, bytes_accessed=1000, transcendentals=0)
LOW_COST = pl.CostEstimate(flops=1_000_000_000, bytes_accessed=1000, transcendentals=0)


def rows_of(*shape):
    return jax.ShapeDtypeStruct(shape, F32)


def call(kernel, name, out_shape, scratch=(), **options):
    return pl.pallas_call(
        kernel,
        out_shape=out_shape,
        scratch_shapes=scratch,
        compiler_params=pltpu.CompilerParams(vmem_limit_bytes=40 * 1024 * 1024),
        name=name,
        **options,
    )


def gather(totals):
    devices = lax.axis_size("vel")
    copies = jnp.broadcast_to(totals[None], (devices, *totals.shape))
    return lax.all_to_all(copies, "vel", 0, 0)


def ring(axis):
    devices = lax.axis_size(axis)
    up = [(i, (i + 1) % devices) for i in range(devices)]
    return up, [(j, i) for i, j in up]


def body(distribution, cell_kind, local_knudsen):
    nx, ny, velocities = distribution.shape
    lanes = -(-velocities // LANE) * LANE
    cells = nx * ny
    chunks = cells // LANE
    block = pltpu.VMEM((COEFFICIENTS * chunks, LANE), F32)
    totals_shape = rows_of(MOMENTS * chunks, LANE)
    side_x, side_y = rows_of(REACH * ny, lanes), rows_of(REACH * nx, lanes)

    moment_basis, relax_basis, courant = call(
        functools.partial(tables_kernel, velocities),
        "tables",
        (
            jax.ShapeDtypeStruct((lanes, LANE), BF16),
            jax.ShapeDtypeStruct((COEFFICIENTS, 2 * lanes + 2 * LANE), BF16),
            rows_of(SUBLANE, lanes),
        ),
        [pltpu.VMEM((LANE, lanes), F32)],
        in_specs=[pl.BlockSpec(memory_space=pltpu.SMEM)],
    )(jnp.full((1,), lax.axis_index("vel") * velocities, jnp.int32))
    totals = call(first_kernel, "first_moments", totals_shape, [block])(
        distribution, moment_basis
    )
    state = (distribution,)
    for step in range(STEPS):
        final = step == STEPS - 1
        relaxed, low_x, high_x, low_y, high_y = call(
            functools.partial(relax_kernel, ny),
            "relax",
            (rows_of(cells, lanes), side_x, side_x, side_y, side_y),
            [block],
        )(gather(totals), local_knudsen, cell_kind, *state, relax_basis)
        up, down = ring("sy")
        from_low_y = lax.ppermute(high_y, "sy", up)
        from_high_y = lax.ppermute(low_y, "sy", down)
        up, down = ring("sx")
        from_low_x = lax.ppermute(high_x, "sx", up)
        from_high_x = lax.ppermute(low_x, "sx", down)
        sides_y = (from_low_y, from_high_y, courant)
        if final:
            out = call(
                functools.partial(inner_kernel, ny, velocities),
                "last_inner",
                rows_of(nx, ny, velocities),
                cost_estimate=INNER_COST,
            )(relaxed, *sides_y)
            for high, side in enumerate((from_low_x, from_high_x)):
                out = call(
                    functools.partial(outer_kernel, ny, high, True),
                    "last_high" if high else "last_low",
                    rows_of(nx, ny, velocities),
                    [pltpu.VMEM((REACH, ny, velocities), F32), pltpu.SemaphoreType.DMA],
                    in_specs=[pl.BlockSpec(memory_space=pltpu.VMEM)] * 5
                    + [pl.BlockSpec(memory_space=pltpu.HBM)],
                    out_specs=pl.BlockSpec(memory_space=pltpu.HBM),
                    input_output_aliases={5: 0},
                    cost_estimate=None if high else LOW_COST,
                )(relaxed, side, *sides_y, out)
            return out
        inner, inner_block = call(
            functools.partial(inner_kernel, ny, None),
            "inner",
            (rows_of(cells - 2 * REACH * ny, lanes), rows_of(16 * chunks, LANE)),
            cost_estimate=INNER_COST,
        )(relaxed, *sides_y, moment_basis)
        low, low_sums = call(
            functools.partial(outer_kernel, ny, False, False),
            "outer_low",
            (side_x, rows_of(REACH * ny, LANE)),
            cost_estimate=LOW_COST,
        )(relaxed, from_low_x, *sides_y, moment_basis)
        high, totals = call(
            functools.partial(outer_kernel, ny, True, False),
            "outer_high",
            (side_x, totals_shape),
            [pltpu.VMEM((16 * chunks, LANE), F32)],
        )(relaxed, from_high_x, *sides_y, moment_basis, low_sums, inner_block)
        state = (inner, low, high)


def solution(mesh):
    return jax.shard_map(
        body,
        mesh=mesh,
        in_specs=(P("sx", "sy", "vel"), P("sx", "sy"), P("sx", "sy")),
        out_specs=P("sx", "sy", "vel"),
        check_vma=False,
    )
```

```python
import functools
import math

import jax
import jax.numpy as jnp
from jax import lax
from jax.experimental import pallas as pl
from jax.experimental.pallas import tpu as pltpu
from jax.sharding import PartitionSpec as P

NVX = 24
STEPS = 2

VEL_LIMIT = 4.8
CLOCK_ADVANCE = 0.09
VISCOUS_RATIO = 2.0 / 3.0
WALL_TEMP = 1.0
INFLOW_DENSITY = 12.0
INFLOW_SPEED = 0.5
INFLOW_TEMP = 1.0

SPACING = 2.0 * VEL_LIMIT / NVX
WEIGHT = SPACING**3
LOG2E = 1.0 / math.log(2.0)

LANE = 128
SUBLANE = 8
REACH = 2
MOMENTS = 13
COEFFICIENTS = 32
F32 = jnp.float32
BF16 = jnp.bfloat16


def lattice(first, velocities, lanes):
    lane = lax.broadcasted_iota(jnp.int32, (1, lanes), 1)
    held = lane < velocities
    index = jnp.where(held, first + lane, 0).astype(F32)

    def split(value, by):
        over = jnp.floor((value + 0.5) * (1.0 / by))
        return over, value - by * over

    def line(points):
        half, odd = split(points, 2.0)
        return jnp.where(odd > 0.5, half, -half - 1.0)

    index, a = split(index, float(NVX))
    c, b = split(index, float(NVX))
    return line(a), line(b), line(c), held


def tables_kernel(velocities, first_ref, moment_ref, relax_ref, courant_ref, turn_ref):
    lanes = courant_ref.shape[1]
    a, b, c, held = lattice(first_ref[0], velocities, lanes)
    zero, one = jnp.zeros((1, lanes), F32), jnp.ones((1, lanes), F32)
    square = a * a + b * b + c * c
    cubic = [a * square, b * square, c * square]
    high = [v.astype(BF16).astype(F32) for v in cubic]
    low = [v - h for v, h in zip(cubic, high)]
    rows = [one, a, b, c, a * a, b * b, c * c, a * b, a * c, b * c, *high, *low]
    rows = [jnp.where(held, v, 0.0) for v in rows]
    turn_ref[...] = jnp.zeros_like(turn_ref)
    for i, value in enumerate(rows):
        turn_ref[i : i + 1, :] = value
    for start in range(0, lanes, LANE):
        turned = turn_ref[:, start : start + LANE].T
        moment_ref[start : start + LANE, :] = turned.astype(BF16)

    half = 0.5 * (square + a + b + c)
    turn_ref[...] = jnp.zeros_like(turn_ref)
    for i, value in enumerate((one, a, b, c, half)):
        for j in range(3):
            turn_ref[3 * i + j : 3 * i + j + 1, :] = jnp.where(held, value, 0.0)
    for i, value in enumerate((one, a, b, c)):
        for j in range(2):
            at = COEFFICIENTS + 15 + 2 * i + j
            turn_ref[at : at + 1, :] = jnp.where(held, value, 0.0)
    for start in range(0, lanes, LANE):
        for i in range(2):
            part = turn_ref[i * COEFFICIENTS : (i + 1) * COEFFICIENTS, start : start + LANE]
            at = 2 * start + i * LANE
            relax_ref[:, at : at + LANE] = part.astype(BF16)
    row = lax.broadcasted_iota(jnp.int32, (COEFFICIENTS, LANE), 0)
    for i in range(2):
        at = 2 * lanes + i * LANE
        picked = jnp.where((row >= 23 + 3 * i) & (row < 26 + 3 * i), 1.0, 0.0)
        relax_ref[:, at : at + LANE] = picked.astype(BF16)

    speeds = [jnp.where(held, CLOCK_ADVANCE * SPACING * (v + 0.5), 0.0) for v in (a, b)]
    signs = [jnp.where(v >= 0.0, 0.5, -0.5) for v in (a, b)]
    for i, value in enumerate([*speeds, *signs, zero, zero, zero, zero]):
        courant_ref[i : i + 1, :] = value


def pieces(value, count):
    out = []
    for _ in range(count - 1):
        high = value.astype(BF16).astype(F32)
        out.append(high)
        value = value - high
    return out + [value]


def moment_sums(rows, basis):
    high = rows.astype(BF16)
    low = (rows - high.astype(F32)).astype(BF16)
    return jnp.dot(high, basis, preferred_element_type=F32) + jnp.dot(
        low, basis, preferred_element_type=F32
    )


def blocks_of(sums, chunk, chunks, block_ref):
    block_ref[pl.ds(chunk, 16, stride=chunks), :] = sums.T[:16, :]


def write_totals(chunks, block_ref, totals_ref):
    totals_ref[: 10 * chunks, :] = block_ref[: 10 * chunks, :]
    totals_ref[10 * chunks :, :] = (
        block_ref[10 * chunks : 13 * chunks, :] + block_ref[13 * chunks : 16 * chunks, :]
    )


def pieces_in_chunk(chunk, nx, ny):
    inner = range(2 * REACH, nx - 2 * REACH)
    if chunk < 2:
        start = REACH * chunk
        xs = [*range(start, start + REACH), *range(nx - start - REACH, nx - start)]
        return [(x, 0, ny) for x in xs]
    end = ny // 4
    if chunk == 2:
        return [(x, y, end) for x in inner for y in (0, ny - end)]
    return [(x, end, ny - 2 * end) for x in inner]


def coefficients(gathered_ref, knudsen_ref, kind_ref, block_ref):
    nx, ny = kind_ref.shape
    chunks = nx * ny // LANE
    for i, value in enumerate((knudsen_ref[...], kind_ref[...].astype(F32))):
        for chunk in range(chunks):
            row = [value[x : x + 1, y : y + n] for x, y, n in pieces_in_chunk(chunk, nx, ny)]
            at = (MOMENTS + i) * chunks + chunk
            block_ref[at : at + 1, :] = jnp.concatenate(row, axis=1)
    total = gathered_ref[0]
    for device in range(1, gathered_ref.shape[0]):
        total = total + gathered_ref[device]
    block_ref[: MOMENTS * chunks, :] = total
    n, nx, ny, nz, xx, yy, zz, xy, xz, yz, cx, cy, cz, knudsen, kind = (
        block_ref[i * chunks : (i + 1) * chunks, :] for i in range(MOMENTS + 2)
    )
    inverse = 1.0 / n
    ux, uy, uz = nx * inverse, ny * inverse, nz * inverse
    uu = ux * ux + uy * uy + uz * uz
    trace = xx + yy + zz
    spread = (trace * inverse - uu) / 3.0
    temperature = SPACING * SPACING * spread
    density = WEIGHT * n
    qx = cx - ux * trace - 2.0 * (ux * xx + uy * xy + uz * xz) + 2.0 * ux * uu * n
    qy = cy - uy * trace - 2.0 * (ux * xy + uy * yy + uz * yz) + 2.0 * uy * uu * n
    qz = cz - uz * trace - 2.0 * (ux * xz + uy * yz + uz * zz) + 2.0 * uz * uu * n
    root = jnp.sqrt(temperature)
    keep = jnp.exp(-CLOCK_ADVANCE * density * root / knudsen)
    scale = (1.0 - keep) * density / ((2.0 * math.pi) ** 1.5 * temperature * root)
    heat = (
        scale
        * ((1.0 - VISCOUS_RATIO) * -2.0 * math.log(2.0) / 10.0)
        / (n * spread * spread)
    )

    wall, inflow = kind == 1.0, kind == 2.0
    solid = wall | inflow
    ux = jnp.where(inflow, INFLOW_SPEED / SPACING - 0.5, jnp.where(wall, -0.5, ux))
    uy = jnp.where(solid, -0.5, uy)
    uz = jnp.where(solid, -0.5, uz)
    spread = jnp.where(
        inflow,
        INFLOW_TEMP / SPACING**2,
        jnp.where(wall, WALL_TEMP / SPACING**2, spread),
    )
    scale = jnp.where(
        inflow,
        INFLOW_DENSITY / (2.0 * math.pi * INFLOW_TEMP) ** 1.5,
        jnp.where(wall, density / (2.0 * math.pi * WALL_TEMP) ** 1.5, scale),
    )
    keep = jnp.where(solid, 0.0, keep)
    qx = jnp.where(solid, 0.0, heat * qx)
    qy = jnp.where(solid, 0.0, heat * qy)
    qz = jnp.where(solid, 0.0, heat * qz)
    rate = (0.5 * LOG2E) / spread

    rows = []
    rows += pieces(-rate * (ux * ux + uy * uy + uz * uz), 3)
    for u in (ux, uy, uz):
        rows += pieces(rate * (2.0 * u + 1.0), 3)
    rows += pieces(-2.0 * rate, 3)
    for q in (-(qx * ux + qy * uy + qz * uz), qx, qy, qz):
        rows += pieces(q, 2)
    rows += pieces(keep, 3)
    rows += pieces(scale, 3)
    rows += [jnp.zeros_like(n)] * (COEFFICIENTS - len(rows))
    for i, value in enumerate(rows):
        block_ref[i * chunks : (i + 1) * chunks, :] = value


def relaxed_rows(load, store, which, chunks, lanes, basis_ref, block_ref):
    tail = 2 * lanes
    for chunk in which:
        left = block_ref[pl.ds(chunk, COEFFICIENTS, stride=chunks), :].T.astype(BF16)
        pair = jnp.dot(left, basis_ref[:, tail : tail + 2 * LANE], preferred_element_type=F32)
        keep, scale = pair[:, :LANE], pair[:, LANE:]
        for lane in range(0, lanes, LANE):
            pair = jnp.dot(
                left, basis_ref[:, 2 * lane : 2 * lane + 2 * LANE], preferred_element_type=F32
            )
            power, linear = pair[:, :LANE], pair[:, LANE:]
            value = load(chunk, lane) * keep + (
                jnp.exp2(power) * (scale + linear * (power + 2.5 * LOG2E))
            )
            store(chunk, lane, value)


def chunk_rows(state_refs, chunk, nx, ny, lane):
    def piece(x, y, n):
        if len(state_refs) == 1:
            width = min(LANE, state_refs[0].shape[2] - lane)
            rows = state_refs[0][x, y : y + n, lane : lane + width]
            if width == LANE:
                return rows
            return jnp.concatenate([rows, jnp.zeros((n, LANE - width), F32)], axis=1)
        inner_ref, low_ref, high_ref = state_refs
        if x < REACH:
            ref, at = low_ref, x * ny
        elif x >= nx - REACH:
            ref, at = high_ref, (x - nx + REACH) * ny
        else:
            ref, at = inner_ref, (x - REACH) * ny
        return ref[at + y : at + y + n, lane : lane + LANE]

    return jnp.concatenate([piece(*p) for p in pieces_in_chunk(chunk, nx, ny)], axis=0)


def limited(left, right):
    least, most = jnp.minimum(left, right), jnp.maximum(left, right)
    return jnp.maximum(least, 0.0) + jnp.minimum(most, 0.0)


def transported_rows(load, side, xs, ny, lanes, courant_ref, write):
    row = ny + SUBLANE
    for lane in range(0, lanes, LANE):
        along = slice(lane, lane + LANE)
        speed_x, speed_y = courant_ref[0:1, along], courant_ref[1:2, along]
        half_x, half_y = courant_ref[2:3, along], courant_ref[3:4, along]
        positive_x = jnp.broadcast_to(half_x, (ny, LANE)) > 0.0
        positive_y = jnp.broadcast_to(half_y, (ny, LANE)) > 0.0

        before, centre = load(xs[0] - 2, lane), load(xs[0] - 1, lane)
        slope_before = centre - before
        edge_before = face_before = centre_before = None
        for x in range(xs[0] - 1, xs[-1] + 2):
            after = load(x + 1, lane)
            slope_after = after - centre
            edge = centre + half_x * limited(slope_before, slope_after)
            face = None if edge_before is None else edge - edge_before
            if face_before is not None:
                middle = jnp.concatenate([centre_before, side(x - 1, lane)], axis=0)
                rise = pltpu.roll(middle, row - 1, 0) - middle
                edge_y = middle + half_y * limited(pltpu.roll(rise, 1, 0), rise)
                face_y = pltpu.roll(edge_y, row - 1, 0) - edge_y
                change_x = jnp.where(positive_x, face_before, face)
                change_y = jnp.where(positive_y, pltpu.roll(face_y, 1, 0)[:ny], face_y[:ny])
                write(x - 1, lane, centre_before - speed_x * change_x - speed_y * change_y)
            centre_before, centre = centre, after
            slope_before = slope_after
            edge_before, face_before = edge, face


def alternate(shape, positive):
    odd = lax.broadcasted_iota(jnp.int32, shape, 1) % 2 == 1
    return odd if positive else ~odd


def pack_layers(near, far, positive, lanes, out_ref):
    for lane in range(0, lanes, LANE):
        along = slice(lane, lane + LANE)
        nearest, second = near(lane), far(lane)
        ny = nearest.shape[0]
        first, rest = second[: ny // 2], second[ny // 2 :]
        out_ref[:ny, along] = nearest
        out_ref[ny:, along] = jnp.where(
            alternate(first.shape, positive), first, pltpu.roll(rest, 1, 1)
        )


def unpack_layer(ref, distance, ny, lane):
    along = slice(lane, lane + LANE)
    if distance == 0:
        return ref[:ny, along]
    packed = ref[ny:, along]
    return jnp.concatenate([packed, pltpu.roll(packed, LANE - 1, 1)], axis=0)


def side_rows(low_ref, high_ref):
    def side(x, lane):
        at, along = slice(x * REACH, (x + 1) * REACH), slice(lane, lane + LANE)
        gap = jnp.zeros((SUBLANE - 2 * REACH, LANE), F32)
        return jnp.concatenate([high_ref[at, along], gap, low_ref[at, along]], axis=0)

    return side


def first_kernel(state_ref, basis_ref, totals_ref, block_ref):
    nx, ny, velocities = state_ref.shape
    chunks = nx * ny // LANE
    basis = basis_ref[:velocities, :]
    for chunk in range(chunks):
        parts = [state_ref[x, y : y + n, :] for x, y, n in pieces_in_chunk(chunk, nx, ny)]
        blocks_of(moment_sums(jnp.concatenate(parts, axis=0), basis), chunk, chunks, block_ref)
    write_totals(chunks, block_ref, totals_ref)


def relax_kernel(ny, gathered_ref, knudsen_ref, kind_ref, *refs):
    *state_refs, basis_ref, out_ref, low_x_ref, high_x_ref, low_y_ref, high_y_ref, block_ref = refs
    cells, lanes = out_ref.shape
    nx, chunks = cells // ny, cells // LANE
    coefficients(gathered_ref, knudsen_ref, kind_ref, block_ref)

    def load(chunk, lane):
        return chunk_rows(state_refs, chunk, nx, ny, lane)

    def store(chunk, lane, value):
        done = 0
        for x, y, n in pieces_in_chunk(chunk, nx, ny):
            at = x * ny + y
            out_ref[at : at + n, lane : lane + LANE] = value[done : done + n, :]
            done += n

    relaxed_rows(load, store, range(chunks - 1), chunks, lanes, basis_ref, block_ref)

    def row_of(x):
        return lambda lane: out_ref[x * ny : (x + 1) * ny, lane : lane + LANE]

    pack_layers(row_of(0), row_of(1), False, lanes, low_x_ref)
    pack_layers(row_of(nx - 1), row_of(nx - 2), True, lanes, high_x_ref)
    for x in range(nx):
        at = slice(x * REACH, (x + 1) * REACH)
        low_y_ref[at, :] = out_ref[x * ny : x * ny + REACH, :]
        high_y_ref[at, :] = out_ref[(x + 1) * ny - REACH : (x + 1) * ny, :]


def inner_kernel(ny, velocities, state_ref, low_y_ref, high_y_ref, courant_ref, coefficient_ref, relax_ref, *refs):
    cells, lanes = state_ref.shape
    nx, chunks = cells // ny, cells // LANE
    *refs, rest_ref = refs
    outputs = 3 if velocities is None else 1
    before_refs, refs = refs[: len(refs) - outputs], refs[len(refs) - outputs :]

    def load_rest(chunk, lane):
        return chunk_rows(before_refs, chunk, nx, ny, lane)

    def store_rest(chunk, lane, value):
        rest_ref[:, lane : lane + LANE] = value

    relaxed_rows(load_rest, store_rest, [chunks - 1], chunks, lanes, relax_ref, coefficient_ref)
    rest = {p[0]: p for p in pieces_in_chunk(chunks - 1, nx, ny)}
    first = min(rest)

    def load(x, lane):
        along, at = slice(lane, lane + LANE), x * ny
        if x not in rest:
            return state_ref[at : at + ny, along]
        _, y, n = rest[x]
        parts = [state_ref[at : at + y, along], rest_ref[(x - first) * n : (x - first + 1) * n, along]]
        return jnp.concatenate([*parts, state_ref[at + y + n : at + ny, along]], axis=0)

    if velocities is None:
        basis_ref, out_ref, block_ref = refs

        def write(x, lane, value):
            at = (x - REACH) * ny
            out_ref[at : at + ny, lane : lane + LANE] = value

    else:
        (out_ref,) = refs

        def write(x, lane, value):
            width = min(LANE, velocities - lane)
            out_ref[x, :, lane : lane + width] = value[:, :width]

    side = side_rows(low_y_ref, high_y_ref)
    transported_rows(load, side, range(REACH, nx - REACH), ny, lanes, courant_ref, write)
    if velocities is None:
        for chunk in range(1, chunks):
            parts = []
            for x, y, n in pieces_in_chunk(chunk, nx, ny):
                at = (x - REACH) * ny + y
                parts.append(out_ref[at : at + n, :])
            sums = moment_sums(jnp.concatenate(parts, axis=0), basis_ref[...])
            blocks_of(sums, chunk, chunks, block_ref)


def outer_kernel(ny, high, final, state_ref, side_x_ref, low_y_ref, high_y_ref, courant_ref, *refs):
    cells, lanes = state_ref.shape
    nx = cells // ny
    first = nx - REACH if high else 0

    def load(x, lane):
        if x < 0:
            return unpack_layer(side_x_ref, -1 - x, ny, lane)
        if x >= nx:
            return unpack_layer(side_x_ref, x - nx, ny, lane)
        return state_ref[x * ny : (x + 1) * ny, lane : lane + LANE]

    if final:
        _, out_ref, edge_ref, sent = refs

        def write(x, lane, value):
            width = min(LANE, out_ref.shape[2] - lane)
            edge_ref[x - first, :, lane : lane + width] = value[:, :width]

    else:
        basis_ref, *refs = refs
        if high:
            low_sums_ref, inner_block_ref, out_ref, totals_ref, block_ref = refs
        else:
            out_ref, sums_ref = refs

        def write(x, lane, value):
            at = (x - first) * ny
            out_ref[at : at + ny, lane : lane + LANE] = value

    side = side_rows(low_y_ref, high_y_ref)
    xs = range(first, first + REACH)
    transported_rows(load, side, xs, ny, lanes, courant_ref, write)
    if final:
        copy = pltpu.make_async_copy(edge_ref, out_ref.at[first : first + REACH], sent)
        copy.start()
        copy.wait()
        return
    sums = moment_sums(out_ref[...], basis_ref[...])
    if not high:
        sums_ref[...] = sums
        return
    chunks = cells // LANE
    block_ref[...] = inner_block_ref[...]
    sums = jnp.concatenate([low_sums_ref[...], sums], axis=0)
    blocks_of(sums, 0, chunks, block_ref)
    write_totals(chunks, block_ref, totals_ref)


INNER_COST = pl.CostEstimate(flops=1_100_000_000, bytes_accessed=1000, transcendentals=0)
LOW_COST = pl.CostEstimate(flops=1_000_000_000, bytes_accessed=1000, transcendentals=0)


def rows_of(*shape):
    return jax.ShapeDtypeStruct(shape, F32)


def call(kernel, name, out_shape, scratch=(), **options):
    return pl.pallas_call(
        kernel,
        out_shape=out_shape,
        scratch_shapes=scratch,
        compiler_params=pltpu.CompilerParams(vmem_limit_bytes=40 * 1024 * 1024),
        name=name,
        **options,
    )


def gather(totals):
    devices = lax.axis_size("vel")
    copies = jnp.broadcast_to(totals[None], (devices, *totals.shape))
    return lax.all_to_all(copies, "vel", 0, 0)


def ring(axis):
    devices = lax.axis_size(axis)
    up = [(i, (i + 1) % devices) for i in range(devices)]
    return up, [(j, i) for i, j in up]


def body(distribution, cell_kind, local_knudsen):
    nx, ny, velocities = distribution.shape
    lanes = -(-velocities // LANE) * LANE
    cells = nx * ny
    chunks = cells // LANE
    block = pltpu.VMEM((COEFFICIENTS * chunks, LANE), F32)
    totals_shape = rows_of(MOMENTS * chunks, LANE)
    edge, side_x, side_y = (rows_of(n, lanes) for n in (REACH * ny, ny + ny // 2, REACH * nx))

    moment_basis, relax_basis, courant = call(
        functools.partial(tables_kernel, velocities),
        "tables",
        (
            jax.ShapeDtypeStruct((lanes, LANE), BF16),
            jax.ShapeDtypeStruct((COEFFICIENTS, 2 * lanes + 2 * LANE), BF16),
            rows_of(SUBLANE, lanes),
        ),
        [pltpu.VMEM((LANE, lanes), F32)],
        in_specs=[pl.BlockSpec(memory_space=pltpu.SMEM)],
    )(jnp.full((1,), lax.axis_index("vel") * velocities, jnp.int32))
    totals = call(first_kernel, "first_moments", totals_shape, [block])(
        distribution, moment_basis
    )
    state = (distribution,)
    for step in range(STEPS):
        final = step == STEPS - 1
        relaxed, low_x, high_x, low_y, high_y, coefficient = call(
            functools.partial(relax_kernel, ny),
            "relax",
            (
                rows_of(cells, lanes), side_x, side_x, side_y, side_y,
                rows_of(COEFFICIENTS * chunks, LANE),
            ),
        )(gather(totals), local_knudsen, cell_kind, *state, relax_basis)
        up, down = ring("sy")
        from_low_y = lax.ppermute(high_y, "sy", up)
        from_high_y = lax.ppermute(low_y, "sy", down)
        up, down = ring("sx")
        from_low_x = lax.ppermute(high_x, "sx", up)
        from_high_x = lax.ppermute(low_x, "sx", down)
        sides_y = (from_low_y, from_high_y, courant)
        if final:
            out = call(
                functools.partial(inner_kernel, ny, velocities),
                "last_inner",
                rows_of(nx, ny, velocities),
                [pltpu.VMEM((LANE, lanes), F32)],
                cost_estimate=INNER_COST,
            )(relaxed, *sides_y, coefficient, relax_basis, *state)
            for high, side in enumerate((from_low_x, from_high_x)):
                out = call(
                    functools.partial(outer_kernel, ny, high, True),
                    "last_high" if high else "last_low",
                    rows_of(nx, ny, velocities),
                    [pltpu.VMEM((REACH, ny, velocities), F32), pltpu.SemaphoreType.DMA],
                    in_specs=[pl.BlockSpec(memory_space=pltpu.VMEM)] * 5
                    + [pl.BlockSpec(memory_space=pltpu.HBM)],
                    out_specs=pl.BlockSpec(memory_space=pltpu.HBM),
                    input_output_aliases={5: 0},
                    cost_estimate=None if high else LOW_COST,
                )(relaxed, side, *sides_y, out)
            return out
        inner, inner_block = call(
            functools.partial(inner_kernel, ny, None),
            "inner",
            (rows_of(cells - 2 * REACH * ny, lanes), rows_of(16 * chunks, LANE)),
            [pltpu.VMEM((LANE, lanes), F32)],
            cost_estimate=INNER_COST,
        )(relaxed, *sides_y, coefficient, relax_basis, *state, moment_basis)
        low, low_sums = call(
            functools.partial(outer_kernel, ny, False, False),
            "outer_low",
            (edge, rows_of(REACH * ny, LANE)),
            cost_estimate=LOW_COST,
        )(relaxed, from_low_x, *sides_y, moment_basis)
        high, totals = call(
            functools.partial(outer_kernel, ny, True, False),
            "outer_high",
            (edge, totals_shape),
            [pltpu.VMEM((16 * chunks, LANE), F32)],
        )(relaxed, from_high_x, *sides_y, moment_basis, low_sums, inner_block)
        state = (inner, low, high)


def solution(mesh):
    return jax.shard_map(
        body,
        mesh=mesh,
        in_specs=(P("sx", "sy", "vel"), P("sx", "sy"), P("sx", "sy")),
        out_specs=P("sx", "sy", "vel"),
        check_vma=False,
    )
```

```python
import functools
import math

import jax
import jax.numpy as jnp
from jax import lax
from jax.experimental import pallas as pl
from jax.experimental.pallas import tpu as pltpu
from jax.sharding import PartitionSpec as P

NVX = 24
STEPS = 2

VEL_LIMIT = 4.8
CLOCK_ADVANCE = 0.09
VISCOUS_RATIO = 2.0 / 3.0
WALL_TEMP = 1.0
INFLOW_DENSITY = 12.0
INFLOW_SPEED = 0.5
INFLOW_TEMP = 1.0

SPACING = 2.0 * VEL_LIMIT / NVX
WEIGHT = SPACING**3
LOG2E = 1.0 / math.log(2.0)

LANE = 128
SUBLANE = 8
REACH = 2
MOMENTS = 13
COEFFICIENTS = 32
F32 = jnp.float32
BF16 = jnp.bfloat16


def lattice(first, velocities, lanes):
    lane = lax.broadcasted_iota(jnp.int32, (1, lanes), 1)
    held = lane < velocities
    index = jnp.where(held, first + lane, 0).astype(F32)

    def split(value, by):
        over = jnp.floor((value + 0.5) * (1.0 / by))
        return over, value - by * over

    def line(points):
        half, odd = split(points, 2.0)
        return jnp.where(odd > 0.5, half, -half - 1.0)

    index, a = split(index, float(NVX))
    c, b = split(index, float(NVX))
    return line(a), line(b), line(c), held


def tables_kernel(velocities, first_ref, moment_ref, relax_ref, courant_ref, turn_ref):
    lanes = courant_ref.shape[1]
    a, b, c, held = lattice(first_ref[0], velocities, lanes)
    zero, one = jnp.zeros((1, lanes), F32), jnp.ones((1, lanes), F32)
    square = a * a + b * b + c * c
    cubic = [a * square, b * square, c * square]
    high = [v.astype(BF16).astype(F32) for v in cubic]
    low = [v - h for v, h in zip(cubic, high)]
    rows = [one, a, b, c, a * a, b * b, c * c, a * b, a * c, b * c, *high, *low]
    rows = [jnp.where(held, v, 0.0) for v in rows]
    turn_ref[...] = jnp.zeros_like(turn_ref)
    for i, value in enumerate(rows):
        turn_ref[i : i + 1, :] = value
    for start in range(0, lanes, LANE):
        turned = turn_ref[:, start : start + LANE].T
        moment_ref[start : start + LANE, :] = turned.astype(BF16)

    half = 0.5 * (square + a + b + c)
    turn_ref[...] = jnp.zeros_like(turn_ref)
    for i, value in enumerate((one, a, b, c, half)):
        for j in range(3):
            turn_ref[3 * i + j : 3 * i + j + 1, :] = jnp.where(held, value, 0.0)
    for i, value in enumerate((one, a, b, c)):
        for j in range(2):
            at = COEFFICIENTS + 15 + 2 * i + j
            turn_ref[at : at + 1, :] = jnp.where(held, value, 0.0)
    for start in range(0, lanes, LANE):
        for i in range(2):
            part = turn_ref[i * COEFFICIENTS : (i + 1) * COEFFICIENTS, start : start + LANE]
            at = 2 * start + i * LANE
            relax_ref[:, at : at + LANE] = part.astype(BF16)
    row = lax.broadcasted_iota(jnp.int32, (COEFFICIENTS, LANE), 0)
    for i in range(2):
        at = 2 * lanes + i * LANE
        picked = jnp.where((row >= 23 + 3 * i) & (row < 26 + 3 * i), 1.0, 0.0)
        relax_ref[:, at : at + LANE] = picked.astype(BF16)

    speeds = [jnp.where(held, CLOCK_ADVANCE * SPACING * (v + 0.5), 0.0) for v in (a, b)]
    signs = [jnp.where(v >= 0.0, 0.5, -0.5) for v in (a, b)]
    for i, value in enumerate([*speeds, *signs, zero, zero, zero, zero]):
        courant_ref[i : i + 1, :] = value


def pieces(value, count):
    out = []
    for _ in range(count - 1):
        high = value.astype(BF16).astype(F32)
        out.append(high)
        value = value - high
    return out + [value]


def moment_sums(rows, basis):
    high = rows.astype(BF16)
    low = (rows - high.astype(F32)).astype(BF16)
    return jnp.dot(high, basis, preferred_element_type=F32) + jnp.dot(
        low, basis, preferred_element_type=F32
    )


def blocks_of(sums, chunk, chunks, block_ref):
    block_ref[pl.ds(chunk, 16, stride=chunks), :] = sums.T[:16, :]


def write_totals(chunks, block_ref, totals_ref):
    totals_ref[: 10 * chunks, :] = block_ref[: 10 * chunks, :]
    totals_ref[10 * chunks :, :] = (
        block_ref[10 * chunks : 13 * chunks, :] + block_ref[13 * chunks : 16 * chunks, :]
    )


def pieces_in_chunk(chunk, nx, ny):
    inner = range(2 * REACH, nx - 2 * REACH)
    if chunk < 2:
        start = REACH * chunk
        xs = [*range(start, start + REACH), *range(nx - start - REACH, nx - start)]
        return [(x, 0, ny) for x in xs]
    end = ny // 4
    if chunk == 2:
        return [(x, y, end) for x in inner for y in (0, ny - end)]
    return [(x, end, ny - 2 * end) for x in inner]


def coefficients(gathered_ref, knudsen_ref, kind_ref, block_ref):
    nx, ny = kind_ref.shape
    chunks = nx * ny // LANE
    for i, value in enumerate((knudsen_ref[...], kind_ref[...].astype(F32))):
        for chunk in range(chunks):
            row = [value[x : x + 1, y : y + n] for x, y, n in pieces_in_chunk(chunk, nx, ny)]
            at = (MOMENTS + i) * chunks + chunk
            block_ref[at : at + 1, :] = jnp.concatenate(row, axis=1)
    total = gathered_ref[0]
    for device in range(1, gathered_ref.shape[0]):
        total = total + gathered_ref[device]
    block_ref[: MOMENTS * chunks, :] = total
    n, nx, ny, nz, xx, yy, zz, xy, xz, yz, cx, cy, cz, knudsen, kind = (
        block_ref[i * chunks : (i + 1) * chunks, :] for i in range(MOMENTS + 2)
    )
    inverse = 1.0 / n
    ux, uy, uz = nx * inverse, ny * inverse, nz * inverse
    uu = ux * ux + uy * uy + uz * uz
    trace = xx + yy + zz
    spread = (trace * inverse - uu) / 3.0
    temperature = SPACING * SPACING * spread
    density = WEIGHT * n
    qx = cx - ux * trace - 2.0 * (ux * xx + uy * xy + uz * xz) + 2.0 * ux * uu * n
    qy = cy - uy * trace - 2.0 * (ux * xy + uy * yy + uz * yz) + 2.0 * uy * uu * n
    qz = cz - uz * trace - 2.0 * (ux * xz + uy * yz + uz * zz) + 2.0 * uz * uu * n
    root = jnp.sqrt(temperature)
    keep = jnp.exp(-CLOCK_ADVANCE * density * root / knudsen)
    scale = (1.0 - keep) * density / ((2.0 * math.pi) ** 1.5 * temperature * root)
    heat = (
        scale
        * ((1.0 - VISCOUS_RATIO) * -2.0 * math.log(2.0) / 10.0)
        / (n * spread * spread)
    )

    wall, inflow = kind == 1.0, kind == 2.0
    solid = wall | inflow
    ux = jnp.where(inflow, INFLOW_SPEED / SPACING - 0.5, jnp.where(wall, -0.5, ux))
    uy = jnp.where(solid, -0.5, uy)
    uz = jnp.where(solid, -0.5, uz)
    spread = jnp.where(
        inflow,
        INFLOW_TEMP / SPACING**2,
        jnp.where(wall, WALL_TEMP / SPACING**2, spread),
    )
    scale = jnp.where(
        inflow,
        INFLOW_DENSITY / (2.0 * math.pi * INFLOW_TEMP) ** 1.5,
        jnp.where(wall, density / (2.0 * math.pi * WALL_TEMP) ** 1.5, scale),
    )
    keep = jnp.where(solid, 0.0, keep)
    qx = jnp.where(solid, 0.0, heat * qx)
    qy = jnp.where(solid, 0.0, heat * qy)
    qz = jnp.where(solid, 0.0, heat * qz)
    rate = (0.5 * LOG2E) / spread

    rows = []
    rows += pieces(-rate * (ux * ux + uy * uy + uz * uz), 3)
    for u in (ux, uy, uz):
        rows += pieces(rate * (2.0 * u + 1.0), 3)
    rows += pieces(-2.0 * rate, 3)
    for q in (-(qx * ux + qy * uy + qz * uz), qx, qy, qz):
        rows += pieces(q, 2)
    rows += pieces(keep, 3)
    rows += pieces(scale, 3)
    rows += [jnp.zeros_like(n)] * (COEFFICIENTS - len(rows))
    for i, value in enumerate(rows):
        block_ref[i * chunks : (i + 1) * chunks, :] = value


def relaxed_rows(load, store, which, chunks, lanes, basis_ref, block_ref):
    tail = 2 * lanes
    for chunk in which:
        left = block_ref[pl.ds(chunk, COEFFICIENTS, stride=chunks), :].T.astype(BF16)
        pair = jnp.dot(left, basis_ref[:, tail : tail + 2 * LANE], preferred_element_type=F32)
        keep, scale = pair[:, :LANE], pair[:, LANE:]
        for lane in range(0, lanes, LANE):
            pair = jnp.dot(
                left, basis_ref[:, 2 * lane : 2 * lane + 2 * LANE], preferred_element_type=F32
            )
            power, linear = pair[:, :LANE], pair[:, LANE:]
            value = load(chunk, lane) * keep + (
                jnp.exp2(power) * (scale + linear * (power + 2.5 * LOG2E))
            )
            store(chunk, lane, value)


def chunk_rows(state_refs, chunk, nx, ny, lane):
    def piece(x, y, n):
        if len(state_refs) == 1:
            width = min(LANE, state_refs[0].shape[2] - lane)
            rows = state_refs[0][x, y : y + n, lane : lane + width]
            if width == LANE:
                return rows
            return jnp.concatenate([rows, jnp.zeros((n, LANE - width), F32)], axis=1)
        inner_ref, edges_ref = state_refs
        if x < REACH:
            ref, at = edges_ref, x * ny
        elif x >= nx - REACH:
            ref, at = edges_ref, (x - nx + 2 * REACH) * ny
        else:
            ref, at = inner_ref, (x - REACH) * ny
        return ref[at + y : at + y + n, lane : lane + LANE]

    return jnp.concatenate([piece(*p) for p in pieces_in_chunk(chunk, nx, ny)], axis=0)


def limited(left, right):
    least, most = jnp.minimum(left, right), jnp.maximum(left, right)
    return jnp.maximum(least, 0.0) + jnp.minimum(most, 0.0)


def transported_rows(load, side, xs, ny, lanes, courant_ref, write):
    row = ny + SUBLANE
    for lane in range(0, lanes, LANE):
        along = slice(lane, lane + LANE)
        speed_x, speed_y = courant_ref[0:1, along], courant_ref[1:2, along]
        half_x, half_y = courant_ref[2:3, along], courant_ref[3:4, along]
        positive_x = jnp.broadcast_to(half_x, (ny, LANE)) > 0.0
        positive_y = jnp.broadcast_to(half_y, (ny, LANE)) > 0.0

        before, centre = load(xs[0] - 2, lane), load(xs[0] - 1, lane)
        slope_before = centre - before
        edge_before = face_before = centre_before = None
        for x in range(xs[0] - 1, xs[-1] + 2):
            after = load(x + 1, lane)
            slope_after = after - centre
            edge = centre + half_x * limited(slope_before, slope_after)
            face = None if edge_before is None else edge - edge_before
            if face_before is not None:
                middle = jnp.concatenate([centre_before, side(x - 1, lane)], axis=0)
                rise = pltpu.roll(middle, row - 1, 0) - middle
                edge_y = middle + half_y * limited(pltpu.roll(rise, 1, 0), rise)
                face_y = pltpu.roll(edge_y, row - 1, 0) - edge_y
                change_x = jnp.where(positive_x, face_before, face)
                change_y = jnp.where(positive_y, pltpu.roll(face_y, 1, 0)[:ny], face_y[:ny])
                write(x - 1, lane, centre_before - speed_x * change_x - speed_y * change_y)
            centre_before, centre = centre, after
            slope_before = slope_after
            edge_before, face_before = edge, face

def alternate(shape, positive):
    odd = lax.broadcasted_iota(jnp.int32, shape, 1) % 2 == 1
    return odd if positive else ~odd


def pack_layers(near, far, positive, lanes, out_ref):
    for lane in range(0, lanes, LANE):
        along = slice(lane, lane + LANE)
        nearest, second = near(lane), far(lane)
        ny = nearest.shape[0]
        first, rest = second[: ny // 2], second[ny // 2 :]
        out_ref[:ny, along] = nearest
        out_ref[ny:, along] = jnp.where(
            alternate(first.shape, positive), first, pltpu.roll(rest, 1, 1)
        )


def unpack_layer(ref, distance, ny, lane):
    along = slice(lane, lane + LANE)
    if distance == 0:
        return ref[:ny, along]
    packed = ref[ny:, along]
    return jnp.concatenate([packed, pltpu.roll(packed, LANE - 1, 1)], axis=0)


def run_alternate(shape, lane, positive):
    odd = (lax.broadcasted_iota(jnp.int32, shape, 1) + lane) // NVX % 2 == 1
    return odd if positive else ~odd


def pack_ends(state_ref, near, far, ny, positive, out_ref, far_ref):
    nx, lanes = far_ref.shape
    for x in range(nx):
        out_ref[x : x + 1, :] = state_ref[x * ny + near : x * ny + near + 1, :]
        far_ref[x : x + 1, :] = state_ref[x * ny + far : x * ny + far + 1, :]
    before = None
    for lane in range(0, lanes, LANE):
        along = slice(lane, lane + LANE)
        second = far_ref[:, along]
        half = nx // 2
        turned = pltpu.roll(second[half:], NVX, 1)
        moved = turned
        if before is not None:
            crossed = lax.broadcasted_iota(jnp.int32, turned.shape, 1) < NVX
            moved = jnp.where(crossed, before, turned)
        before = turned
        own = run_alternate(turned.shape, lane, positive)
        out_ref[nx:, along] = jnp.where(own, second[:half], moved)


def unpack_ends(ref, near_at, far_at, side_ref):
    rows, lanes = ref.shape
    half = rows // 3
    after = None
    for lane in range(lanes - LANE, -1, -LANE):
        along = slice(lane, lane + LANE)
        block = lane // LANE
        side_ref[block, pl.ds(near_at, 2 * half, stride=SUBLANE), :] = ref[: 2 * half, along]
        packed = ref[2 * half :, along]
        turned = pltpu.roll(packed, LANE - NVX, 1)
        moved = turned
        if after is not None:
            crossed = lax.broadcasted_iota(jnp.int32, turned.shape, 1) >= LANE - NVX
            moved = jnp.where(crossed, after, turned)
        after = turned
        both = jnp.concatenate([packed, moved], axis=0)
        side_ref[block, pl.ds(far_at, 2 * half, stride=SUBLANE), :] = both


def side_rows(side_ref):
    def side(x, lane):
        return side_ref[lane // LANE, x * SUBLANE : (x + 1) * SUBLANE, :]

    return side


def first_kernel(state_ref, basis_ref, totals_ref, block_ref):
    nx, ny, velocities = state_ref.shape
    chunks = nx * ny // LANE
    basis = basis_ref[:velocities, :]
    for chunk in range(chunks):
        parts = [state_ref[x, y : y + n, :] for x, y, n in pieces_in_chunk(chunk, nx, ny)]
        blocks_of(moment_sums(jnp.concatenate(parts, axis=0), basis), chunk, chunks, block_ref)
    write_totals(chunks, block_ref, totals_ref)


def by_parity(odd_ref, do, first_ref, second_ref):
    @pl.when(odd_ref[0] == 0)
    def _():
        do(second_ref, first_ref)

    @pl.when(odd_ref[0] != 0)
    def _():
        do(first_ref, second_ref)


def relax_kernel(ny, odd_x_ref, odd_y_ref, gathered_ref, knudsen_ref, kind_ref, *refs):
    *state_refs, basis_ref, out_ref, first_x_ref, second_x_ref, first_y_ref, second_y_ref = refs[:-2]
    block_ref, far_ref = refs[-2:]
    cells, lanes = out_ref.shape
    nx, chunks = cells // ny, cells // LANE
    coefficients(gathered_ref, knudsen_ref, kind_ref, block_ref)

    def load(chunk, lane):
        return chunk_rows(state_refs, chunk, nx, ny, lane)

    def store(chunk, lane, value):
        done = 0
        for x, y, n in pieces_in_chunk(chunk, nx, ny):
            at = x * ny + y
            out_ref[at : at + n, lane : lane + LANE] = value[done : done + n, :]
            done += n

    relaxed_rows(load, store, range(chunks - 1), chunks, lanes, basis_ref, block_ref)


    def row_of(x):
        return lambda lane: out_ref[x * ny : (x + 1) * ny, lane : lane + LANE]

    def pack_x(low_ref, high_ref):
        pack_layers(row_of(0), row_of(1), False, lanes, low_ref)
        pack_layers(row_of(nx - 1), row_of(nx - 2), True, lanes, high_ref)

    def pack_y(low_ref, high_ref):
        pack_ends(out_ref, 0, 1, ny, False, low_ref, far_ref)
        pack_ends(out_ref, ny - 1, ny - 2, ny, True, high_ref, far_ref)

    by_parity(odd_x_ref, pack_x, first_x_ref, second_x_ref)
    by_parity(odd_y_ref, pack_y, first_y_ref, second_y_ref)


def inner_kernel(ny, velocities, odd_y_ref, state_ref, first_y_ref, second_y_ref, courant_ref, coefficient_ref, relax_ref, *refs):
    cells, lanes = state_ref.shape
    nx, chunks = cells // ny, cells // LANE
    if velocities is None:
        *refs, side_ref, rest_ref = refs
        outputs = 3
    else:
        *refs, side_ref, rest_ref, stage_ref, sent = refs
        outputs = 1
    before_refs, refs = refs[: len(refs) - outputs], refs[len(refs) - outputs :]

    def load_rest(chunk, lane):
        return chunk_rows(before_refs, chunk, nx, ny, lane)

    def store_rest(chunk, lane, value):
        rest_ref[:, lane : lane + LANE] = value

    relaxed_rows(load_rest, store_rest, [chunks - 1], chunks, lanes, relax_ref, coefficient_ref)
    rest = {p[0]: p for p in pieces_in_chunk(chunks - 1, nx, ny)}
    first = min(rest)

    def load(x, lane):
        along, at = slice(lane, lane + LANE), x * ny
        if x not in rest:
            return state_ref[at : at + ny, along]
        _, y, n = rest[x]
        parts = [state_ref[at : at + y, along], rest_ref[(x - first) * n : (x - first + 1) * n, along]]
        return jnp.concatenate([*parts, state_ref[at + y + n : at + ny, along]], axis=0)

    side_ref[...] = jnp.zeros_like(side_ref)

    def unpack_y(low_ref, high_ref):
        unpack_ends(high_ref, 0, 1, side_ref)
        unpack_ends(low_ref, SUBLANE - 1, SUBLANE - 2, side_ref)

    by_parity(odd_y_ref, unpack_y, first_y_ref, second_y_ref)
    copies = []
    if velocities is None:
        basis_ref, out_ref, block_ref = refs

        def write(x, lane, value):
            at = (x - REACH) * ny
            out_ref[at : at + ny, lane : lane + LANE] = value

        groups = 1
    else:
        (out_ref,) = refs
        groups = sent.shape[0]

        def write(x, lane, value):
            width = min(LANE, velocities - lane)
            stage_ref[x - REACH, :, lane : lane + width] = value[:, :width]

    count = (nx - 2 * REACH) // groups
    for group in range(groups):
        start = REACH + group * count
        xs = range(start, start + count)
        transported_rows(load, side_rows(side_ref), xs, ny, lanes, courant_ref, write)
        if velocities is not None:
            part = stage_ref.at[start - REACH : start - REACH + count]
            copies.append(
                pltpu.make_async_copy(part, out_ref.at[start : start + count], sent.at[group])
            )
            copies[-1].start()
    for copy in copies:
        copy.wait()
    if velocities is None:
        for chunk in range(1, chunks):
            parts = []
            for x, y, n in pieces_in_chunk(chunk, nx, ny):
                at = (x - REACH) * ny + y
                parts.append(out_ref[at : at + n, :])
            sums = moment_sums(jnp.concatenate(parts, axis=0), basis_ref[...])
            blocks_of(sums, chunk, chunks, block_ref)


def outer_kernel(ny, second, final, odd_x_ref, state_ref, side_x_ref, side_ref, courant_ref, *refs):
    cells, lanes = state_ref.shape
    nx, edge = cells // ny, REACH * ny
    odd = odd_x_ref[0] != 0
    high = odd if second else ~odd

    def load(x, lane):
        if x < 0:
            return unpack_layer(side_x_ref, -1 - x, ny, lane)
        if x >= nx:
            return unpack_layer(side_x_ref, x - nx, ny, lane)
        return state_ref[x * ny : (x + 1) * ny, lane : lane + LANE]

    def transport(write):
        for start, chosen in ((0, ~high), (nx - REACH, high)):

            @pl.when(chosen)
            def _(start=start):
                def write_row(x, lane, value):
                    write(x - start, lane, value)

                xs = range(start, start + REACH)
                transported_rows(load, side_rows(side_ref), xs, ny, lanes, courant_ref, write_row)

    if final:
        if second:
            other_ref, _, out_ref, edge_ref, sent = refs
            own_at = jnp.where(high, nx - REACH, 0)
            other_at = jnp.where(high, 0, nx - REACH)
            other_copy = pltpu.make_async_copy(
                other_ref, out_ref.at[pl.ds(other_at, REACH)], sent.at[0]
            )
            other_copy.start()
        else:
            (edge_ref,) = refs

        def write(x, lane, value):
            width = min(LANE, edge_ref.shape[2] - lane)
            edge_ref[x, :, lane : lane + width] = value[:, :width]

        transport(write)
        if second:
            copy = pltpu.make_async_copy(
                edge_ref, out_ref.at[pl.ds(own_at, REACH)], sent.at[1]
            )
            copy.start()
            other_copy.wait()
            copy.wait()
        return

    basis_ref, *refs = refs
    if second:
        other_ref, other_sums_ref, inner_block_ref, edges_ref, totals_ref, own_ref, sums_ref, block_ref = refs
    else:
        own_ref, own_sums_ref = refs

    def write(x, lane, value):
        own_ref[x * ny : (x + 1) * ny, lane : lane + LANE] = value

    transport(write)
    own_sums = moment_sums(own_ref[...], basis_ref[...])
    if not second:
        own_sums_ref[...] = own_sums
        return
    own_at = pl.multiple_of(jnp.where(high, edge, 0), edge)
    other_at = pl.multiple_of(jnp.where(high, 0, edge), edge)
    edges_ref[pl.ds(own_at, edge), :] = own_ref[...]
    edges_ref[pl.ds(other_at, edge), :] = other_ref[...]
    sums_ref[pl.ds(own_at, edge), :] = own_sums
    sums_ref[pl.ds(other_at, edge), :] = other_sums_ref[...]
    chunks = cells // LANE
    block_ref[...] = inner_block_ref[...]
    blocks_of(sums_ref[...], 0, chunks, block_ref)
    write_totals(chunks, block_ref, totals_ref)


INNER_COST = pl.CostEstimate(flops=1_100_000_000, bytes_accessed=1000, transcendentals=0)
LOW_COST = pl.CostEstimate(flops=1_000_000_000, bytes_accessed=1000, transcendentals=0)


def rows_of(*shape):
    return jax.ShapeDtypeStruct(shape, F32)


def call(kernel, name, out_shape, scratch=(), **options):
    return pl.pallas_call(
        kernel,
        out_shape=out_shape,
        scratch_shapes=scratch,
        compiler_params=pltpu.CompilerParams(vmem_limit_bytes=40 * 1024 * 1024),
        name=name,
        **options,
    )


def gather(totals):
    devices = lax.axis_size("vel")
    copies = jnp.broadcast_to(totals[None], (devices, *totals.shape))
    return lax.all_to_all(copies, "vel", 0, 0)


def partners(axis):
    devices = lax.axis_size(axis)
    pairs = []
    for first in (0, 1):
        couples = [((i + first) % devices, (i + first + 1) % devices) for i in range(0, devices, 2)]
        pairs.append(couples + [(b, a) for a, b in couples])
    return pairs


def body(distribution, cell_kind, local_knudsen):
    nx, ny, velocities = distribution.shape
    lanes = -(-velocities // LANE) * LANE
    cells = nx * ny
    chunks = cells // LANE
    block = pltpu.VMEM((COEFFICIENTS * chunks, LANE), F32)
    totals_shape = rows_of(MOMENTS * chunks, LANE)
    edge, side_x, side_y = (rows_of(n, lanes) for n in (REACH * ny, ny + ny // 2, nx + nx // 2))

    first, odd_x, odd_y = lax.optimization_barrier(
        tuple(
            jnp.full((1,), value, jnp.int32)
            for value in (
                lax.axis_index("vel") * velocities,
                lax.axis_index("sx") % 2,
                lax.axis_index("sy") % 2,
            )
        )
    )
    moment_basis, relax_basis, courant = call(
        functools.partial(tables_kernel, velocities),
        "tables",
        (
            jax.ShapeDtypeStruct((lanes, LANE), BF16),
            jax.ShapeDtypeStruct((COEFFICIENTS, 2 * lanes + 2 * LANE), BF16),
            rows_of(SUBLANE, lanes),
        ),
        [pltpu.VMEM((LANE, lanes), F32)],
        in_specs=[pl.BlockSpec(memory_space=pltpu.SMEM)],
    )(first)
    totals = call(first_kernel, "first_moments", totals_shape, [block])(
        distribution, moment_basis
    )
    state = (distribution,)
    for step in range(STEPS):
        final = step == STEPS - 1
        smem, vmem, hbm = (
            pl.BlockSpec(memory_space=m) for m in (pltpu.SMEM, pltpu.VMEM, pltpu.HBM)
        )
        operands = (gather(totals), local_knudsen, cell_kind, *state, relax_basis)
        relaxed, first_x, second_x, first_y, second_y, coefficient = call(
            functools.partial(relax_kernel, ny),
            "relax",
            (
                rows_of(cells, lanes), side_x, side_x, side_y, side_y,
                rows_of(COEFFICIENTS * chunks, LANE),
            ),
            [pltpu.VMEM((nx, lanes), F32)],
            in_specs=[smem, smem] + [vmem] * len(operands),
        )(odd_x, odd_y, *operands)
        to_first, to_second = partners("sy")
        sides_y = (lax.ppermute(first_y, "sy", to_first), lax.ppermute(second_y, "sy", to_second))
        to_first, to_second = partners("sx")
        first_x = lax.ppermute(first_x, "sx", to_first)
        second_x = lax.ppermute(second_x, "sx", to_second)
        side_shape = rows_of(lanes // LANE, nx * SUBLANE, LANE)
        rest = pltpu.VMEM((LANE, lanes), F32)
        operands = (relaxed, *sides_y, courant, coefficient, relax_basis, *state)
        if final:
            inner, side = call(
                functools.partial(inner_kernel, ny, velocities),
                "last_inner",
                (rows_of(nx, ny, velocities), side_shape),
                [
                    rest,
                    pltpu.VMEM((nx - 2 * REACH, ny, velocities), F32),
                    pltpu.SemaphoreType.DMA((3,)),
                ],
                in_specs=[smem] + [vmem] * len(operands),
                out_specs=(hbm, vmem),
                cost_estimate=INNER_COST,
            )(odd_y, *operands)
            ends = rows_of(REACH, ny, velocities)
            other = call(
                functools.partial(outer_kernel, ny, False, True),
                "last_first",
                ends,
                in_specs=[smem] + [vmem] * 4,
                cost_estimate=LOW_COST,
            )(odd_x, relaxed, first_x, side, courant)
            return call(
                functools.partial(outer_kernel, ny, True, True),
                "last_second",
                rows_of(nx, ny, velocities),
                [pltpu.VMEM(ends.shape, F32), pltpu.SemaphoreType.DMA((2,))],
                in_specs=[smem] + [vmem] * 5 + [hbm],
                out_specs=hbm,
                input_output_aliases={6: 0},
            )(odd_x, relaxed, second_x, side, courant, other, inner)
        inner, inner_block, side = call(
            functools.partial(inner_kernel, ny, None),
            "inner",
            (rows_of(cells - 2 * REACH * ny, lanes), rows_of(16 * chunks, LANE), side_shape),
            [rest],
            in_specs=[smem] + [vmem] * (len(operands) + 1),
            cost_estimate=INNER_COST,
        )(odd_y, *operands, moment_basis)
        other, other_sums = call(
            functools.partial(outer_kernel, ny, False, False),
            "outer_first",
            (edge, rows_of(REACH * ny, LANE)),
            in_specs=[smem] + [vmem] * 5,
            cost_estimate=LOW_COST,
        )(odd_x, relaxed, first_x, side, courant, moment_basis)
        edges, totals = call(
            functools.partial(outer_kernel, ny, True, False),
            "outer_second",
            (rows_of(2 * REACH * ny, lanes), totals_shape),
            [
                pltpu.VMEM((REACH * ny, lanes), F32),
                pltpu.VMEM((2 * REACH * ny, LANE), F32),
                pltpu.VMEM((16 * chunks, LANE), F32),
            ],
            in_specs=[smem] + [vmem] * 8,
        )(odd_x, relaxed, second_x, side, courant, moment_basis, other, other_sums, inner_block)
        state = (inner, edges)


def solution(mesh):
    return jax.shard_map(
        body,
        mesh=mesh,
        in_specs=(P("sx", "sy", "vel"), P("sx", "sy"), P("sx", "sy")),
        out_specs=P("sx", "sy", "vel"),
        check_vma=False,
    )
```

```python
import functools
import math

import jax
import jax.numpy as jnp
from jax import lax
from jax.experimental import pallas as pl
from jax.experimental.pallas import tpu as pltpu
from jax.sharding import PartitionSpec as P

NVX = 24
STEPS = 2

VEL_LIMIT = 4.8
CLOCK_ADVANCE = 0.09
VISCOUS_RATIO = 2.0 / 3.0
WALL_TEMP = 1.0
INFLOW_DENSITY = 12.0
INFLOW_SPEED = 0.5
INFLOW_TEMP = 1.0

SPACING = 2.0 * VEL_LIMIT / NVX
WEIGHT = SPACING**3
LOG2E = 1.0 / math.log(2.0)

LANE = 128
SUBLANE = 8
REACH = 2
MOMENTS = 13
COEFFICIENTS = 32
F32 = jnp.float32
BF16 = jnp.bfloat16


def lattice(first, velocities, lanes):
    lane = lax.broadcasted_iota(jnp.int32, (1, lanes), 1)
    held = lane < velocities
    index = jnp.where(held, first + lane, 0).astype(F32)

    def split(value, by):
        over = jnp.floor((value + 0.5) * (1.0 / by))
        return over, value - by * over

    def line(points):
        half, odd = split(points, 2.0)
        return jnp.where(odd > 0.5, half, -half - 1.0)

    index, a = split(index, float(NVX))
    c, b = split(index, float(NVX))
    return line(a), line(b), line(c), held


def tables_kernel(velocities, first_ref, moment_ref, relax_ref, courant_ref, turn_ref):
    lanes = courant_ref.shape[1]
    a, b, c, held = lattice(first_ref[0], velocities, lanes)
    zero, one = jnp.zeros((1, lanes), F32), jnp.ones((1, lanes), F32)
    square = a * a + b * b + c * c
    cubic = [a * square, b * square, c * square]
    high = [v.astype(BF16).astype(F32) for v in cubic]
    low = [v - h for v, h in zip(cubic, high)]
    rows = [one, a, b, c, a * a, b * b, c * c, a * b, a * c, b * c, *high, *low]
    rows = [jnp.where(held, v, 0.0) for v in rows]
    turn_ref[...] = jnp.zeros_like(turn_ref)
    for i, value in enumerate(rows):
        turn_ref[i : i + 1, :] = value
    for start in range(0, lanes, LANE):
        turned = turn_ref[:, start : start + LANE].T
        moment_ref[start : start + LANE, :] = turned.astype(BF16)

    half = 0.5 * (square + a + b + c)
    turn_ref[...] = jnp.zeros_like(turn_ref)
    for i, value in enumerate((one, a, b, c, half)):
        for j in range(3):
            turn_ref[3 * i + j : 3 * i + j + 1, :] = jnp.where(held, value, 0.0)
    for i, value in enumerate((one, a, b, c)):
        for j in range(2):
            at = COEFFICIENTS + 15 + 2 * i + j
            turn_ref[at : at + 1, :] = jnp.where(held, value, 0.0)
    for start in range(0, lanes, LANE):
        for i in range(2):
            part = turn_ref[i * COEFFICIENTS : (i + 1) * COEFFICIENTS, start : start + LANE]
            at = 2 * start + i * LANE
            relax_ref[:, at : at + LANE] = part.astype(BF16)
    row = lax.broadcasted_iota(jnp.int32, (COEFFICIENTS, LANE), 0)
    for i in range(2):
        at = 2 * lanes + i * LANE
        picked = jnp.where((row >= 23 + 3 * i) & (row < 26 + 3 * i), 1.0, 0.0)
        relax_ref[:, at : at + LANE] = picked.astype(BF16)

    speeds = [jnp.where(held, CLOCK_ADVANCE * SPACING * (v + 0.5), 0.0) for v in (a, b)]
    signs = [jnp.where(v >= 0.0, 0.5, -0.5) for v in (a, b)]
    for i, value in enumerate([*speeds, *signs, zero, zero, zero, zero]):
        courant_ref[i : i + 1, :] = value


def pieces(value, count):
    out = []
    for _ in range(count - 1):
        high = value.astype(BF16).astype(F32)
        out.append(high)
        value = value - high
    return out + [value]


def moment_sums(rows, basis):
    high = rows.astype(BF16)
    low = (rows - high.astype(F32)).astype(BF16)
    return jnp.dot(high, basis, preferred_element_type=F32) + jnp.dot(
        low, basis, preferred_element_type=F32
    )


def blocks_of(sums, chunk, chunks, block_ref):
    block_ref[pl.ds(chunk, 16, stride=chunks), :] = sums.T[:16, :]


def write_totals(chunks, block_ref, totals_ref):
    totals_ref[: 10 * chunks, :] = block_ref[: 10 * chunks, :]
    totals_ref[10 * chunks :, :] = (
        block_ref[10 * chunks : 13 * chunks, :] + block_ref[13 * chunks : 16 * chunks, :]
    )


def pieces_in_chunk(chunk, nx, ny):
    inner = range(2 * REACH, nx - 2 * REACH)
    if chunk < 2:
        start = REACH * chunk
        xs = [*range(start, start + REACH), *range(nx - start - REACH, nx - start)]
        return [(x, 0, ny) for x in xs]
    end = ny // 4
    if chunk == 2:
        return [(x, y, end) for x in inner for y in (0, ny - end)]
    return [(x, end, ny - 2 * end) for x in inner]


def coefficients(gathered_ref, knudsen_ref, kind_ref, block_ref):
    nx, ny = kind_ref.shape
    chunks = nx * ny // LANE
    for i, value in enumerate((knudsen_ref[...], kind_ref[...].astype(F32))):
        for chunk in range(chunks):
            row = [value[x : x + 1, y : y + n] for x, y, n in pieces_in_chunk(chunk, nx, ny)]
            at = (MOMENTS + i) * chunks + chunk
            block_ref[at : at + 1, :] = jnp.concatenate(row, axis=1)
    total = gathered_ref[0]
    for device in range(1, gathered_ref.shape[0]):
        total = total + gathered_ref[device]
    block_ref[: MOMENTS * chunks, :] = total
    n, nx, ny, nz, xx, yy, zz, xy, xz, yz, cx, cy, cz, knudsen, kind = (
        block_ref[i * chunks : (i + 1) * chunks, :] for i in range(MOMENTS + 2)
    )
    inverse = 1.0 / n
    ux, uy, uz = nx * inverse, ny * inverse, nz * inverse
    uu = ux * ux + uy * uy + uz * uz
    trace = xx + yy + zz
    spread = (trace * inverse - uu) / 3.0
    temperature = SPACING * SPACING * spread
    density = WEIGHT * n
    qx = cx - ux * trace - 2.0 * (ux * xx + uy * xy + uz * xz) + 2.0 * ux * uu * n
    qy = cy - uy * trace - 2.0 * (ux * xy + uy * yy + uz * yz) + 2.0 * uy * uu * n
    qz = cz - uz * trace - 2.0 * (ux * xz + uy * yz + uz * zz) + 2.0 * uz * uu * n
    root = jnp.sqrt(temperature)
    keep = jnp.exp(-CLOCK_ADVANCE * density * root / knudsen)
    scale = (1.0 - keep) * density / ((2.0 * math.pi) ** 1.5 * temperature * root)
    heat = (
        scale
        * ((1.0 - VISCOUS_RATIO) * -2.0 * math.log(2.0) / 10.0)
        / (n * spread * spread)
    )

    wall, inflow = kind == 1.0, kind == 2.0
    solid = wall | inflow
    ux = jnp.where(inflow, INFLOW_SPEED / SPACING - 0.5, jnp.where(wall, -0.5, ux))
    uy = jnp.where(solid, -0.5, uy)
    uz = jnp.where(solid, -0.5, uz)
    spread = jnp.where(
        inflow,
        INFLOW_TEMP / SPACING**2,
        jnp.where(wall, WALL_TEMP / SPACING**2, spread),
    )
    scale = jnp.where(
        inflow,
        INFLOW_DENSITY / (2.0 * math.pi * INFLOW_TEMP) ** 1.5,
        jnp.where(wall, density / (2.0 * math.pi * WALL_TEMP) ** 1.5, scale),
    )
    keep = jnp.where(solid, 0.0, keep)
    qx = jnp.where(solid, 0.0, heat * qx)
    qy = jnp.where(solid, 0.0, heat * qy)
    qz = jnp.where(solid, 0.0, heat * qz)
    rate = (0.5 * LOG2E) / spread

    rows = []
    rows += pieces(-rate * (ux * ux + uy * uy + uz * uz), 3)
    for u in (ux, uy, uz):
        rows += pieces(rate * (2.0 * u + 1.0), 3)
    rows += pieces(-2.0 * rate, 3)
    for q in (-(qx * ux + qy * uy + qz * uz), qx, qy, qz):
        rows += pieces(q, 2)
    rows += pieces(keep, 3)
    rows += pieces(scale, 3)
    rows += [jnp.zeros_like(n)] * (COEFFICIENTS - len(rows))
    for i, value in enumerate(rows):
        block_ref[i * chunks : (i + 1) * chunks, :] = value


def relaxed_rows(load, store, which, chunks, lanes, basis_ref, block_ref):
    tail = 2 * lanes
    for chunk in which:
        left = block_ref[pl.ds(chunk, COEFFICIENTS, stride=chunks), :].T.astype(BF16)
        pair = jnp.dot(left, basis_ref[:, tail : tail + 2 * LANE], preferred_element_type=F32)
        keep, scale = pair[:, :LANE], pair[:, LANE:]
        for lane in range(0, lanes, LANE):
            pair = jnp.dot(
                left, basis_ref[:, 2 * lane : 2 * lane + 2 * LANE], preferred_element_type=F32
            )
            power, linear = pair[:, :LANE], pair[:, LANE:]
            value = load(chunk, lane) * keep + (
                jnp.exp2(power) * (scale + linear * (power + 2.5 * LOG2E))
            )
            store(chunk, lane, value)


def chunk_rows(state_refs, chunk, nx, ny, lane):
    def piece(x, y, n):
        if len(state_refs) == 1:
            width = min(LANE, state_refs[0].shape[2] - lane)
            rows = state_refs[0][x, y : y + n, lane : lane + width]
            if width == LANE:
                return rows
            return jnp.concatenate([rows, jnp.zeros((n, LANE - width), F32)], axis=1)
        inner_ref, edges_ref = state_refs
        if x < REACH:
            ref, at = edges_ref, x * ny
        elif x >= nx - REACH:
            ref, at = edges_ref, (x - nx + 2 * REACH) * ny
        else:
            ref, at = inner_ref, (x - REACH) * ny
        return ref[at + y : at + y + n, lane : lane + LANE]

    return jnp.concatenate([piece(*p) for p in pieces_in_chunk(chunk, nx, ny)], axis=0)


def limited(left, right):
    least, most = jnp.minimum(left, right), jnp.maximum(left, right)
    return jnp.maximum(least, 0.0) + jnp.minimum(most, 0.0)


def transported_rows(load, side, xs, ny, lanes, courant_ref, write):
    row = ny + SUBLANE
    for lane in range(0, lanes, LANE):
        along = slice(lane, lane + LANE)
        speed_x, speed_y = courant_ref[0:1, along], courant_ref[1:2, along]
        half_x, half_y = courant_ref[2:3, along], courant_ref[3:4, along]
        positive_x = jnp.broadcast_to(half_x, (ny, LANE)) > 0.0
        positive_y = jnp.broadcast_to(half_y, (ny, LANE)) > 0.0

        before, centre = load(xs[0] - 2, lane), load(xs[0] - 1, lane)
        slope_before = centre - before
        edge_before = face_before = centre_before = None
        for x in range(xs[0] - 1, xs[-1] + 2):
            after = load(x + 1, lane)
            slope_after = after - centre
            edge = centre + half_x * limited(slope_before, slope_after)
            face = None if edge_before is None else edge - edge_before
            if face_before is not None:
                middle = jnp.concatenate([centre_before, side(x - 1, lane)], axis=0)
                rise = pltpu.roll(middle, row - 1, 0) - middle
                edge_y = middle + half_y * limited(pltpu.roll(rise, 1, 0), rise)
                face_y = pltpu.roll(edge_y, row - 1, 0) - edge_y
                change_x = jnp.where(positive_x, face_before, face)
                change_y = jnp.where(positive_y, pltpu.roll(face_y, 1, 0)[:ny], face_y[:ny])
                write(x - 1, lane, centre_before - speed_x * change_x - speed_y * change_y)
            centre_before, centre = centre, after
            slope_before = slope_after
            edge_before, face_before = edge, face

def alternate(shape, positive):
    odd = lax.broadcasted_iota(jnp.int32, shape, 1) % 2 == 1
    return odd if positive else ~odd


def pack_layers(near, far, positive, lanes, out_ref):
    for lane in range(0, lanes, LANE):
        along = slice(lane, lane + LANE)
        nearest, second = near(lane), far(lane)
        ny = nearest.shape[0]
        first, rest = second[: ny // 2], second[ny // 2 :]
        out_ref[:ny, along] = nearest
        out_ref[ny:, along] = jnp.where(
            alternate(first.shape, positive), first, pltpu.roll(rest, 1, 1)
        )


def unpack_layer(ref, distance, ny, lane):
    along = slice(lane, lane + LANE)
    if distance == 0:
        return ref[:ny, along]
    packed = ref[ny:, along]
    return jnp.concatenate([packed, pltpu.roll(packed, LANE - 1, 1)], axis=0)


def run_alternate(shape, lane, positive):
    odd = (lax.broadcasted_iota(jnp.int32, shape, 1) + lane) // NVX % 2 == 1
    return odd if positive else ~odd


def pack_ends(state_ref, near, far, ny, positive, out_ref, far_ref):
    nx, lanes = far_ref.shape
    for x in range(nx):
        out_ref[x : x + 1, :] = state_ref[x * ny + near : x * ny + near + 1, :]
        far_ref[x : x + 1, :] = state_ref[x * ny + far : x * ny + far + 1, :]
    before = None
    for lane in range(0, lanes, LANE):
        along = slice(lane, lane + LANE)
        second = far_ref[:, along]
        half = nx // 2
        turned = pltpu.roll(second[half:], NVX, 1)
        moved = turned
        if before is not None:
            crossed = lax.broadcasted_iota(jnp.int32, turned.shape, 1) < NVX
            moved = jnp.where(crossed, before, turned)
        before = turned
        own = run_alternate(turned.shape, lane, positive)
        out_ref[nx:, along] = jnp.where(own, second[:half], moved)


def unpack_ends(ref, near_at, far_at, side_ref):
    rows, lanes = ref.shape
    half = rows // 3
    after = None
    for lane in range(lanes - LANE, -1, -LANE):
        along = slice(lane, lane + LANE)
        block = lane // LANE
        side_ref[block, pl.ds(near_at, 2 * half, stride=SUBLANE), :] = ref[: 2 * half, along]
        packed = ref[2 * half :, along]
        turned = pltpu.roll(packed, LANE - NVX, 1)
        moved = turned
        if after is not None:
            crossed = lax.broadcasted_iota(jnp.int32, turned.shape, 1) >= LANE - NVX
            moved = jnp.where(crossed, after, turned)
        after = turned
        both = jnp.concatenate([packed, moved], axis=0)
        side_ref[block, pl.ds(far_at, 2 * half, stride=SUBLANE), :] = both


def side_rows(side_ref):
    def side(x, lane):
        return side_ref[lane // LANE, x * SUBLANE : (x + 1) * SUBLANE, :]

    return side


def first_kernel(state_ref, basis_ref, totals_ref, block_ref):
    nx, ny, velocities = state_ref.shape
    chunks = nx * ny // LANE
    basis = basis_ref[:velocities, :]
    for chunk in range(chunks):
        parts = [state_ref[x, y : y + n, :] for x, y, n in pieces_in_chunk(chunk, nx, ny)]
        blocks_of(moment_sums(jnp.concatenate(parts, axis=0), basis), chunk, chunks, block_ref)
    write_totals(chunks, block_ref, totals_ref)


def by_parity(odd_ref, do, first_ref, second_ref):
    @pl.when(odd_ref[0] == 0)
    def _():
        do(second_ref, first_ref)

    @pl.when(odd_ref[0] != 0)
    def _():
        do(first_ref, second_ref)


def relax_kernel(ny, odd_x_ref, odd_y_ref, gathered_ref, knudsen_ref, kind_ref, *refs):
    *state_refs, basis_ref, out_ref, first_x_ref, second_x_ref, first_y_ref, second_y_ref = refs[:-2]
    block_ref, far_ref = refs[-2:]
    cells, lanes = out_ref.shape
    nx, chunks = cells // ny, cells // LANE
    coefficients(gathered_ref, knudsen_ref, kind_ref, block_ref)

    def load(chunk, lane):
        return chunk_rows(state_refs, chunk, nx, ny, lane)

    def store(chunk, lane, value):
        done = 0
        for x, y, n in pieces_in_chunk(chunk, nx, ny):
            at = x * ny + y
            out_ref[at : at + n, lane : lane + LANE] = value[done : done + n, :]
            done += n

    relaxed_rows(load, store, range(chunks - 1), chunks, lanes, basis_ref, block_ref)


    def row_of(x):
        return lambda lane: out_ref[x * ny : (x + 1) * ny, lane : lane + LANE]

    def pack_x(low_ref, high_ref):
        pack_layers(row_of(0), row_of(1), False, lanes, low_ref)
        pack_layers(row_of(nx - 1), row_of(nx - 2), True, lanes, high_ref)

    def pack_y(low_ref, high_ref):
        pack_ends(out_ref, 0, 1, ny, False, low_ref, far_ref)
        pack_ends(out_ref, ny - 1, ny - 2, ny, True, high_ref, far_ref)

    by_parity(odd_x_ref, pack_x, first_x_ref, second_x_ref)
    by_parity(odd_y_ref, pack_y, first_y_ref, second_y_ref)


def inner_kernel(ny, velocities, odd_y_ref, state_ref, first_y_ref, second_y_ref, courant_ref, coefficient_ref, relax_ref, *refs):
    cells, lanes = state_ref.shape
    nx, chunks = cells // ny, cells // LANE
    if velocities is None:
        *refs, side_ref, rest_ref = refs
        outputs = 3
    else:
        *refs, side_ref, rest_ref, stage_ref, sent = refs
        outputs = 1
    before_refs, refs = refs[: len(refs) - outputs], refs[len(refs) - outputs :]

    def load_rest(chunk, lane):
        return chunk_rows(before_refs, chunk, nx, ny, lane)

    def store_rest(chunk, lane, value):
        rest_ref[:, lane : lane + LANE] = value

    relaxed_rows(load_rest, store_rest, [chunks - 1], chunks, lanes, relax_ref, coefficient_ref)
    rest = {p[0]: p for p in pieces_in_chunk(chunks - 1, nx, ny)}
    first = min(rest)

    def load(x, lane):
        along, at = slice(lane, lane + LANE), x * ny
        if x not in rest:
            return state_ref[at : at + ny, along]
        _, y, n = rest[x]
        parts = [state_ref[at : at + y, along], rest_ref[(x - first) * n : (x - first + 1) * n, along]]
        return jnp.concatenate([*parts, state_ref[at + y + n : at + ny, along]], axis=0)

    side_ref[...] = jnp.zeros_like(side_ref)

    def unpack_y(low_ref, high_ref):
        unpack_ends(high_ref, 0, 1, side_ref)
        unpack_ends(low_ref, SUBLANE - 1, SUBLANE - 2, side_ref)

    by_parity(odd_y_ref, unpack_y, first_y_ref, second_y_ref)
    copies = []
    if velocities is None:
        basis_ref, out_ref, block_ref = refs

        def write(x, lane, value):
            at = (x - REACH) * ny
            out_ref[at : at + ny, lane : lane + LANE] = value

        groups = 1
    else:
        (out_ref,) = refs
        groups = sent.shape[0]

        def write(x, lane, value):
            width = min(LANE, velocities - lane)
            stage_ref[x - REACH, :, lane : lane + width] = value[:, :width]

    count = (nx - 2 * REACH) // groups
    for group in range(groups):
        start = REACH + group * count
        xs = range(start, start + count)
        transported_rows(load, side_rows(side_ref), xs, ny, lanes, courant_ref, write)
        if velocities is not None:
            part = stage_ref.at[start - REACH : start - REACH + count]
            copies.append(
                pltpu.make_async_copy(part, out_ref.at[start : start + count], sent.at[group])
            )
            copies[-1].start()
    for copy in copies:
        copy.wait()
    if velocities is None:
        for chunk in range(1, chunks):
            parts = []
            for x, y, n in pieces_in_chunk(chunk, nx, ny):
                at = (x - REACH) * ny + y
                parts.append(out_ref[at : at + n, :])
            sums = moment_sums(jnp.concatenate(parts, axis=0), basis_ref[...])
            blocks_of(sums, chunk, chunks, block_ref)


def outer_kernel(ny, second, final, odd_x_ref, state_ref, side_x_ref, side_ref, courant_ref, *refs):
    cells, lanes = state_ref.shape
    nx, edge = cells // ny, REACH * ny
    odd = odd_x_ref[0] != 0
    high = odd if second else ~odd

    def load(x, lane):
        if x < 0:
            return unpack_layer(side_x_ref, -1 - x, ny, lane)
        if x >= nx:
            return unpack_layer(side_x_ref, x - nx, ny, lane)
        return state_ref[x * ny : (x + 1) * ny, lane : lane + LANE]

    def transport(write):
        for start, chosen in ((0, ~high), (nx - REACH, high)):

            @pl.when(chosen)
            def _(start=start):
                def write_row(x, lane, value):
                    write(x - start, lane, value)

                xs = range(start, start + REACH)
                transported_rows(load, side_rows(side_ref), xs, ny, lanes, courant_ref, write_row)

    if final:
        if second:
            other_ref, _, out_ref, edge_ref, sent = refs
            own_at = jnp.where(high, nx - REACH, 0)
            other_at = jnp.where(high, 0, nx - REACH)
            other_copy = pltpu.make_async_copy(
                other_ref, out_ref.at[pl.ds(other_at, REACH)], sent.at[0]
            )
            other_copy.start()
        else:
            (edge_ref,) = refs

        def write(x, lane, value):
            width = min(LANE, edge_ref.shape[2] - lane)
            edge_ref[x, :, lane : lane + width] = value[:, :width]

        transport(write)
        if second:
            copy = pltpu.make_async_copy(
                edge_ref, out_ref.at[pl.ds(own_at, REACH)], sent.at[1]
            )
            copy.start()
            other_copy.wait()
            copy.wait()
        return

    basis_ref, *refs = refs
    if second:
        other_ref, other_sums_ref, inner_block_ref, edges_ref, totals_ref, own_ref, sums_ref, block_ref = refs
    else:
        own_ref, own_sums_ref = refs

    def write(x, lane, value):
        own_ref[x * ny : (x + 1) * ny, lane : lane + LANE] = value

    transport(write)
    own_sums = moment_sums(own_ref[...], basis_ref[...])
    if not second:
        own_sums_ref[...] = own_sums
        return
    own_at = pl.multiple_of(jnp.where(high, edge, 0), edge)
    other_at = pl.multiple_of(jnp.where(high, 0, edge), edge)
    edges_ref[pl.ds(own_at, edge), :] = own_ref[...]
    edges_ref[pl.ds(other_at, edge), :] = other_ref[...]
    sums_ref[pl.ds(own_at, edge), :] = own_sums
    sums_ref[pl.ds(other_at, edge), :] = other_sums_ref[...]
    chunks = cells // LANE
    block_ref[...] = inner_block_ref[...]
    blocks_of(sums_ref[...], 0, chunks, block_ref)
    write_totals(chunks, block_ref, totals_ref)


INNER_COST = pl.CostEstimate(flops=1_100_000_000, bytes_accessed=1000, transcendentals=0)
LOW_COST = pl.CostEstimate(flops=1_000_000_000, bytes_accessed=1000, transcendentals=0)


def rows_of(*shape):
    return jax.ShapeDtypeStruct(shape, F32)


def call(kernel, name, out_shape, scratch=(), **options):
    return pl.pallas_call(
        kernel,
        out_shape=out_shape,
        scratch_shapes=scratch,
        compiler_params=pltpu.CompilerParams(vmem_limit_bytes=40 * 1024 * 1024),
        name=name,
        **options,
    )


def gather(totals):
    devices = lax.axis_size("vel")
    copies = jnp.broadcast_to(totals[None], (devices, *totals.shape))
    return lax.all_to_all(copies, "vel", 0, 0)


OFFSETS = {"sx": 0, "sy": 1}


def partners(axis):
    devices = lax.axis_size(axis)
    pairs = []
    for first in (OFFSETS[axis], 1 - OFFSETS[axis]):
        couples = [((i + first) % devices, (i + first + 1) % devices) for i in range(0, devices, 2)]
        pairs.append(couples + [(b, a) for a, b in couples])
    return pairs


def body(distribution, cell_kind, local_knudsen):
    nx, ny, velocities = distribution.shape
    lanes = -(-velocities // LANE) * LANE
    cells = nx * ny
    chunks = cells // LANE
    block = pltpu.VMEM((COEFFICIENTS * chunks, LANE), F32)
    totals_shape = rows_of(MOMENTS * chunks, LANE)
    edge, side_x, side_y = (rows_of(n, lanes) for n in (REACH * ny, ny + ny // 2, nx + nx // 2))

    first, odd_x, odd_y = lax.optimization_barrier(
        tuple(
            jnp.full((1,), value, jnp.int32)
            for value in (
                lax.axis_index("vel") * velocities,
                (lax.axis_index("sx") + OFFSETS["sx"]) % 2,
                (lax.axis_index("sy") + OFFSETS["sy"]) % 2,
            )
        )
    )
    moment_basis, relax_basis, courant = call(
        functools.partial(tables_kernel, velocities),
        "tables",
        (
            jax.ShapeDtypeStruct((lanes, LANE), BF16),
            jax.ShapeDtypeStruct((COEFFICIENTS, 2 * lanes + 2 * LANE), BF16),
            rows_of(SUBLANE, lanes),
        ),
        [pltpu.VMEM((LANE, lanes), F32)],
        in_specs=[pl.BlockSpec(memory_space=pltpu.SMEM)],
    )(first)
    totals = call(first_kernel, "first_moments", totals_shape, [block])(
        distribution, moment_basis
    )
    state = (distribution,)
    for step in range(STEPS):
        final = step == STEPS - 1
        smem, vmem, hbm = (
            pl.BlockSpec(memory_space=m) for m in (pltpu.SMEM, pltpu.VMEM, pltpu.HBM)
        )
        operands = (gather(totals), local_knudsen, cell_kind, *state, relax_basis)
        relaxed, first_x, second_x, first_y, second_y, coefficient = call(
            functools.partial(relax_kernel, ny),
            "relax",
            (
                rows_of(cells, lanes), side_x, side_x, side_y, side_y,
                rows_of(COEFFICIENTS * chunks, LANE),
            ),
            [pltpu.VMEM((nx, lanes), F32)],
            in_specs=[smem, smem] + [vmem] * len(operands),
        )(odd_x, odd_y, *operands)
        to_first, to_second = partners("sy")
        sides_y = (lax.ppermute(first_y, "sy", to_first), lax.ppermute(second_y, "sy", to_second))
        to_first, to_second = partners("sx")
        first_x = lax.ppermute(first_x, "sx", to_first)
        second_x = lax.ppermute(second_x, "sx", to_second)
        side_shape = rows_of(lanes // LANE, nx * SUBLANE, LANE)
        rest = pltpu.VMEM((LANE, lanes), F32)
        operands = (relaxed, *sides_y, courant, coefficient, relax_basis, *state)
        if final:
            inner, side = call(
                functools.partial(inner_kernel, ny, velocities),
                "last_inner",
                (rows_of(nx, ny, velocities), side_shape),
                [
                    rest,
                    pltpu.VMEM((nx - 2 * REACH, ny, velocities), F32),
                    pltpu.SemaphoreType.DMA((3,)),
                ],
                in_specs=[smem] + [vmem] * len(operands),
                out_specs=(hbm, vmem),
                cost_estimate=INNER_COST,
            )(odd_y, *operands)
            ends = rows_of(REACH, ny, velocities)
            other = call(
                functools.partial(outer_kernel, ny, False, True),
                "last_first",
                ends,
                in_specs=[smem] + [vmem] * 4,
                cost_estimate=LOW_COST,
            )(odd_x, relaxed, first_x, side, courant)
            return call(
                functools.partial(outer_kernel, ny, True, True),
                "last_second",
                rows_of(nx, ny, velocities),
                [pltpu.VMEM(ends.shape, F32), pltpu.SemaphoreType.DMA((2,))],
                in_specs=[smem] + [vmem] * 5 + [hbm],
                out_specs=hbm,
                input_output_aliases={6: 0},
            )(odd_x, relaxed, second_x, side, courant, other, inner)
        inner, inner_block, side = call(
            functools.partial(inner_kernel, ny, None),
            "inner",
            (rows_of(cells - 2 * REACH * ny, lanes), rows_of(16 * chunks, LANE), side_shape),
            [rest],
            in_specs=[smem] + [vmem] * (len(operands) + 1),
            cost_estimate=INNER_COST,
        )(odd_y, *operands, moment_basis)
        other, other_sums = call(
            functools.partial(outer_kernel, ny, False, False),
            "outer_first",
            (edge, rows_of(REACH * ny, LANE)),
            in_specs=[smem] + [vmem] * 5,
            cost_estimate=LOW_COST,
        )(odd_x, relaxed, first_x, side, courant, moment_basis)
        edges, totals = call(
            functools.partial(outer_kernel, ny, True, False),
            "outer_second",
            (rows_of(2 * REACH * ny, lanes), totals_shape),
            [
                pltpu.VMEM((REACH * ny, lanes), F32),
                pltpu.VMEM((2 * REACH * ny, LANE), F32),
                pltpu.VMEM((16 * chunks, LANE), F32),
            ],
            in_specs=[smem] + [vmem] * 8,
        )(odd_x, relaxed, second_x, side, courant, moment_basis, other, other_sums, inner_block)
        state = (inner, edges)


def solution(mesh):
    return jax.shard_map(
        body,
        mesh=mesh,
        in_specs=(P("sx", "sy", "vel"), P("sx", "sy"), P("sx", "sy")),
        out_specs=P("sx", "sy", "vel"),
        check_vma=False,
    )
```
